32 devices in a mesh: ulysses: 4 (over y, x), blk: 8 (over z, core).
Axes of the slice: x: 2, y: 2, z: 4, core: 2. Of those that a mesh axis runs over, the one named last changes fastest.
Arguments:
- tokens: bfloat16 [4096, 1024], P(('ulysses', 'blk')), may hold values from -6 to 6
- ln1_gain: bfloat16 [1024], P(('ulysses', 'blk')), may hold values from 0.5 to 1.5
- ln1_bias: bfloat16 [1024], P(('ulysses', 'blk')), may hold values from -1.75 to 1.75
- qkv_weight: bfloat16 [1024, 3072], P(('ulysses', 'blk')), may hold values from -0.1875 to 0.1875
- qv_bias: bfloat16 [2048], P(('ulysses', 'blk')), may hold values from -0.625 to 0.625
- proj_weight: bfloat16 [1024, 1024], P(('ulysses', 'blk')), may hold values from -1.5 to 1.5
- proj_bias: bfloat16 [1024], P(('ulysses', 'blk')), may hold values from -1.75 to 1.75
- ln2_gain: bfloat16 [1024], P(('ulysses', 'blk')), may hold values from 0.5 to 1.5
- ln2_bias: bfloat16 [1024], P(('ulysses', 'blk')), may hold values from -1.75 to 1.75
- up_weight: bfloat16 [1024, 4096], P(('ulysses', 'blk')), may hold values from -0.1875 to 0.1875
- up_bias: bfloat16 [4096], P(('ulysses', 'blk')), may hold values from -1.75 to 1.75
- down_weight: bfloat16 [4096, 1024], P(('ulysses', 'blk')), may hold values from -0.09375 to 0.09375
- down_bias: bfloat16 [1024], P(('ulysses', 'blk')), may hold values from -1.75 to 1.75
- alibi_slopes: float32 [16], replicated, may hold values from 0 to 1
- doc_starts: int32 [7], replicated, may hold values from 0 to 3584, as said below
- cotangent: bfloat16 [4096, 1024], P(('ulysses', 'blk')), may hold values from -12 to 12
Outputs:
- output: bfloat16 [4096, 1024], P(('ulysses', 'blk'))
- input_grad: bfloat16 [4096, 1024], P(('ulysses', 'blk'))
- ln1_gain_grad: float32 [1024], P(('ulysses', 'blk'))
- ln1_bias_grad: float32 [1024], P(('ulysses', 'blk'))
- qkv_weight_grad: float32 [1024, 3072], P(('ulysses', 'blk'))
- qv_bias_grad: float32 [2048], P(('ulysses', 'blk'))
- proj_weight_grad: float32 [1024, 1024], P(('ulysses', 'blk'))
- proj_bias_grad: float32 [1024], P(('ulysses', 'blk'))
- ln2_gain_grad: float32 [1024], P(('ulysses', 'blk'))
- ln2_bias_grad: float32 [1024], P(('ulysses', 'blk'))
- up_weight_grad: float32 [1024, 4096], P(('ulysses', 'blk'))
- up_bias_grad: float32 [4096], P(('ulysses', 'blk'))
- down_weight_grad: float32 [4096, 1024], P(('ulysses', 'blk'))
- down_bias_grad: float32 [1024], P(('ulysses', 'blk'))
The draws below stay inside these ranges and needn't reach their ends.
Inputs may be any that keep to these rules, and one draw needn't show every extreme that they name: `doc_starts`: strictly increasing, the first entry 0, the last entry exactly 3584. Document d holds the tokens from entry d up to the next entry, the last one up to the end. No document is longer than 1024 tokens, and one is exactly 1024 tokens long.
All inputs are finite; a program needn't handle non-finite values.
Results may differ from the reference program's by a relative error of at most 0.017.
Values may be sent and summed in bfloat16 or wider, within the bound.
A program may use at most 256 MiB of HBM per device.

```python
import math
import jax
import jax.numpy as jnp
from jax import lax

D = 1024
HEADS = 16
HEAD_DIM = 64
FF = 4096
TOKENS = 4096
DOC_MAX = 1024
DOCS = 7


def draw_alibi_slopes(key, part):
    key = jax.random.fold_in(key, 11)
    order_key, slow_key, quick_key = jax.random.split(key, 3)
    ranking = jax.random.permutation(order_key, HEADS)
    quick_count = HEADS // 2
    slow_rate = jax.random.uniform(slow_key, (HEADS,), jnp.float32, 0.2, 2.0) / DOC_MAX
    quick_rate = jnp.exp(jax.random.uniform(quick_key, (HEADS,), jnp.float32, math.log(0.02), math.log(0.1)))
    return jnp.where(ranking < quick_count, quick_rate, slow_rate).astype(jnp.float32)


def draw_doc_starts(key, part):
    key = jax.random.fold_in(key, 23)
    pick_key, shift_key = jax.random.split(key, 2)
    cell_rows = DOC_MAX // 2
    long_cell = jax.random.randint(pick_key, (), 0, DOCS - 1, dtype=jnp.int32)
    index_all = jnp.arange(DOCS, dtype=jnp.int32)
    cell_of = index_all + (index_all > long_cell).astype(jnp.int32)
    jitter = jax.random.randint(shift_key, (DOCS,), 0, cell_rows // 2, dtype=jnp.int32)
    fixed = (cell_of == 0) | (cell_of == long_cell) | (cell_of == long_cell + 2) | (index_all == DOCS - 1)
    jitter = jnp.where(fixed, jnp.zeros_like(jitter), jitter)
    return (cell_of * cell_rows - jitter).astype(jnp.int32)


def strengthened(drawn, rng, source, target, shards_of, factor):
    def block_of(position):
        return (jnp.arange(drawn.shape[position]) // (drawn.shape[position] // shards_of)).reshape((-1,) + (1,) * (drawn.ndim - 1 - position))

    near = jax.random.permutation(rng, shards_of)[block_of(target)]
    other_side = (block_of(target) + shards_of // 2) % shards_of
    return jnp.where((block_of(source) == near) | (block_of(source) == other_side), factor * drawn, drawn)


def level_of(rng, shape, pieces, low, largest):
    def one(dim, parts):
        steps = jax.random.uniform(jax.random.fold_in(jax.random.fold_in(rng, 6), dim), (parts,), jnp.float32, low / len(pieces), largest / len(pieces))
        return jnp.repeat(jnp.exp(steps), shape[dim] // parts).reshape((-1,) + (1,) * (len(shape) - dim - 1))

    loudness = one(*pieces[0])
    for cut in pieces[1:]:
        loudness = loudness * one(*cut)
    return loudness


def gaussian(key, dims, scale, bound, cuts=(), kind=jnp.bfloat16):
    array = jax.random.normal(key, dims, jnp.float32) * scale
    if len(cuts) > 0:
        array = level_of(key, dims, cuts, -0.22, 0.18) * array
    return jnp.clip(array, min=-bound, max=bound).astype(kind)


def gaussian_with(own_key, extent, scale, most, cuts, heavy, held_as=jnp.bfloat16):
    drawn = scale * jax.random.normal(own_key, extent, jnp.float32)
    if cuts:
        drawn = drawn * level_of(own_key, extent, cuts, -0.22, 0.18)
    return jnp.clip(strengthened(drawn, jax.random.fold_in(own_key, 3), *heavy), -most, most).astype(held_as)


def setup_inputs(seed: int = 0) -> dict:
    streams_of = jax.random.split(jax.random.key(seed), 17)
    tokens = gaussian(streams_of[0], (TOKENS, D), 1.0, 6.0, ((0, 32),))
    ln1_gain = jnp.clip(1.0 + 0.1 * jax.random.normal(streams_of[1], (D,), jnp.float32), 0.5, 1.5).astype(jnp.bfloat16)
    ln1_bias = gaussian(streams_of[2], (D,), 0.3, 1.75, ((0, 32),))
    qkv_weight = gaussian(streams_of[3], (D, 3 * D), D ** -0.5, 0.1875, ((0, 32),))
    qv_bias = gaussian(streams_of[4], (2 * D,), 0.1, 0.625, ((0, 32),))
    proj_weight = gaussian(streams_of[5], (D, D), (D // 64) ** -0.5, 1.5, ((0, 32),))
    proj_bias = gaussian(streams_of[6], (D,), 0.3, 1.75, ((0, 32),))
    ln2_gain = jnp.clip(1.0 + 0.1 * jax.random.normal(streams_of[7], (D,), jnp.float32), 0.5, 1.5).astype(jnp.bfloat16)
    ln2_bias = gaussian(streams_of[8], (D,), 0.3, 1.75, ((0, 32),))
    up_weight = gaussian(streams_of[9], (D, FF), D ** -0.5, 0.1875, ((0, 32),))
    up_bias = gaussian(streams_of[10], (FF,), 0.3, 1.75, ((0, 32),))
    down_weight = gaussian(streams_of[11], (FF, D), FF ** -0.5, 0.09375, ((0, 32),))
    down_bias = gaussian(streams_of[12], (D,), 0.3, 1.75, ((0, 32),))
    alibi_slopes = draw_alibi_slopes(jax.random.fold_in(streams_of[16], 71), 0)
    doc_starts = draw_doc_starts(jax.random.fold_in(streams_of[16], 71), 0)
    cotangent = gaussian_with(streams_of[15], (TOKENS, D), 1.0, 12.0, ((0, 32),), (0, 1, 32, 2.75))
    return dict(tokens=tokens, ln1_gain=ln1_gain, ln1_bias=ln1_bias, qkv_weight=qkv_weight, qv_bias=qv_bias, proj_weight=proj_weight, proj_bias=proj_bias, ln2_gain=ln2_gain, ln2_bias=ln2_bias, up_weight=up_weight, up_bias=up_bias, down_weight=down_weight, down_bias=down_bias, alibi_slopes=alibi_slopes, doc_starts=doc_starts, cotangent=cotangent)


@jax.custom_vjp
def low(v):
    return lax.optimization_barrier(v.astype(jnp.bfloat16)).astype(jnp.float32)

@jax.custom_vjp
def low_back(v):
    return v

def low_keep(v):
    return (low(v), None)

def low_pass(kept, grad):
    return (grad,)

def back_keep(v):
    return (v, None)

def back_low(kept, grad):
    return (low(grad),)
low.defvjp(low_keep, low_pass)
low_back.defvjp(back_keep, back_low)

def layer_norm(values, norm_gain, norm_shift):
    center = lax.optimization_barrier(jnp.mean(values, axis=-1, keepdims=True))
    offset = values - center
    spread = lax.optimization_barrier(jnp.mean(offset * offset, axis=-1, keepdims=True))
    return offset * lax.rsqrt(spread + 1e-05) * norm_gain + norm_shift

def gelu_tanh(values):
    return 0.5 * values * (1.0 + jnp.tanh(0.7978845608028654 * (values + 0.044715 * values * values * values)))

def reference(tokens, ln1_gain, ln1_bias, qkv_weight, qv_bias, proj_weight, proj_bias, ln2_gain, ln2_bias, up_weight, up_bias, down_weight, down_bias, alibi_slopes, doc_starts, cotangent):
    total_rows = tokens.shape[0]
    positions = jnp.arange(total_rows, dtype=jnp.int32)
    doc_ids = lax.optimization_barrier(jnp.sum((positions[:, None] >= doc_starts[None, :]).astype(jnp.int32), axis=1)) - 1
    block_rows = math.gcd(512, total_rows)
    block_count = total_rows // block_rows
    scale_factor = HEAD_DIM ** (-0.5)
    slopes = alibi_slopes.astype(jnp.float32)
    highest = lax.Precision.HIGHEST

    def forward(inputs_f, gain_one, shift_one, qkv_proj, qv_shift, proj_mat, proj_shift, gain_two, shift_two, up_mat, up_shift, down_mat, down_shift):
        normed_one = low(layer_norm(inputs_f, gain_one, shift_one))
        joined_bias = jnp.concatenate([qv_shift[:D], jnp.zeros((D,), qv_shift.dtype), qv_shift[D:]])
        joined = jnp.dot(normed_one, qkv_proj, precision=highest) + joined_bias
        queries = low(low_back(joined[:, :D])).reshape(total_rows, HEADS, HEAD_DIM)
        keys = low(low_back(joined[:, D:2 * D])).reshape(total_rows, HEADS, HEAD_DIM)
        values = low(low_back(joined[:, 2 * D:])).reshape(total_rows, HEADS, HEAD_DIM)

        def attend(index):
            query_block = lax.dynamic_slice_in_dim(queries, index * block_rows, block_rows, 0)
            query_pos = lax.dynamic_slice_in_dim(positions, index * block_rows, block_rows, 0)
            query_doc = lax.dynamic_slice_in_dim(doc_ids, index * block_rows, block_rows, 0)
            raw_scores = jnp.einsum('qhd,khd->hqk', query_block, keys, precision=highest) * scale_factor
            distance = (query_pos[:, None] - positions[None, :]).astype(jnp.float32)
            raw_scores = low_back(raw_scores - slopes[:, None, None] * distance[None])
            allowed = (positions[None, :] <= query_pos[:, None]) & (doc_ids[None, :] == query_doc[:, None])
            masked = jnp.where(allowed[None], raw_scores, -1e+30)
            top_score = lax.optimization_barrier(jnp.max(masked, axis=-1, keepdims=True))
            weights = jnp.exp(masked - top_score)
            probs = low(weights / lax.optimization_barrier(jnp.sum(weights, axis=-1, keepdims=True)))
            return jnp.einsum('hqk,khd->qhd', probs, values, precision=highest)
        attended_parts = lax.map(jax.checkpoint(attend), jnp.arange(block_count, dtype=jnp.int32))
        attended = low(low_back(attended_parts.reshape(total_rows, D)))
        mixed = inputs_f + low_back(jnp.dot(attended, proj_mat, precision=highest) + proj_shift)
        normed_two = low(layer_norm(mixed, gain_two, shift_two))
        up_values = low_back(jnp.dot(normed_two, up_mat, precision=highest) + up_shift)
        activated = low(gelu_tanh(up_values))
        return mixed + low_back(jnp.dot(activated, down_mat, precision=highest) + down_shift)
    params = (ln1_gain, ln1_bias, qkv_weight, qv_bias, proj_weight, proj_bias, ln2_gain, ln2_bias, up_weight, up_bias, down_weight, down_bias)
    params_f = tuple((param.astype(jnp.float32) for param in params))
    result, pullback = jax.vjp(forward, tokens.astype(jnp.float32), *params_f)
    grads = pullback(cotangent.astype(jnp.float32))
    return (result.astype(jnp.bfloat16), grads[0].astype(jnp.bfloat16), grads[1], grads[2], grads[3], grads[4], grads[5], grads[6], grads[7], grads[8], grads[9], grads[10], grads[11], grads[12])
```

```python
import functools

import jax
import jax.numpy as jnp
from jax import lax
from jax.experimental import pallas as pl
from jax.experimental.pallas import tpu as pltpu
from jax.sharding import PartitionSpec as P

BF = jnp.bfloat16
F32 = jnp.float32
MESH = pl.DeviceIdType.MESH
VMEM_LIMIT = 60 * 2**20
NT = (((1,), (1,)), ((), ()))
TN = (((0,), (0,)), ((), ()))
NN = (((1,), (0,)), ((), ()))


def dot(a, b, dims=NN):
    return lax.dot_general(a, b, dims, preferred_element_type=F32)


def flip(index, mask):
    out = index
    bit = 1
    while bit <= mask:
        if mask & bit:
            out = out + bit - 2 * bit * ((index // bit) % 2)
        bit *= 2
    return out


def ds(start, size, align=None):
    if not isinstance(start, int):
        start = pl.multiple_of(start, align or size)
    return pl.ds(start, size)


class Wire:
    def __init__(self, ssem, rsem, lsem=None):
        self.ssem, self.rsem, self.lsem = ssem, rsem, lsem
        self.used = 0
        self.local = 0
        self.u = lax.axis_index("ulysses")
        self.b = lax.axis_index("blk")
        self.sent = []

    def take(self, count):
        first = self.used
        self.used += count
        return first

    def make(self, src, dst, device, at, sent_at=None):
        return pltpu.make_async_remote_copy(
            src_ref=src,
            dst_ref=dst,
            send_sem=self.ssem.at[at if sent_at is None else sent_at],
            recv_sem=self.rsem.at[at],
            device_id=device,
            device_id_type=MESH,
        )

    def blk(self, k, src, dst):
        copy = self.make(src, dst, (self.u, flip(self.b, k)), self.take(1))
        copy.start()
        self.sent.append(copy)
        return copy

    def uly(self, k, src, dst):
        copy = self.make(src, dst, (flip(self.u, k), self.b), self.take(1))
        copy.start()
        self.sent.append(copy)
        return copy

    def near(self, ku, kb, src, dst):
        copy = self.make(src, dst, (flip(self.u, ku), flip(self.b, kb)), self.take(1))
        copy.start()
        self.sent.append(copy)
        return copy

    def here(self, src, dst):
        copy = pltpu.make_async_copy(src, dst, self.lsem.at[self.local])
        self.local += 1
        copy.start()
        return copy

    def finish(self):
        for copy in self.sent:
            copy.wait_send()


def greet(u, b, blk_masks, uly_masks, both=()):
    barrier = pltpu.get_barrier_semaphore()
    for k in blk_masks:
        pl.semaphore_signal(barrier, inc=1, device_id=(u, flip(b, k)), device_id_type=MESH)
    for k in uly_masks:
        pl.semaphore_signal(barrier, inc=1, device_id=(flip(u, k), b), device_id_type=MESH)
    for ku, kb in both:
        pl.semaphore_signal(barrier, inc=1, device_id=(flip(u, ku), flip(b, kb)), device_id_type=MESH)
    pl.semaphore_wait(barrier, len(blk_masks) + len(uly_masks) + len(both))


def norm_parts(values):
    center = jnp.mean(values, axis=-1, keepdims=True)
    offset = values - center
    spread = jnp.mean(offset * offset, axis=-1, keepdims=True)
    inv = lax.rsqrt(spread + 1e-05)
    return offset * inv, inv


def head_mask(shape, head):
    lane = lax.broadcasted_iota(jnp.int32, shape, len(shape) - 1)
    return (lane // 64) == head


def doc_begin(starts_ref, positions):
    begin = jnp.zeros_like(positions)
    for d in range(starts_ref.shape[0]):
        first = starts_ref[d]
        begin = jnp.where(positions >= first, jnp.full_like(positions, first), begin)
    return begin


def forward_kernel(
    tok, wqkv, wproj, wup, wdown, pack, slopes, starts,
    att_o, q_o, kv_o, lse_o, n1_o, wqkv_o, par_o, wproj_o, wup_o, wdown_o,
    x_ag, stq, stu, atth, vec, ssem, rsem, lsem,
):
    w = Wire(ssem, rsem, lsem)
    u, b = w.u, w.b
    z, c, zh = b // 2, b % 2, b // 4
    x, y = u % 2, u // 2
    rows = tok.shape[0]
    group = 8 * rows
    pair = 2 * rows
    greet(u, b, range(1, 8), range(1, 4), [(1, k) for k in range(1, 4)])

    par_o[pl.ds(u * 8 + b, 1)] = pack[...][None]
    p1 = [w.blk(k, pack, par_o.at[u * 8 + b]) for k in range(1, 8)]
    for r in range(8):
        for part in range(3):
            stq[r, :, part * 128:(part + 1) * 128] = wqkv[:, part * 1024 + r * 128:part * 1024 + (r + 1) * 128]
    wrow = ds((u * 8 + b) * 32, 32)
    q1 = [w.blk(k, stq.at[flip(b, k)], wqkv_o.at[wrow]) for k in range(1, 8)]
    wqkv_o[wrow] = stq[b]
    t_sib = w.blk(1, tok, x_ag.at[ds(b * rows, rows)])
    t_z = {k: w.blk(2 * k, tok, x_ag.at[ds(b * rows, rows)]) for k in (1, 2, 3)}
    x_ag[ds(b * rows, rows)] = tok[...]
    for r in range(8):
        for ch in range(4):
            src = ((ch // 2) * 16 + (r // 4) * 8 + (ch % 2) * 4 + r % 4) * 128
            stu[r, :, ch * 128:(ch + 1) * 128] = wup[:, src:src + 128]
    rank = x * 4 + b % 4
    up_row = ds((b % 4) * 32, 32)
    up_mine = wup_o.at[u, zh, up_row]
    up1 = [
        w.near(k // 4, k % 4, stu.at[flip(rank, k)], up_mine) for k in range(1, 8)
    ]
    l_up = w.here(stu.at[rank], up_mine)
    l_down = w.here(wdown, wdown_o.at[y, zh])
    l_proj = w.here(wproj, wproj_o.at[u, z, c])

    for copy in p1:
        copy.wait_recv()
    mine = par_o.at[ds(u * 8, 8)]
    p2 = [w.uly(k, mine, mine) for k in range(1, 4)]
    for copy in q1:
        copy.wait_recv()
    mine = wqkv_o.at[ds(u * 256, 256)]
    q2 = [w.uly(k, mine, mine) for k in range(1, 4)]
    t_sib.wait_recv()
    t_z[1].wait_recv()
    fwd = {}

    def to_sibling(k):
        slot = x_ag.at[ds(flip(b, 2 * k) * rows, rows)]
        fwd[k] = w.blk(1, slot, slot)

    to_sibling(1)
    d1 = w.blk(4, wdown, wdown_o.at[y, zh])
    for copy in up1:
        copy.wait_recv()
    l_up.wait()
    mine = wup_o.at[ds(y * 2, 2), zh]
    up2 = w.blk(4, mine, mine)
    pr1 = [w.blk(2 * k, wproj, wproj_o.at[u, z, c]) for k in range(1, 4)]

    for copy in p2:
        copy.wait_recv()
    for t in range(8):
        tiles = [pltpu.roll(par_o[4 * t + k], 32 * k, 1) if k else par_o[4 * t] for k in range(4)]
        vec[:, t * 128:(t + 1) * 128] = (tiles[0] + tiles[1]) + (tiles[2] + tiles[3])
    q_bias = (par_o[2 * b] + pltpu.roll(par_o[2 * b + 1], 64, 1))[6:7]
    v_bias = (par_o[16 + 2 * b] + pltpu.roll(par_o[17 + 2 * b], 64, 1))[6:7]
    bias = jnp.concatenate([q_bias, jnp.zeros_like(q_bias), v_bias], axis=1)

    def normalize(zc):
        at = ds(zc * pair, pair)
        n, _ = norm_parts(x_ag[at].astype(F32))
        n1_o[at] = (n * vec[0:1] + vec[1:2]).astype(BF)

    halo = w.take(4)
    hand = []

    def project(zc):
        at = ds(zc * pair, pair)
        out = (dot(n1_o[at], wqkv_o[...]) + bias).astype(BF)
        q_o[at] = out[:, :128]
        own = ds(group + zc * pair, pair)
        kv_o[own] = out[:, 128:]
        copy = w.make(kv_o.at[own], kv_o.at[at], (jnp.minimum(u + 1, 3), b), halo + zc)

        @pl.when(u < 3)
        def _():
            copy.start()

        hand.append(copy)

    normalize(z)
    t_z[2].wait_recv()
    to_sibling(2)
    fwd[1].wait_recv()
    normalize(flip(z, 1))
    for copy in q2:
        copy.wait_recv()
    project(z)
    project(flip(z, 1))
    t_z[3].wait_recv()
    to_sibling(3)
    for k in (2, 3):
        fwd[k].wait_recv()
        normalize(flip(z, k))
        project(flip(z, k))
    d1.wait_recv()
    l_down.wait()
    mine = wdown_o.at[y]
    d2 = w.uly(2, mine, mine)
    up2.wait_recv()
    mine = wup_o.at[ds(y * 2, 2)]
    up3 = w.uly(2, mine, mine)
    for copy in pr1:
        copy.wait_recv()
    l_proj.wait()
    mine = wproj_o.at[u, :, c]
    pr2 = [w.uly(k, mine, mine) for k in range(1, 4)]

    @pl.when(u == 0)
    def _():
        kv_o[0:group] = jnp.zeros((group, 256), BF)

    window = group + pair
    krow = lax.broadcasted_iota(jnp.int32, (window, pair), 0)
    qcol = lax.broadcasted_iota(jnp.int32, (window, pair), 1)
    causal = krow - group <= qcol
    kslope = (krow[:, :1] - group).astype(F32)
    att_at = w.take(8)
    lanes = ds(b * 128, 128)

    def attend(step, carry):
        i = 3 - step

        @pl.when(u > 0)
        def _():
            w.make(
                kv_o.at[ds(i * pair, pair)], kv_o.at[ds(i * pair, pair)], (u, b), halo + i
            ).wait_recv()

        qpos = lax.broadcasted_iota(jnp.int32, (1, pair), 1) + i * pair
        begin = doc_begin(starts, qpos + u * group) - u * group - i * pair + group
        allowed = causal & (krow >= begin)
        span = ds(i * pair, window, pair)
        keys = kv_o[span, 0:128]
        vals = kv_o[span, 128:256]
        at = ds(i * pair, pair)
        query = q_o[at]
        out = None
        for h in range(2):
            qh = jnp.where(head_mask((pair, 128), h), query, jnp.zeros_like(query))
            s = dot(keys, qh, NT) * 0.125 + slopes[2 * b + h] * kslope
            s = jnp.where(allowed, s, -1e30)
            top = jnp.max(s, axis=0, keepdims=True)
            p = jnp.exp(s - top)
            total = jnp.sum(p, axis=0, keepdims=True)
            lse_o[h:h + 1, at] = top + jnp.log(total)
            o = dot(vals, p.astype(BF), TN) * (1.0 / total)
            if h == 0:
                out = o
            else:
                out = jnp.where(lax.broadcasted_iota(jnp.int32, o.shape, 0) < 64, out, o)
        atth[at] = out.T.astype(BF)
        for half in range(2):
            target = 2 * i + half
            piece = atth.at[ds(target * rows, rows)]

            @pl.when(target != b)
            def _():
                w.make(piece, att_o.at[:, lanes], (u, target), att_at + b, att_at + target).start()

        return carry

    lax.fori_loop(0, 4, attend, 0)
    att_o[:, lanes] = atth[ds(b * rows, rows)]

    for copy in pr2:
        copy.wait_recv()
    mine = wproj_o.at[:, :, c]
    pr3 = w.blk(1, mine, mine)
    for k in range(1, 8):
        other = flip(b, k)
        w.make(
            atth.at[ds(other * rows, rows)], att_o.at[:, ds(other * 128, 128)], (u, other), att_at + other
        ).wait_recv()
        w.make(
            atth.at[ds(other * rows, rows)], att_o.at[:, lanes], (u, other), att_at + b, att_at + other
        ).wait_send()
    up3.wait_recv()
    d2.wait_recv()
    pr3.wait_recv()

    @pl.when(u < 3)
    def _():
        for copy in hand:
            copy.wait_send()

    w.finish()


def forward_call(tok, wqkv, wproj, wup, wdown, pack, slopes, starts):
    rows = tok.shape[0]
    group = 8 * rows
    v = pl.BlockSpec(memory_space=pltpu.VMEM)
    s = pl.BlockSpec(memory_space=pltpu.SMEM)
    a = pl.BlockSpec(memory_space=pl.ANY)
    sds = jax.ShapeDtypeStruct
    return pl.pallas_call(
        forward_kernel,
        name="forward_attention",
        out_shape=(
            sds((rows, 1024), BF),
            sds((group, 128), BF),
            sds((2 * group, 256), BF),
            sds((2, group), F32),
            sds((group, 1024), BF),
            sds((1024, 384), BF),
            sds((32, 8, 128), F32),
            sds((4, 4, 2, 32, 1024), BF),
            sds((4, 2, 128, 512), BF),
            sds((2, 2, rows, 1024), BF),
        ),
        in_specs=[v, v, a, v, a, v, s, s],
        out_specs=(v, v, v, v, v, v, v, a, a, a),
        scratch_shapes=[
            pltpu.VMEM((group, 1024), BF),
            pltpu.VMEM((8, 32, 384), BF),
            pltpu.VMEM((8, 32, 512), BF),
            pltpu.VMEM((group, 128), BF),
            pltpu.VMEM((8, 1024), F32),
            pltpu.SemaphoreType.DMA((64,)),
            pltpu.SemaphoreType.DMA((64,)),
            pltpu.SemaphoreType.DMA((4,)),
        ],
        compiler_params=pltpu.CompilerParams(
            collective_id=0, has_side_effects=True, vmem_limit_bytes=VMEM_LIMIT
        ),
    )(tok, wqkv, wproj, wup, wdown, pack, slopes, starts)


def pack_vectors(*vectors):
    parts = []
    for v in vectors:
        parts.append(v)
        if v.shape[0] < 128:
            parts.append(jnp.zeros((128 - v.shape[0],), v.dtype))
    return jnp.concatenate(parts).reshape(8, 128).astype(F32)


def mlp_kernel(
    tok, att, wproj, wup, wdown, cot, par,
    out_o, gmix_o, gbr_o, gatt_o, gdown_o, gup_o, small_o, upb_o,
    n_all, c_all, act_all, gup_all, p_out, p_g, s_out, s_g, z_out, z_g, keep_out, keep_g, vec, ssem, rsem,
):
    w = Wire(ssem, rsem)
    u, b = w.u, w.b
    x, c = u % 2, b % 2
    rows = tok.shape[0]
    pair = 2 * rows
    rank = x * 4 + b % 4
    hops = ((0, 2), (1, 0), (1, 2))
    greet(u, b, (), (), [(k // 4, k % 4) for k in range(1, 8)])

    def gather(src, buf):
        slot = buf.at[ds(rank * rows, rows)]
        sib = w.blk(1, src, slot)
        return sib, [w.near(ku, kb, src, slot) for ku, kb in hops]

    def pass_on(copies, buf, i):
        ku, kb = hops[i]
        copies[i].wait_recv()
        slot = buf.at[ds(flip(rank, ku * 4 + kb) * rows, rows)]
        return w.blk(1, slot, slot)

    c_sib, c_far = gather(cot, c_all)
    c_all[ds(rank * rows, rows)] = cot[...]
    for t in range(8):
        tiles = [pltpu.roll(par[4 * t + k], 32 * k, 1) if k else par[4 * t] for k in range(4)]
        vec[:, t * 128:(t + 1) * 128] = (tiles[0] + tiles[1]) + (tiles[2] + tiles[3])
    up_bias = jnp.concatenate(
        [par[(ch // 2) * 16 + x * 8 + (ch % 2) * 4 + b % 4][7:8] for ch in range(4)], axis=1
    )
    mixed = tok[...].astype(F32) + dot(att[...], wproj[...]) + vec[2:3]
    n2, inv2 = norm_parts(mixed)
    n_all[ds(rank * rows, rows)] = (n2 * vec[3:4] + vec[4:5]).astype(BF)
    n_sib, n_far = gather(n_all.at[ds(rank * rows, rows)], n_all)
    c_fwd = [pass_on(c_far, c_all, i) for i in range(3)]
    cot_f = cot[...].astype(F32)
    small_o[0:1] = jnp.sum(cot_f, axis=0, keepdims=True)

    def forward(chip):
        at = ds(chip * pair, pair)
        up = dot(n_all[at], wup[...]) + up_bias
        square = up * up
        th = jnp.tanh(0.7978845608028654 * (up + 0.044715 * square * up))
        act = (0.5 * up * (1.0 + th)).astype(BF)
        slope = 0.5 * (1.0 + th) + 0.5 * up * (1.0 - th * th) * (
            0.7978845608028654 * (1.0 + 3.0 * 0.044715 * square)
        )
        gup = (dot(c_all[at], wdown[...], NT) * slope).astype(BF)
        act_all[at] = act
        gup_all[at] = gup
        p_out[at] = dot(act, wdown[...]).astype(BF)
        p_g[at] = dot(gup, wup[...], NT).astype(BF)

    def swap(chip, i):
        other = ds(chip * pair + (1 - c) * rows, rows)
        return (w.blk(1, p_g.at[other], s_g.at[i]), w.blk(1, p_out.at[other], s_out.at[i]))

    chip = rank // 2
    c_sib.wait_recv()
    n_sib.wait_recv()
    forward(chip)
    swaps = [swap(chip, 3)]
    sends = []

    def merge(i):
        ku, kb = hops[i]
        far = flip(chip, (ku * 4 + kb) // 2)
        own = ds(far * pair + c * rows, rows)
        for copy in swaps[i + 1]:
            copy.wait_recv()
        keep_g[i] = (p_g[own].astype(F32) + s_g[i].astype(F32)).astype(BF)
        first = w.near(ku, kb, keep_g.at[i], z_g.at[i])
        keep_out[i] = (p_out[own].astype(F32) + s_out[i].astype(F32)).astype(BF)
        sends.append((first, w.near(ku, kb, keep_out.at[i], z_out.at[i])))

    n_fwd = [None] * 3
    n_fwd[0] = pass_on(n_far, n_all, 0)
    for i in range(3):
        if i < 2:
            n_fwd[i + 1] = pass_on(n_far, n_all, i + 1)
        c_fwd[i].wait_recv()
        n_fwd[i].wait_recv()
        ku, kb = hops[i]
        far = flip(chip, (ku * 4 + kb) // 2)
        forward(far)
        swaps.append(swap(far, i))
        if i > 0:
            merge(i - 1)
    merge(2)
    half = act_all.shape[1] // 2
    for j in range(2):
        span = slice(j * half, (j + 1) * half)
        gdown_o[span] = dot(act_all[:, span], c_all[...], TN).astype(BF)
        gup_o[:, span] = dot(n_all[...], gup_all[:, span], TN).astype(BF)
    upb_o[...] = jnp.sum(gup_all[...].astype(F32), axis=0, keepdims=True)

    own = ds(chip * pair + c * rows, rows)
    for copy in swaps[0]:
        copy.wait_recv()
    g = p_g[own].astype(F32) + s_g[3].astype(F32)
    for i in range(3):
        sends[i][0].wait_recv()
        g = g + z_g[i].astype(F32)
    small_o[1:2] = jnp.sum(g * n2, axis=0, keepdims=True)
    small_o[2:3] = jnp.sum(g, axis=0, keepdims=True)
    e = g * vec[3:4]
    gmix = cot_f + inv2 * (
        e - jnp.mean(e, axis=-1, keepdims=True) - n2 * jnp.mean(e * n2, axis=-1, keepdims=True)
    )
    gmix_o[...] = gmix
    small_o[3:4] = jnp.sum(gmix, axis=0, keepdims=True)
    gbr = gmix.astype(BF)
    gbr_o[...] = gbr
    gatt_o[...] = dot(gbr, wproj[...], NT).astype(BF)
    out = mixed + vec[5:6] + p_out[own].astype(F32) + s_out[3].astype(F32)
    for i in range(3):
        sends[i][1].wait_recv()
        out = out + z_out[i].astype(F32)
    out_o[...] = out.astype(BF)
    w.finish()


def mlp_call(tok, att, wproj, wup, wdown, cot, par):
    rows = tok.shape[0]
    group = 8 * rows
    width = tok.shape[1]
    hidden = wup.shape[1]
    v = pl.BlockSpec(memory_space=pltpu.VMEM)
    sds = jax.ShapeDtypeStruct
    return pl.pallas_call(
        mlp_kernel,
        name="feed_forward",
        out_shape=(
            sds((rows, width), BF),
            sds((rows, width), F32),
            sds((rows, width), BF),
            sds((rows, width), BF),
            sds((hidden, width), BF),
            sds((width, hidden), BF),
            sds((4, width), F32),
            sds((1, hidden), F32),
        ),
        in_specs=[v] * 7,
        out_specs=(v,) * 8,
        scratch_shapes=[
            pltpu.VMEM((group, width), BF),
            pltpu.VMEM((group, width), BF),
            pltpu.VMEM((group, hidden), BF),
            pltpu.VMEM((group, hidden), BF),
            pltpu.VMEM((group, width), BF),
            pltpu.VMEM((group, width), BF),
            pltpu.VMEM((4, rows, width), BF),
            pltpu.VMEM((4, rows, width), BF),
            pltpu.VMEM((3, rows, width), BF),
            pltpu.VMEM((3, rows, width), BF),
            pltpu.VMEM((3, rows, width), BF),
            pltpu.VMEM((3, rows, width), BF),
            pltpu.VMEM((8, width), F32),
            pltpu.SemaphoreType.DMA((40,)),
            pltpu.SemaphoreType.DMA((40,)),
        ],
        compiler_params=pltpu.CompilerParams(
            collective_id=1, has_side_effects=True, vmem_limit_bytes=VMEM_LIMIT
        ),
    )(tok, att, wproj, wup, wdown, cot, par)


def backward_kernel(
    tok, gatt, q, kv, lse, n1, wqkv, gmix, gbr, att, gdown, gup, small, upb, par, slopes, starts,
    in_o, down_o, up_o, qkv_o, proj_o, vec_o,
    gh, dkv, halo_b, gqkv, pieces, p_g, s_g, keep_g, z_g,
    r_down, r_up, k_down, k_up, f_down, f_up, m_up, a_up,
    p_proj, s_proj, k_proj, r_proj, m_proj, a_proj,
    p_qkv, r_qkv, m_qkv, a_qkv,
    sm, sm_r, sm_k, sm_a, vec, ssem, rsem,
):
    w = Wire(ssem, rsem)
    u, b = w.u, w.b
    z, c, zh = b // 2, b % 2, b // 4
    x, y = u % 2, u // 2
    rows = tok.shape[0]
    group = 8 * rows
    pair = 2 * rows
    rank = x * 4 + b % 4
    greet(u, b, range(1, 8), range(1, 4), [(1, k) for k in range(1, 4)])

    g_to = w.take(8)
    g_sent = []
    for k in range(1, 8):
        other = flip(b, k)
        copy = w.make(
            gatt.at[:, ds(other * 128, 128)], gh.at[ds(b * rows, rows)], (u, other), g_to + b, g_to + other
        )
        copy.start()
        g_sent.append(copy)
    gh[ds(b * rows, rows)] = gatt[:, ds(b * 128, 128)]
    y1 = w.uly(2, gdown.at[1 - y], r_down)
    y2 = w.uly(2, gup.at[ds((1 - y) * 2, 2)], r_up)
    for j in range(4):
        p_proj[j] = dot(att[:, j * 256:(j + 1) * 256], gbr[...], TN).astype(BF).reshape(4, 2, 32, 1024)
    pr1 = w.blk(1, p_proj.at[:, :, 1 - c], s_proj)
    for t in range(8):
        tiles = [pltpu.roll(par[4 * t + k], 32 * k, 1) if k else par[4 * t] for k in range(4)]
        vec[:, t * 128:(t + 1) * 128] = (tiles[0] + tiles[1]) + (tiles[2] + tiles[3])

    window = group + pair
    krow = lax.broadcasted_iota(jnp.int32, (window, pair), 0)
    qcol = lax.broadcasted_iota(jnp.int32, (window, pair), 1)
    causal = krow - group <= qcol
    kslope = (krow[:, :1] - group).astype(F32)
    dkv[...] = jnp.zeros_like(dkv)
    halo = w.take(4)

    def hand_back(i):
        at = ds(i * pair, pair)
        return w.make(
            pieces.at[at], halo_b.at[at], (jnp.maximum(u - 1, 0), b), halo + i
        )

    def attend(i):
        for half in range(2):
            source = 2 * i + half

            @pl.when(source != b)
            def _():
                w.make(
                    gatt.at[:, ds(b * 128, 128)], gh.at[ds(source * rows, rows)], (u, b), g_to + source
                ).wait_recv()

        qpos = lax.broadcasted_iota(jnp.int32, (1, pair), 1) + i * pair
        begin = doc_begin(starts, qpos + u * group) - u * group - i * pair + group
        allowed = causal & (krow >= begin)
        span = slice(i * pair, i * pair + window)
        at = slice(i * pair, (i + 1) * pair)
        keys = kv[span, 0:128]
        vals = kv[span, 128:256]
        query = q[at]
        grads = gh[at]
        dk = dv = dq = None
        for h in range(2):
            mask = head_mask((pair, 128), h)
            qh = jnp.where(mask, query, jnp.zeros_like(query))
            gr = jnp.where(mask, grads, jnp.zeros_like(grads))
            s = dot(keys, qh, NT) * 0.125 + slopes[2 * b + h] * kslope
            p = jnp.where(allowed, jnp.exp(s - lse[h:h + 1, at]), 0.0)
            dp = dot(vals, gr, NT)
            delta = jnp.sum(p * dp, axis=0, keepdims=True)
            gs = (p * (dp - delta)).astype(BF)
            dv_h = dot(p.astype(BF), gr)
            dk_h = dot(gs, qh)
            dq_h = dot(keys, gs, TN)
            if h == 0:
                dk, dv, dq = dk_h, dv_h, dq_h
            else:
                dk, dv = dk + dk_h, dv + dv_h
                dq = jnp.where(lax.broadcasted_iota(jnp.int32, dq.shape, 0) < 64, dq, dq_h)
        gqkv[at, 0:128] = (dq.T * 0.125).astype(BF)
        dkv[span, 0:128] += dk
        dkv[span, 128:256] += dv
        pieces[at] = dkv[at].astype(BF)

        @pl.when(u > 0)
        def _():
            hand_back(i).start()

    attend(0)
    attend(1)
    pr1.wait_recv()
    k_proj[...] = (p_proj[:, :, c].astype(F32) + s_proj[...].astype(F32)).astype(BF)
    pr2 = [w.uly(k, k_proj.at[flip(u, k)], r_proj.at[k - 1]) for k in range(1, 4)]
    attend(2)
    attend(3)
    y1.wait_recv()
    k_down[...] = (gdown[y].astype(F32) + r_down[...].astype(F32)).astype(BF)
    z1 = w.blk(4, k_down.at[1 - zh], f_down)
    y2.wait_recv()
    k_up[...] = (gup[ds(y * 2, 2)].astype(F32) + r_up[...].astype(F32)).astype(BF)
    z2 = w.blk(4, k_up.at[:, 1 - zh], f_up)

    for i in range(4):
        at = slice(i * pair, (i + 1) * pair)
        own = slice(group + i * pair, group + (i + 1) * pair)

        @pl.when(u < 3)
        def _():
            w.make(pieces.at[at], halo_b.at[at], (u, b), halo + i).wait_recv()
            dkv[own] += halo_b[at].astype(F32)

        gqkv[at, 128:256] = (dkv[own, 0:128] * 0.125).astype(BF)
        gqkv[at, 256:384] = dkv[own, 128:256].astype(BF)

    swaps = {}

    def spread(k):
        chip = flip(z, k)
        at = ds(chip * pair, pair)
        p_g[at] = dot(gqkv[at], wqkv[...], NT).astype(BF)
        other = ds(chip * pair + (1 - c) * rows, rows)
        swaps[k] = w.blk(1, p_g.at[other], s_g.at[k])

    sends = {}

    def merge(k):
        own = ds(flip(z, k) * pair + c * rows, rows)
        swaps[k].wait_recv()
        keep_g[k - 1] = (p_g[own].astype(F32) + s_g[k].astype(F32)).astype(BF)
        sends[k] = w.blk(2 * k, keep_g.at[k - 1], z_g.at[k - 1])

    spread(3)
    spread(2)
    merge(3)
    spread(1)
    merge(2)
    spread(0)
    merge(1)
    p_qkv[...] = dot(n1[...], gqkv[...], TN).astype(BF)
    q2 = [w.uly(k, p_qkv.at[ds(flip(u, k) * 256, 256)], r_qkv.at[k - 1]) for k in range(1, 4)]
    g_sums = jnp.sum(gqkv[...].astype(F32), axis=0, keepdims=True)

    for copy in pr2:
        copy.wait_recv()
    m_proj[...] = (
        k_proj[u].astype(F32) + r_proj[0].astype(F32) + r_proj[1].astype(F32) + r_proj[2].astype(F32)
    ).astype(BF)
    pr3 = [w.blk(2 * k, m_proj.at[flip(z, k)], a_proj.at[k - 1]) for k in range(1, 4)]
    z1.wait_recv()
    down_o[...] = (gdown[y, zh].astype(F32) + r_down[zh].astype(F32)) + f_down[...].astype(F32)
    z2.wait_recv()
    m_up[...] = (
        (gup[ds(y * 2, 2), zh].astype(F32) + r_up[:, zh].astype(F32)) + f_up[...].astype(F32)
    ).astype(BF).reshape(8, 32, 512)
    up3 = [w.near(k // 4, k % 4, m_up.at[flip(rank, k)], a_up.at[rank]) for k in range(1, 8)]
    a_up[rank] = m_up[rank]

    own = ds(b * rows, rows)
    swaps[0].wait_recv()
    g = p_g[own].astype(F32) + s_g[0].astype(F32)
    n, inv = norm_parts(tok[...].astype(F32))
    for k in (1, 2, 3):
        sends[k].wait_recv()
        g = g + z_g[k - 1].astype(F32)
    e = g * vec[0:1]
    in_o[...] = (
        gmix[...]
        + inv * (e - jnp.mean(e, axis=-1, keepdims=True) - n * jnp.mean(e * n, axis=-1, keepdims=True))
    ).astype(BF)
    lines = jnp.concatenate(
        [
            jnp.sum(g * n, axis=0, keepdims=True), jnp.sum(g, axis=0, keepdims=True),
            small[3:4], small[1:2], small[2:3], small[0:1], jnp.zeros((2, 1024), F32),
        ],
        axis=0,
    )
    for d in range(32):
        sm[d] = lines[:, (d // 4) * 128:(d // 4 + 1) * 128]
    for at, line in ((2 * b, g_sums[:, 0:128]), (16 + 2 * b, g_sums[:, 256:384])):
        sm[at, 6:7] = line
        sm[at + 1, 6:7] = line
    for ch in range(4):
        sm[(ch // 2) * 16 + x * 8 + (ch % 2) * 4 + b % 4, 7:8] = upb[:, ch * 128:(ch + 1) * 128]
    s1 = [w.uly(k, sm.at[ds(flip(u, k) * 8, 8)], sm_r.at[k - 1]) for k in range(1, 4)]

    for copy in q2:
        copy.wait_recv()
    m_qkv[...] = (
        (p_qkv[ds(u * 256, 256)].astype(F32) + r_qkv[0].astype(F32))
        + (r_qkv[1].astype(F32) + r_qkv[2].astype(F32))
    ).astype(BF).reshape(8, 32, 384)
    q3 = [w.blk(k, m_qkv.at[flip(b, k)], a_qkv.at[b]) for k in range(1, 8)]
    a_qkv[b] = m_qkv[b]
    for copy in s1:
        copy.wait_recv()
    sm_k[...] = (sm[ds(u * 8, 8)] + sm_r[0]) + (sm_r[1] + sm_r[2])
    s2 = [w.blk(k, sm_k.at[flip(b, k)], sm_a.at[k - 1]) for k in range(1, 8)]

    for copy in pr3:
        copy.wait_recv()
    proj_o[...] = (m_proj[z].astype(F32) + a_proj[0].astype(F32)) + (
        a_proj[1].astype(F32) + a_proj[2].astype(F32)
    )
    for copy in up3:
        copy.wait_recv()
    for r in range(8):
        for ch in range(4):
            to = ((ch // 2) * 16 + (r // 4) * 8 + (ch % 2) * 4 + r % 4) * 128
            up_o[:, to:to + 128] = a_up[r, :, ch * 128:(ch + 1) * 128].astype(F32)
    for copy in q3:
        copy.wait_recv()
    for r in range(8):
        for part in range(3):
            qkv_o[:, part * 1024 + r * 128:part * 1024 + (r + 1) * 128] = a_qkv[
                r, :, part * 128:(part + 1) * 128
            ].astype(F32)
    for copy in s2:
        copy.wait_recv()
    total = sm_k[b]
    for k in range(7):
        total = total + sm_a[k]
    line = lax.broadcasted_iota(jnp.int32, (8, 128), 0)
    by32 = pltpu.roll(total, (128 - 32 * (b % 4)) % 128, 1)
    by64 = pltpu.roll(total, (128 - 64 * (b % 2)) % 128, 1)
    vec_o[...] = jnp.where(line < 6, by32, jnp.where(line == 6, by64, total))
    for copy in g_sent:
        copy.wait_send()

    @pl.when(u > 0)
    def _():
        for i in range(4):
            hand_back(i).wait_send()

    w.finish()


def backward_call(tok, gatt, q, kv, lse, n1, wqkv, gmix, gbr, att, gdown, gup, small, upb, par, slopes, starts):
    rows, width = tok.shape
    group = 8 * rows
    v = pl.BlockSpec(memory_space=pltpu.VMEM)
    s = pl.BlockSpec(memory_space=pltpu.SMEM)
    sds = jax.ShapeDtypeStruct
    vm = pltpu.VMEM
    return pl.pallas_call(
        backward_kernel,
        name="backward_attention",
        out_shape=(
            sds((rows, width), BF),
            sds((rows, width), F32),
            sds((32, 4096), F32),
            sds((32, 3072), F32),
            sds((32, width), F32),
            sds((8, 128), F32),
        ),
        in_specs=[v] * 15 + [s, s],
        out_specs=(v,) * 6,
        scratch_shapes=[
            vm((group, 128), BF),
            vm((2 * group, 256), F32),
            vm((group, 256), BF),
            vm((group, 384), BF),
            vm((group, 256), BF),
            vm((group, width), BF),
            vm((4, rows, width), BF),
            vm((3, rows, width), BF),
            vm((3, rows, width), BF),
            vm((2, rows, width), BF),
            vm((2, 2, 128, 512), BF),
            vm((2, rows, width), BF),
            vm((2, 2, 128, 512), BF),
            vm((rows, width), BF),
            vm((2, 128, 512), BF),
            vm((8, 32, 512), BF),
            vm((8, 32, 512), BF),
            vm((4, 4, 2, 32, width), BF),
            vm((4, 4, 32, width), BF),
            vm((4, 4, 32, width), BF),
            vm((3, 4, 32, width), BF),
            vm((4, 32, width), BF),
            vm((3, 32, width), BF),
            vm((1024, 384), BF),
            vm((3, 256, 384), BF),
            vm((8, 32, 384), BF),
            vm((8, 32, 384), BF),
            vm((32, 8, 128), F32),
            vm((3, 8, 8, 128), F32),
            vm((8, 8, 128), F32),
            vm((7, 8, 128), F32),
            vm((8, width), F32),
            pltpu.SemaphoreType.DMA((72,)),
            pltpu.SemaphoreType.DMA((72,)),
        ],
        compiler_params=pltpu.CompilerParams(
            collective_id=2, has_side_effects=True, vmem_limit_bytes=VMEM_LIMIT
        ),
    )(tok, gatt, q, kv, lse, n1, wqkv, gmix, gbr, att, gdown, gup, small, upb, par, slopes, starts)


def fast_body(
    tokens, ln1_gain, ln1_bias, qkv_weight, qv_bias, proj_weight, proj_bias, ln2_gain, ln2_bias,
    up_weight, up_bias, down_weight, down_bias, alibi_slopes, doc_starts, cotangent,
):
    rows, width = tokens.shape
    pack = pack_vectors(
        ln1_gain, ln1_bias, proj_bias, ln2_gain, ln2_bias, down_bias, qv_bias, up_bias
    )
    att, q, kv, lse, n1, wqkv, par, wproj, wup, wdown = forward_call(
        tokens, qkv_weight, proj_weight, up_weight, down_weight, pack, alibi_slopes, doc_starts
    )
    output, gmix, gbr, gatt, gdown, gup, small, upb = mlp_call(
        tokens, att, wproj.reshape(width, width), wup.reshape(width, 512), wdown.reshape(512, width),
        cotangent, par,
    )
    grad_in, gd, gu, gq, gp, vec = backward_call(
        tokens, gatt, q, kv, lse, n1, wqkv, gmix, gbr, att,
        gdown.reshape(2, 2, rows, width), gup.reshape(4, 2, 128, 512), small, upb, par,
        alibi_slopes, doc_starts,
    )
    return (
        output, grad_in, vec[0, :32], vec[1, :32], gq, vec[6, :64], gp, vec[2, :32],
        vec[3, :32], vec[4, :32], gu, vec[7], gd, vec[5, :32],
    )


HEADS = 16
HEAD_DIM = 64


def layer_norm(values, norm_gain, norm_shift):
    center = jnp.mean(values, axis=-1, keepdims=True)
    offset = values - center
    spread = jnp.mean(offset * offset, axis=-1, keepdims=True)
    return offset * lax.rsqrt(spread + 1e-05) * norm_gain + norm_shift


def gelu_tanh(values):
    return (
        0.5
        * values
        * (1.0 + jnp.tanh(0.7978845608028654 * (values + 0.044715 * values * values * values)))
    )


def place_rows(local_rows, team_size, blk_count, tok_rows):
    team_span = team_size * tok_rows
    return (
        local_rows % team_span // tok_rows * blk_count + local_rows // team_span
    ) * tok_rows + local_rows % tok_rows


def doc_index(positions, doc_starts):
    return jnp.sum((positions[:, None] >= doc_starts[None, :]).astype(jnp.int32), axis=1) - 1


def split_rows(row_count, step_rows):
    return (row_count // step_rows, step_rows)


def score_block(queries, keys, query_pos, key_pos, query_doc, key_doc, slopes):
    raw_scores = jnp.einsum(
        "qhd,khd->hqk", queries, keys, preferred_element_type=jnp.float32
    ) * HEAD_DIM ** (-0.5)
    distance = (query_pos[:, None] - key_pos[None, :]).astype(jnp.float32)
    raw_scores = raw_scores - slopes[:, None, None] * distance[None]
    allowed = (key_pos[None, :] <= query_pos[:, None]) & (query_doc[:, None] == key_doc[None, :])
    return (jnp.where(allowed[None], raw_scores, -1e30), allowed[None])


def general_body(
    tokens,
    ln1_gain,
    ln1_bias,
    qkv_weight,
    qv_bias,
    proj_weight,
    proj_bias,
    ln2_gain,
    ln2_bias,
    up_weight,
    up_bias,
    down_weight,
    down_bias,
    alibi_slopes,
    doc_starts,
    cotangent,
):
    team_size = lax.axis_size("ulysses")
    blk_count = lax.axis_size("blk")
    tok_rows = tokens.shape[0]
    width_all = tokens.shape[1]
    head_rows = team_size * tok_rows
    heads_here = HEADS // team_size
    features = heads_here * HEAD_DIM
    scale_factor = HEAD_DIM ** (-0.5)
    gathered = (
        lax.all_gather(ln1_gain, ("ulysses", "blk"), axis=0, tiled=True),
        lax.all_gather(ln1_bias, ("ulysses", "blk"), axis=0, tiled=True),
        lax.all_gather(qkv_weight, ("ulysses", "blk"), axis=0, tiled=True),
        lax.all_gather(qv_bias, ("ulysses", "blk"), axis=0, tiled=True),
        lax.all_gather(proj_weight, ("ulysses", "blk"), axis=0, tiled=True),
        lax.all_gather(proj_bias, ("ulysses", "blk"), axis=0, tiled=True),
        lax.all_gather(ln2_gain, ("ulysses", "blk"), axis=0, tiled=True),
        lax.all_gather(ln2_bias, ("ulysses", "blk"), axis=0, tiled=True),
        lax.all_gather(up_weight, ("ulysses", "blk"), axis=0, tiled=True),
        lax.all_gather(up_bias, ("ulysses", "blk"), axis=0, tiled=True),
        lax.all_gather(down_weight, ("ulysses", "blk"), axis=0, tiled=True),
        lax.all_gather(down_bias, ("ulysses", "blk"), axis=0, tiled=True),
    )
    gain_one = gathered[0].astype(jnp.float32)
    shift_one = gathered[1].astype(jnp.float32)
    qkv_proj = gathered[2]
    qv_shift = gathered[3].astype(jnp.float32)
    proj_mat = gathered[4]
    proj_shift = gathered[5].astype(jnp.float32)
    gain_two = gathered[6].astype(jnp.float32)
    shift_two = gathered[7].astype(jnp.float32)
    up_mat = gathered[8]
    up_shift = gathered[9].astype(jnp.float32)
    down_mat = gathered[10]
    down_shift = gathered[11].astype(jnp.float32)
    inputs_f = tokens.astype(jnp.float32)
    normed_one = layer_norm(inputs_f, gain_one, shift_one).astype(jnp.bfloat16)
    joined_bias = jnp.concatenate(
        [qv_shift[:width_all], jnp.zeros((width_all,), jnp.float32), qv_shift[width_all:]]
    )
    joined = (
        jnp.dot(normed_one, qkv_proj, preferred_element_type=jnp.float32) + joined_bias
    ).astype(jnp.bfloat16)
    head_local = lax.all_to_all(
        joined.reshape(tok_rows, 3, team_size, features),
        "ulysses",
        split_axis=2,
        concat_axis=0,
        tiled=True,
    )
    queries_flat = head_local[:, 0, 0]
    queries = queries_flat.reshape(head_rows, heads_here, HEAD_DIM)
    key_value = head_local[:, 1:, 0]
    own_keys = key_value[:, 0].reshape(head_rows, heads_here, HEAD_DIM)
    own_values = key_value[:, 1].reshape(head_rows, heads_here, HEAD_DIM)
    slopes = lax.dynamic_slice_in_dim(
        alibi_slopes, lax.axis_index("ulysses") * heads_here, heads_here, 0
    )
    own_rows = lax.axis_index("blk") * head_rows + jnp.arange(head_rows, dtype=jnp.int32)
    own_pos = place_rows(own_rows, team_size, blk_count, tok_rows)
    own_doc = doc_index(own_pos, doc_starts)
    start_state = (
        jnp.full((heads_here, head_rows), -1e30, jnp.float32),
        jnp.zeros((heads_here, head_rows), jnp.float32),
        jnp.zeros((heads_here, head_rows, HEAD_DIM), jnp.float32),
    )
    carried = start_state
    piece_rows = lax.all_gather(key_value, "blk", axis=0, tiled=True)
    number, step_rows = split_rows(piece_rows.shape[0], head_rows)
    stacked = piece_rows.reshape(number, step_rows, 2, heads_here, HEAD_DIM)
    offsets = step_rows * jnp.arange(number, dtype=jnp.int32)

    def online_step(running, inputs_pair):
        best_now, norm_sum, accumulated = running
        kv_block, offset_now = inputs_pair
        key_pos = place_rows(
            offset_now + jnp.arange(step_rows, dtype=jnp.int32), team_size, blk_count, tok_rows
        )
        key_doc = doc_index(key_pos, doc_starts)
        masked, allowed = score_block(
            queries, kv_block[:, 0], own_pos, key_pos, own_doc, key_doc, slopes
        )
        best_next = jnp.maximum(best_now, jnp.max(masked, axis=-1))
        weights = jnp.where(allowed, jnp.exp(masked - best_next[..., None]), 0.0)
        shrink = jnp.exp(best_now - best_next)
        norm_sum = norm_sum * shrink + jnp.sum(weights, axis=-1)
        accumulated = accumulated * shrink[..., None] + jnp.einsum(
            "hqk,khd->hqd",
            weights.astype(jnp.bfloat16),
            kv_block[:, 1],
            preferred_element_type=jnp.float32,
        )
        return ((best_next, norm_sum, accumulated), None)

    carried, _ = lax.scan(online_step, carried, (stacked, offsets))
    best_all, norm_all, acc_all = carried
    attended_heads = acc_all / norm_all[..., None]
    log_norm = best_all + jnp.log(norm_all)
    attended_rows = (
        attended_heads.transpose(1, 0, 2).reshape(head_rows, 1, features).astype(jnp.bfloat16)
    )
    attended = lax.all_to_all(
        attended_rows, "ulysses", split_axis=0, concat_axis=1, tiled=True
    ).reshape(tok_rows, width_all)
    mixed = inputs_f + jnp.dot(attended, proj_mat, preferred_element_type=jnp.float32) + proj_shift
    normed_two = layer_norm(mixed, gain_two, shift_two).astype(jnp.bfloat16)
    up_values = jnp.dot(normed_two, up_mat, preferred_element_type=jnp.float32) + up_shift
    activated = gelu_tanh(up_values).astype(jnp.bfloat16)
    output = (
        mixed + jnp.dot(activated, down_mat, preferred_element_type=jnp.float32) + down_shift
    ).astype(jnp.bfloat16)
    contract_rows = (((0,), (0,)), ((), ()))
    contract_cols = (((1,), (1,)), ((), ()))
    grad_out = cotangent.astype(jnp.float32)
    down_grad = lax.dot_general(
        activated, cotangent, contract_rows, preferred_element_type=jnp.float32
    )
    down_bias_grad = jnp.sum(grad_out, axis=0)
    grad_act = lax.dot_general(
        cotangent, down_mat, contract_cols, preferred_element_type=jnp.float32
    )
    _, gelu_pull = jax.vjp(gelu_tanh, up_values)
    grad_up = gelu_pull(grad_act)[0].astype(jnp.bfloat16)
    up_grad = lax.dot_general(
        normed_two, grad_up, contract_rows, preferred_element_type=jnp.float32
    )
    up_bias_grad = jnp.sum(grad_up.astype(jnp.float32), axis=0)
    grad_norm_two = lax.dot_general(
        grad_up, up_mat, contract_cols, preferred_element_type=jnp.float32
    )
    _, norm_two_pull = jax.vjp(layer_norm, mixed, gain_two, shift_two)
    grad_mixed_part, ln2_gain_grad, ln2_bias_grad = norm_two_pull(grad_norm_two)
    grad_mixed = grad_out + grad_mixed_part
    grad_branch = grad_mixed.astype(jnp.bfloat16)
    proj_grad = lax.dot_general(
        attended, grad_branch, contract_rows, preferred_element_type=jnp.float32
    )
    proj_bias_grad = jnp.sum(grad_mixed, axis=0)
    grad_att = lax.dot_general(
        grad_branch, proj_mat, contract_cols, preferred_element_type=jnp.float32
    ).astype(jnp.bfloat16)
    grad_heads = lax.all_to_all(
        grad_att.reshape(tok_rows, team_size, features),
        "ulysses",
        split_axis=1,
        concat_axis=0,
        tiled=True,
    )
    grad_heads_flat = grad_heads[:, 0]
    grad_att_heads = grad_heads_flat.reshape(head_rows, heads_here, HEAD_DIM)
    delta = jnp.sum(grad_att_heads.astype(jnp.float32).transpose(1, 0, 2) * attended_heads, axis=-1)
    carried = jnp.zeros((heads_here, head_rows, HEAD_DIM), jnp.float32)
    piece_rows = lax.all_gather(key_value, "blk", axis=0, tiled=True)
    number, query_step_rows = split_rows(piece_rows.shape[0], head_rows)
    stacked = piece_rows.reshape(number, query_step_rows, 2, heads_here, HEAD_DIM)
    offsets = query_step_rows * jnp.arange(number, dtype=jnp.int32)

    def query_step(running, inputs_pair):
        kv_block, offset_now = inputs_pair
        key_pos = place_rows(
            offset_now + jnp.arange(query_step_rows, dtype=jnp.int32),
            team_size,
            blk_count,
            tok_rows,
        )
        key_doc = doc_index(key_pos, doc_starts)
        masked, allowed = score_block(
            queries, kv_block[:, 0], own_pos, key_pos, own_doc, key_doc, slopes
        )
        probs = jnp.where(allowed, jnp.exp(masked - log_norm[..., None]), 0.0)
        grad_probs = jnp.einsum(
            "qhd,khd->hqk", grad_att_heads, kv_block[:, 1], preferred_element_type=jnp.float32
        )
        grad_scores = (probs * (grad_probs - delta[..., None])).astype(jnp.bfloat16)
        running = running + jnp.einsum(
            "hqk,khd->hqd", grad_scores, kv_block[:, 0], preferred_element_type=jnp.float32
        )
        return (running, None)

    carried, _ = lax.scan(query_step, carried, (stacked, offsets))
    grad_queries = carried * scale_factor
    all_norms, all_deltas = (
        lax.all_gather(log_norm.T, "blk", axis=0, tiled=True),
        lax.all_gather(delta.T, "blk", axis=0, tiled=True),
    )
    empty_keys = jnp.zeros((head_rows, heads_here, HEAD_DIM), jnp.float32)
    carried = (empty_keys, empty_keys)
    pieces = (
        lax.all_gather(queries_flat, "blk", axis=0, tiled=True),
        lax.all_gather(grad_heads_flat, "blk", axis=0, tiled=True),
    )
    number, key_step_rows = split_rows(pieces[0].shape[0], head_rows)
    query_stack = pieces[0].reshape(number, key_step_rows, heads_here, HEAD_DIM)
    grad_stack = pieces[1].reshape(number, key_step_rows, heads_here, HEAD_DIM)
    offsets = key_step_rows * jnp.arange(number, dtype=jnp.int32)

    def key_step(running, inputs_triple):
        grad_keys_now, grad_values_now = running
        query_block, grad_block, offset_now = inputs_triple
        query_pos = place_rows(
            offset_now + jnp.arange(key_step_rows, dtype=jnp.int32), team_size, blk_count, tok_rows
        )
        query_doc = doc_index(query_pos, doc_starts)
        norm_block = lax.dynamic_slice_in_dim(all_norms, offset_now, key_step_rows, 0).T
        delta_block = lax.dynamic_slice_in_dim(all_deltas, offset_now, key_step_rows, 0).T
        masked, allowed = score_block(
            query_block, own_keys, query_pos, own_pos, query_doc, own_doc, slopes
        )
        probs = jnp.where(allowed, jnp.exp(masked - norm_block[..., None]), 0.0)
        grad_values_now = grad_values_now + jnp.einsum(
            "hqk,qhd->khd",
            probs.astype(jnp.bfloat16),
            grad_block,
            preferred_element_type=jnp.float32,
        )
        grad_probs = jnp.einsum(
            "qhd,khd->hqk", grad_block, own_values, preferred_element_type=jnp.float32
        )
        grad_scores = (probs * (grad_probs - delta_block[..., None])).astype(jnp.bfloat16)
        grad_keys_now = grad_keys_now + jnp.einsum(
            "hqk,qhd->khd", grad_scores, query_block, preferred_element_type=jnp.float32
        )
        return ((grad_keys_now, grad_values_now), None)

    carried, _ = lax.scan(key_step, carried, (query_stack, grad_stack, offsets))
    grad_keys, grad_values = carried
    grad_pack = jnp.stack(
        [
            grad_queries.transpose(1, 0, 2).reshape(head_rows, features),
            (grad_keys * scale_factor).reshape(head_rows, features),
            grad_values.reshape(head_rows, features),
        ],
        axis=1,
    ).astype(jnp.bfloat16)
    grad_joined = lax.all_to_all(
        grad_pack.reshape(head_rows, 3, 1, features),
        "ulysses",
        split_axis=0,
        concat_axis=2,
        tiled=True,
    ).reshape(tok_rows, 3 * width_all)
    qkv_grad = lax.dot_general(
        normed_one, grad_joined, contract_rows, preferred_element_type=jnp.float32
    )
    joined_sums = jnp.sum(grad_joined.astype(jnp.float32), axis=0)
    qv_bias_grad = jnp.concatenate([joined_sums[:width_all], joined_sums[2 * width_all :]])
    grad_norm_one = lax.dot_general(
        grad_joined, qkv_proj, contract_cols, preferred_element_type=jnp.float32
    )
    _, norm_one_pull = jax.vjp(layer_norm, inputs_f, gain_one, shift_one)
    grad_inputs_part, ln1_gain_grad, ln1_bias_grad = norm_one_pull(grad_norm_one)
    input_grad = (grad_mixed + grad_inputs_part).astype(jnp.bfloat16)
    shares = (
        lax.psum_scatter(ln1_gain_grad, ("ulysses", "blk"), scatter_dimension=0, tiled=True),
        lax.psum_scatter(ln1_bias_grad, ("ulysses", "blk"), scatter_dimension=0, tiled=True),
        lax.psum_scatter(qkv_grad, ("ulysses", "blk"), scatter_dimension=0, tiled=True),
        lax.psum_scatter(qv_bias_grad, ("ulysses", "blk"), scatter_dimension=0, tiled=True),
        lax.psum_scatter(proj_grad, ("ulysses", "blk"), scatter_dimension=0, tiled=True),
        lax.psum_scatter(proj_bias_grad, ("ulysses", "blk"), scatter_dimension=0, tiled=True),
        lax.psum_scatter(ln2_gain_grad, ("ulysses", "blk"), scatter_dimension=0, tiled=True),
        lax.psum_scatter(ln2_bias_grad, ("ulysses", "blk"), scatter_dimension=0, tiled=True),
        lax.psum_scatter(up_grad, ("ulysses", "blk"), scatter_dimension=0, tiled=True),
        lax.psum_scatter(up_bias_grad, ("ulysses", "blk"), scatter_dimension=0, tiled=True),
        lax.psum_scatter(down_grad, ("ulysses", "blk"), scatter_dimension=0, tiled=True),
        lax.psum_scatter(down_bias_grad, ("ulysses", "blk"), scatter_dimension=0, tiled=True),
    )
    return (
        output,
        input_grad,
        shares[0],
        shares[1],
        shares[2],
        shares[3],
        shares[4],
        shares[5],
        shares[6],
        shares[7],
        shares[8],
        shares[9],
        shares[10],
        shares[11],
    )


TOKEN_ROWS = P(("ulysses", "blk"), None)
VECTOR = P(("ulysses", "blk"))


def solution(mesh):
    whole = P()
    in_specs = (
        TOKEN_ROWS, VECTOR, VECTOR, TOKEN_ROWS, VECTOR, TOKEN_ROWS, VECTOR, VECTOR, VECTOR, TOKEN_ROWS,
        VECTOR, TOKEN_ROWS, VECTOR, whole, whole, TOKEN_ROWS,
    )
    out_specs = (
        TOKEN_ROWS, TOKEN_ROWS, VECTOR, VECTOR, TOKEN_ROWS, VECTOR, TOKEN_ROWS, VECTOR, VECTOR, VECTOR,
        TOKEN_ROWS, VECTOR, TOKEN_ROWS, VECTOR,
    )
    fits = mesh.shape["ulysses"] == 4 and mesh.shape["blk"] == 8
    return jax.shard_map(
        fast_body if fits else general_body,
        mesh=mesh, in_specs=in_specs, out_specs=out_specs, check_vma=False,
    )
```

```python
import collections
import functools

import jax
import jax.numpy as jnp
from jax import lax
from jax.experimental import pallas as pl
from jax.experimental.pallas import tpu as pltpu
from jax.sharding import PartitionSpec as P

BF = jnp.bfloat16
F32 = jnp.float32
MESH = pl.DeviceIdType.MESH
VMEM_LIMIT = 60 * 2**20
NT = (((1,), (1,)), ((), ()))
TN = (((0,), (0,)), ((), ()))
NN = (((1,), (0,)), ((), ()))


def dot(a, b, dims=NN):
    return lax.dot_general(a, b, dims, preferred_element_type=F32)


def flip(index, mask):
    out = index
    bit = 1
    while bit <= mask:
        if mask & bit:
            out = out + bit - 2 * bit * ((index // bit) % 2)
        bit *= 2
    return out


def ds(start, size, align=None):
    if not isinstance(start, int):
        start = pl.multiple_of(start, align or size)
    return pl.ds(start, size)


class Wire:
    def __init__(self, ssem, rsem, lsem=None):
        self.ssem, self.rsem, self.lsem = ssem, rsem, lsem
        self.used = 0
        self.local = 0
        self.u = lax.axis_index("ulysses")
        self.b = lax.axis_index("blk")
        self.sent = []

    def take(self, count):
        first = self.used
        self.used += count
        return first

    def make(self, src, dst, device, at, sent_at=None):
        return pltpu.make_async_remote_copy(
            src_ref=src,
            dst_ref=dst,
            send_sem=self.ssem.at[at if sent_at is None else sent_at],
            recv_sem=self.rsem.at[at],
            device_id=device,
            device_id_type=MESH,
        )

    def blk(self, k, src, dst):
        copy = self.make(src, dst, (self.u, flip(self.b, k)), self.take(1))
        copy.start()
        self.sent.append(copy)
        return copy

    def uly(self, k, src, dst):
        copy = self.make(src, dst, (flip(self.u, k), self.b), self.take(1))
        copy.start()
        self.sent.append(copy)
        return copy

    def near(self, ku, kb, src, dst):
        copy = self.make(src, dst, (flip(self.u, ku), flip(self.b, kb)), self.take(1))
        copy.start()
        self.sent.append(copy)
        return copy

    def here(self, src, dst):
        copy = pltpu.make_async_copy(src, dst, self.lsem.at[self.local])
        self.local += 1
        copy.start()
        return copy

    def finish(self):
        for copy in self.sent:
            copy.wait_send()


def greet(u, b, blk_masks, uly_masks, both=()):
    barrier = pltpu.get_barrier_semaphore()
    for k in blk_masks:
        pl.semaphore_signal(barrier, inc=1, device_id=(u, flip(b, k)), device_id_type=MESH)
    for k in uly_masks:
        pl.semaphore_signal(barrier, inc=1, device_id=(flip(u, k), b), device_id_type=MESH)
    for ku, kb in both:
        pl.semaphore_signal(barrier, inc=1, device_id=(flip(u, ku), flip(b, kb)), device_id_type=MESH)
    pl.semaphore_wait(barrier, len(blk_masks) + len(uly_masks) + len(both))


def norm_parts(values):
    center = jnp.mean(values, axis=-1, keepdims=True)
    offset = values - center
    spread = jnp.mean(offset * offset, axis=-1, keepdims=True)
    inv = lax.rsqrt(spread + 1e-05)
    return offset * inv, inv


def head_mask(shape, head):
    lane = lax.broadcasted_iota(jnp.int32, shape, len(shape) - 1)
    return (lane // 64) == head


def doc_begin(starts_ref, positions):
    begin = jnp.zeros_like(positions)
    for d in range(starts_ref.shape[0]):
        first = starts_ref[d]
        begin = jnp.where(positions >= first, jnp.full_like(positions, first), begin)
    return begin


def buffer_shapes(rows, width, hidden, heads):
    group = 8 * rows
    cols = 3 * heads
    third = hidden // 4
    return (
        ("x_all", (group, width), BF),
        ("n1", (group, width), BF),
        ("q_out", (8, 32, cols), BF),
        ("wqkv", (width, cols), BF),
        ("up_out", (8, 32, hidden), BF),
        ("wup", (4, 2, 128, hidden), BF),
        ("wdown", (2, 2, rows, width), BF),
        ("wproj", (4, 4, 2, 32, width), BF),
        ("q", (group, heads), BF),
        ("kv", (2 * group, 2 * heads), BF),
        ("lse", (2, group), F32),
        ("att_heads", (group, heads), BF),
        ("att", (rows, width), BF),
        ("par", (32, 8, 128), F32),
        ("vec", (8, width), F32),
        ("n2_all", (group, width), BF),
        ("c_all", (group, width), BF),
        ("act", (group, hidden), BF),
        ("gup", (group, hidden), BF),
        ("out_part", (group, width), BF),
        ("g2_part", (group, width), BF),
        ("out_sib", (4, rows, width), BF),
        ("g2_sib", (4, rows, width), BF),
        ("out_keep", (3, rows, width), BF),
        ("g2_keep", (3, rows, width), BF),
        ("out_far", (3, rows, width), BF),
        ("g2_far", (3, rows, width), BF),
        ("mixed", (rows, width), F32),
        ("gmix", (rows, width), F32),
        ("gbr", (rows, width), BF),
        ("gatt", (rows, width), BF),
        ("dwn", (2, 2, rows, width), BF),
        ("dup", (4, 2, 128, hidden), BF),
        ("dwn_y", (2, rows, width), BF),
        ("dup_y", (2, 2, 128, hidden), BF),
        ("dwn_keep", (2, rows, width), BF),
        ("dup_keep", (2, 2, 128, hidden), BF),
        ("dwn_z", (rows, width), BF),
        ("dup_z", (2, 128, hidden), BF),
        ("dup_own", (8, 32, hidden), BF),
        ("gh", (group, heads), BF),
        ("dkv", (2 * group, 2 * heads), F32),
        ("halo_out", (group, 2 * heads), BF),
        ("halo_in", (group, 2 * heads), BF),
        ("gqkv", (group, cols), BF),
        ("g1_part", (group, width), BF),
        ("g1_sib", (4, rows, width), BF),
        ("g1_keep", (3, rows, width), BF),
        ("g1_far", (3, rows, width), BF),
        ("dpr", (4, 4, 2, 32, width), BF),
        ("dpr_sib", (4, 4, 32, width), BF),
        ("dpr_keep", (4, 4, 32, width), BF),
        ("dpr_u", (3, 4, 32, width), BF),
        ("dpr_own", (4, 32, width), BF),
        ("dpr_z", (3, 32, width), BF),
        ("dq", (width, cols), BF),
        ("dq_u", (3, 256, cols), BF),
        ("dq_own", (8, 32, cols), BF),
        ("sm", (32, 8, 128), F32),
        ("sm_u", (3, 8, 8, 128), F32),
        ("sm_keep", (8, 8, 128), F32),
        ("sm_b", (7, 8, 128), F32),
    )


SEMAPHORES = 200


def block_kernel(shapes, *refs):
    (
        tok, wqkv_in, wproj_in, wup_in, wdown_in, cot,
        ln1_gain, ln1_bias, proj_bias, ln2_gain, ln2_bias, down_bias, qv_bias, up_bias_in, slopes, starts,
    ) = refs[:16]
    out_o, in_o, down_o, up_o, qkv_o, proj_o, vec_o = refs[16:23]
    ssem, rsem, lsem = refs[23 + len(shapes):]
    m = collections.namedtuple("Buffers", [s[0] for s in shapes])(*refs[23:23 + len(shapes)])

    w = Wire(ssem, rsem, lsem)
    u, b = w.u, w.b
    z, c, zh = b // 2, b % 2, b // 4
    x, y = u % 2, u // 2
    rows, width = tok.shape
    group = 8 * rows
    pair = 2 * rows
    rank = x * 4 + b % 4
    chip2 = rank // 2
    mine_b = ds(b * rows, rows)
    mine_r = ds(rank * rows, rows)
    at = u * 8 + b
    m.par[at] = jnp.zeros((8, 128), F32)
    for row, v in enumerate((ln1_gain, ln1_bias, proj_bias, ln2_gain, ln2_bias, down_bias, qv_bias, up_bias_in)):
        m.par[at, row:row + 1, 0:v.shape[0]] = v[...].astype(F32).reshape(1, v.shape[0])
    greet(u, b, range(1, 8), range(1, 4), [(1, k) for k in range(1, 4)])

    p1 = [w.blk(k, m.par.at[at], m.par.at[at]) for k in range(1, 8)]
    slot = m.x_all.at[mine_b]
    t_z = {2: w.blk(4, tok, slot), 1: w.blk(2, tok, slot)}
    t_sib = w.blk(1, tok, slot)
    m.x_all[mine_b] = tok[...]
    for r in range(8):
        for part in range(3):
            m.q_out[r, :, part * 128:(part + 1) * 128] = wqkv_in[
                :, part * width + r * 128:part * width + (r + 1) * 128
            ]
    wrow = ds(at * 32, 32)
    q1 = [w.blk(k, m.q_out.at[flip(b, k)], m.wqkv.at[wrow]) for k in range(1, 8)]
    m.wqkv[wrow] = m.q_out[b]
    for r in range(8):
        for ch in range(4):
            src = ((ch // 2) * 16 + (r // 4) * 8 + (ch % 2) * 4 + r % 4) * 128
            m.up_out[r, :, ch * 128:(ch + 1) * 128] = wup_in[:, src:src + 128]
    up_mine = m.wup.at[u, zh, ds((b % 4) * 32, 32)]
    up1 = [w.near(k // 4, k % 4, m.up_out.at[flip(rank, k)], up_mine) for k in range(1, 8)]
    l_up = w.here(m.up_out.at[rank], up_mine)
    l_down = w.here(wdown_in, m.wdown.at[y, zh])
    l_proj = w.here(wproj_in, m.wproj.at[u, z, c])

    for copy in p1:
        copy.wait_recv()
    mine = m.par.at[ds(u * 8, 8)]
    p2 = [w.uly(k, mine, mine) for k in range(1, 4)]
    for copy in q1:
        copy.wait_recv()
    mine = m.wqkv.at[ds(u * 256, 256)]
    q2 = [w.uly(k, mine, mine) for k in range(1, 4)]

    fwd = {}

    def to_sibling(k):
        slot = m.x_all.at[ds(flip(b, 2 * k) * rows, rows)]
        fwd[k] = w.blk(1, slot, slot)

    t_z[2].wait_recv()
    slot = m.x_all.at[ds(flip(b, 4) * rows, rows)]
    t_z[3] = w.blk(2, slot, slot)
    to_sibling(2)
    d1 = w.blk(4, wdown_in, m.wdown.at[y, zh])
    for copy in up1:
        copy.wait_recv()
    l_up.wait()
    mine = m.wup.at[ds(y * 2, 2), zh]
    up2 = w.blk(4, mine, mine)
    pr1 = {k: w.blk(2 * k, wproj_in, m.wproj.at[u, z, c]) for k in (2, 1)}

    for copy in p2:
        copy.wait_recv()
    for t in range(8):
        tiles = [pltpu.roll(m.par[4 * t + k], 32 * k, 1) if k else m.par[4 * t] for k in range(4)]
        m.vec[:, t * 128:(t + 1) * 128] = (tiles[0] + tiles[1]) + (tiles[2] + tiles[3])
    vec = m.vec
    q_bias = (m.par[2 * b] + pltpu.roll(m.par[2 * b + 1], 64, 1))[6:7]
    v_bias = (m.par[16 + 2 * b] + pltpu.roll(m.par[17 + 2 * b], 64, 1))[6:7]
    bias = jnp.concatenate([q_bias, jnp.zeros_like(q_bias), v_bias], axis=1)
    up_bias = jnp.concatenate(
        [m.par[(ch // 2) * 16 + x * 8 + (ch % 2) * 4 + b % 4][7:8] for ch in range(4)], axis=1
    )

    def normalize(zc):
        at = ds(zc * pair, pair)
        n, _ = norm_parts(m.x_all[at].astype(F32))
        m.n1[at] = (n * vec[0:1] + vec[1:2]).astype(BF)

    halo = w.take(4)
    hand = []

    def project(zc):
        at = ds(zc * pair, pair)
        out = (dot(m.n1[at], m.wqkv[...]) + bias).astype(BF)
        m.q[at] = out[:, :128]
        own = ds(group + zc * pair, pair)
        m.kv[own] = out[:, 128:]
        copy = w.make(m.kv.at[own], m.kv.at[at], (jnp.minimum(u + 1, 3), b), halo + zc)

        @pl.when(u < 3)
        def _():
            copy.start()

        hand.append(copy)

    t_sib.wait_recv()
    normalize(z)
    t_z[1].wait_recv()
    to_sibling(1)
    fwd[2].wait_recv()
    normalize(flip(z, 2))
    for copy in q2:
        copy.wait_recv()
    project(z)
    project(flip(z, 2))
    fwd[1].wait_recv()
    normalize(flip(z, 1))
    project(flip(z, 1))
    t_z[3].wait_recv()
    to_sibling(3)
    d1.wait_recv()
    l_down.wait()
    mine = m.wdown.at[y]
    d2 = w.uly(2, mine, mine)
    fwd[3].wait_recv()
    normalize(flip(z, 3))
    project(flip(z, 3))
    pr1[2].wait_recv()
    slot = m.wproj.at[u, flip(z, 2), c]
    pr1[3] = w.blk(2, slot, slot)
    up2.wait_recv()
    mine = m.wup.at[ds(y * 2, 2)]
    up3 = w.uly(2, mine, mine)

    hops = ((0, 2), (1, 0), (1, 2))

    def gather(src, buf):
        slot = buf.at[mine_r]
        return w.blk(1, src, slot), [w.near(ku, kb, src, slot) for ku, kb in hops]

    def pass_on(copies, buf, i):
        ku, kb = hops[i]
        copies[i].wait_recv()
        slot = buf.at[ds(flip(rank, ku * 4 + kb) * rows, rows)]
        return w.blk(1, slot, slot)

    c_sib, c_far = gather(cot, m.c_all)
    m.c_all[mine_r] = cot[...]

    @pl.when(u == 0)
    def _():
        m.kv[0:group] = jnp.zeros((group, 256), BF)

    window = group + pair
    krow = lax.broadcasted_iota(jnp.int32, (window, pair), 0)
    qcol = lax.broadcasted_iota(jnp.int32, (window, pair), 1)
    causal = krow - group <= qcol
    kslope = (krow[:, :1] - group).astype(F32)
    att_at = w.take(8)
    lanes = ds(b * 128, 128)

    def allowed_pairs(i):
        qpos = lax.broadcasted_iota(jnp.int32, (1, pair), 1) + i * pair
        begin = doc_begin(starts, qpos + u * group) - u * group - i * pair + group
        return causal & (krow >= begin)

    def attend(step, carry):
        i = 3 - step

        @pl.when(u > 0)
        def _():
            w.make(
                m.kv.at[ds(i * pair, pair)], m.kv.at[ds(i * pair, pair)], (u, b), halo + i
            ).wait_recv()

        allowed = allowed_pairs(i)
        span = ds(i * pair, window, pair)
        keys = m.kv[span, 0:128]
        vals = m.kv[span, 128:256]
        at = ds(i * pair, pair)
        query = m.q[at]
        out = None
        for h in range(2):
            qh = jnp.where(head_mask((pair, 128), h), query, jnp.zeros_like(query))
            s = dot(keys, qh, NT) * 0.125 + slopes[2 * b + h] * kslope
            s = jnp.where(allowed, s, -1e30)
            top = jnp.max(s, axis=0, keepdims=True)
            p = jnp.exp(s - top)
            total = jnp.sum(p, axis=0, keepdims=True)
            m.lse[h:h + 1, at] = top + jnp.log(total)
            o = dot(vals, p.astype(BF), TN) * (1.0 / total)
            if h == 0:
                out = o
            else:
                out = jnp.where(lax.broadcasted_iota(jnp.int32, o.shape, 0) < 64, out, o)
        m.att_heads[at] = out.T.astype(BF)
        for half in range(2):
            target = 2 * i + half
            piece = m.att_heads.at[ds(target * rows, rows)]

            @pl.when(target != b)
            def _():
                w.make(piece, m.att.at[:, lanes], (u, target), att_at + b, att_at + target).start()

        return carry

    lax.fori_loop(0, 4, attend, 0)
    m.att[:, lanes] = m.att_heads[mine_b]
    pr1[1].wait_recv()
    pr1[3].wait_recv()
    l_proj.wait()
    mine = m.wproj.at[u, :, c]
    pr2 = [w.uly(k, mine, mine) for k in range(1, 4)]
    c_fwd = [pass_on(c_far, m.c_all, i) for i in range(3)]
    cot_f = cot[...].astype(F32)
    down_bias_sum = jnp.sum(cot_f, axis=0, keepdims=True)
    for copy in pr2:
        copy.wait_recv()
    mine = m.wproj.at[:, :, c]
    pr3 = w.blk(1, mine, mine)
    for k in range(1, 8):
        other = flip(b, k)
        w.make(
            m.att_heads.at[ds(other * rows, rows)], m.att.at[:, ds(other * 128, 128)], (u, other), att_at + other
        ).wait_recv()
        w.make(
            m.att_heads.at[ds(other * rows, rows)], m.att.at[:, lanes], (u, other), att_at + b, att_at + other
        ).wait_send()
    pr3.wait_recv()

    wproj = m.wproj[...].reshape(width, width)
    mixed = tok[...].astype(F32) + dot(m.att[...], wproj) + vec[2:3]
    m.mixed[...] = mixed
    n2, inv2 = norm_parts(mixed)
    m.n2_all[mine_r] = (n2 * vec[3:4] + vec[4:5]).astype(BF)
    n_sib, n_far = gather(m.n2_all.at[mine_r], m.n2_all)
    up3.wait_recv()
    d2.wait_recv()
    hidden = m.act.shape[1]
    wup = m.wup[...].reshape(width, hidden)
    wdown = m.wdown[...].reshape(hidden, width)

    def feed(chip):
        at = ds(chip * pair, pair)
        up = dot(m.n2_all[at], wup) + up_bias
        square = up * up
        th = jnp.tanh(0.7978845608028654 * (up + 0.044715 * square * up))
        act = (0.5 * up * (1.0 + th)).astype(BF)
        slope = 0.5 * (1.0 + th) + 0.5 * up * (1.0 - th * th) * (
            0.7978845608028654 * (1.0 + 3.0 * 0.044715 * square)
        )
        gup = (dot(m.c_all[at], wdown, NT) * slope).astype(BF)
        m.act[at] = act
        m.gup[at] = gup
        m.g2_part[at] = dot(gup, wup, NT).astype(BF)
        m.out_part[at] = dot(act, wdown).astype(BF)

    def swap(chip, i):
        other = ds(chip * pair + (1 - c) * rows, rows)
        return (
            w.blk(1, m.g2_part.at[other], m.g2_sib.at[i]),
            w.blk(1, m.out_part.at[other], m.out_sib.at[i]),
        )

    c_sib.wait_recv()
    n_sib.wait_recv()
    feed(chip2)
    swaps = [swap(chip2, 3)]
    g2_sends, out_sends = [], []

    def merge(i):
        ku, kb = hops[i]
        far = flip(chip2, (ku * 4 + kb) // 2)
        own = ds(far * pair + c * rows, rows)
        swaps[i + 1][0].wait_recv()
        m.g2_keep[i] = (m.g2_part[own].astype(F32) + m.g2_sib[i].astype(F32)).astype(BF)
        g2_sends.append(w.near(ku, kb, m.g2_keep.at[i], m.g2_far.at[i]))

    def merge_out(i):
        ku, kb = hops[i]
        far = flip(chip2, (ku * 4 + kb) // 2)
        own = ds(far * pair + c * rows, rows)
        swaps[i + 1][1].wait_recv()
        m.out_keep[i] = (m.out_part[own].astype(F32) + m.out_sib[i].astype(F32)).astype(BF)
        out_sends.append(w.near(ku, kb, m.out_keep.at[i], m.out_far.at[i]))

    n_fwd = [pass_on(n_far, m.n2_all, 0)]
    for i in range(3):
        if i < 2:
            n_fwd.append(pass_on(n_far, m.n2_all, i + 1))
        c_fwd[i].wait_recv()
        n_fwd[i].wait_recv()
        ku, kb = hops[i]
        far = flip(chip2, (ku * 4 + kb) // 2)
        feed(far)
        swaps.append(swap(far, i))
        if i > 0:
            merge(i - 1)
    merge(2)
    half = hidden // 2
    for j in range(2):
        span = slice(j * half, (j + 1) * half)
        m.dwn[j] = dot(m.act[:, span], m.c_all[...], TN).astype(BF).reshape(2, rows, width)
    y1 = w.uly(2, m.dwn.at[1 - y], m.dwn_y)
    for j in range(2):
        span = slice(j * half, (j + 1) * half)
        m.dup[:, :, :, span] = dot(m.n2_all[...], m.gup[:, span], TN).astype(BF).reshape(4, 2, 128, half)
    y2 = w.uly(2, m.dup.at[ds((1 - y) * 2, 2)], m.dup_y)
    up_bias_sum = jnp.sum(m.gup[...].astype(F32), axis=0, keepdims=True)

    own = ds(chip2 * pair + c * rows, rows)
    swaps[0][0].wait_recv()
    g = m.g2_part[own].astype(F32) + m.g2_sib[3].astype(F32)
    for i in range(3):
        g2_sends[i].wait_recv()
        g = g + m.g2_far[i].astype(F32)
    ln2_gain_sum = jnp.sum(g * n2, axis=0, keepdims=True)
    ln2_bias_sum = jnp.sum(g, axis=0, keepdims=True)
    e = g * vec[3:4]
    gmix = cot_f + inv2 * (
        e - jnp.mean(e, axis=-1, keepdims=True) - n2 * jnp.mean(e * n2, axis=-1, keepdims=True)
    )
    m.gmix[...] = gmix
    proj_bias_sum = jnp.sum(gmix, axis=0, keepdims=True)
    gbr = gmix.astype(BF)
    m.gbr[...] = gbr
    m.gatt[...] = dot(gbr, wproj, NT).astype(BF)

    g_to = w.take(8)
    g_sent = []
    for k in range(1, 8):
        other = flip(b, k)
        copy = w.make(
            m.gatt.at[:, ds(other * 128, 128)], m.gh.at[mine_b], (u, other), g_to + b, g_to + other
        )
        copy.start()
        g_sent.append(copy)
    m.gh[mine_b] = m.gatt[:, ds(b * 128, 128)]
    for i in range(3):
        merge_out(i)
    for j in range(4):
        m.dpr[j] = dot(m.att[:, j * 256:(j + 1) * 256], gbr, TN).astype(BF).reshape(4, 2, 32, width)
    pg1 = w.blk(1, m.dpr.at[:, :, 1 - c], m.dpr_sib)
    m.dkv[...] = jnp.zeros_like(m.dkv)
    back = w.take(4)

    def hand_back(i):
        at = ds(i * pair, pair)
        return w.make(m.halo_out.at[at], m.halo_in.at[at], (jnp.maximum(u - 1, 0), b), back + i)

    def attend_back(i):
        for half in range(2):
            source = 2 * i + half

            @pl.when(source != b)
            def _():
                w.make(
                    m.gatt.at[:, lanes], m.gh.at[ds(source * rows, rows)], (u, b), g_to + source
                ).wait_recv()

        allowed = allowed_pairs(i)
        span = slice(i * pair, i * pair + window)
        at = slice(i * pair, (i + 1) * pair)
        keys = m.kv[span, 0:128]
        vals = m.kv[span, 128:256]
        query = m.q[at]
        grads = m.gh[at]
        dk = dv = dq = None
        for h in range(2):
            mask = head_mask((pair, 128), h)
            qh = jnp.where(mask, query, jnp.zeros_like(query))
            gr = jnp.where(mask, grads, jnp.zeros_like(grads))
            s = dot(keys, qh, NT) * 0.125 + slopes[2 * b + h] * kslope
            p = jnp.where(allowed, jnp.exp(s - m.lse[h:h + 1, at]), 0.0)
            dp = dot(vals, gr, NT)
            delta = jnp.sum(p * dp, axis=0, keepdims=True)
            gs = (p * (dp - delta)).astype(BF)
            dv_h = dot(p.astype(BF), gr)
            dk_h = dot(gs, qh)
            dq_h = dot(keys, gs, TN)
            if h == 0:
                dk, dv, dq = dk_h, dv_h, dq_h
            else:
                dk, dv = dk + dk_h, dv + dv_h
                dq = jnp.where(lax.broadcasted_iota(jnp.int32, dq.shape, 0) < 64, dq, dq_h)
        m.gqkv[at, 0:128] = (dq.T * 0.125).astype(BF)
        m.dkv[span, 0:128] += dk
        m.dkv[span, 128:256] += dv
        m.halo_out[at] = m.dkv[at].astype(BF)

        @pl.when(u > 0)
        def _():
            hand_back(i).start()

    attend_back(0)
    attend_back(1)
    pg1.wait_recv()
    m.dpr_keep[...] = (m.dpr[:, :, c].astype(F32) + m.dpr_sib[...].astype(F32)).astype(BF)
    pg2 = [w.uly(k, m.dpr_keep.at[flip(u, k)], m.dpr_u.at[k - 1]) for k in range(1, 4)]
    y1.wait_recv()
    m.dwn_keep[...] = (m.dwn[y].astype(F32) + m.dwn_y[...].astype(F32)).astype(BF)
    z1 = w.blk(4, m.dwn_keep.at[1 - zh], m.dwn_z)
    attend_back(2)
    attend_back(3)
    y2.wait_recv()
    m.dup_keep[...] = (m.dup[ds(y * 2, 2)].astype(F32) + m.dup_y[...].astype(F32)).astype(BF)
    z2 = w.blk(4, m.dup_keep.at[:, 1 - zh], m.dup_z)

    for i in range(4):
        at = slice(i * pair, (i + 1) * pair)
        own = slice(group + i * pair, group + (i + 1) * pair)

        @pl.when(u < 3)
        def _():
            w.make(m.halo_out.at[at], m.halo_in.at[at], (u, b), back + i).wait_recv()
            m.dkv[own] += m.halo_in[at].astype(F32)

        m.gqkv[at, 128:256] = (m.dkv[own, 0:128] * 0.125).astype(BF)
        m.gqkv[at, 256:384] = m.dkv[own, 128:256].astype(BF)

    swaps1 = {}

    def spread(k):
        chip = flip(z, k)
        at = ds(chip * pair, pair)
        m.g1_part[at] = dot(m.gqkv[at], m.wqkv[...], NT).astype(BF)
        other = ds(chip * pair + (1 - c) * rows, rows)
        swaps1[k] = w.blk(1, m.g1_part.at[other], m.g1_sib.at[k])

    def chip_sum(k):
        own = ds(flip(z, k) * pair + c * rows, rows)
        swaps1[k].wait_recv()
        return m.g1_part[own].astype(F32) + m.g1_sib[k].astype(F32)

    spread(3)
    spread(1)
    m.g1_keep[2] = chip_sum(3).astype(BF)
    via = w.blk(2, m.g1_keep.at[2], m.g1_far.at[2])
    spread(2)
    m.g1_keep[0] = chip_sum(1).astype(BF)
    g1_near = w.blk(2, m.g1_keep.at[0], m.g1_far.at[0])
    spread(0)
    sum2 = chip_sum(2)
    via.wait_recv()
    m.g1_keep[1] = (sum2 + m.g1_far[2].astype(F32)).astype(BF)
    g1_cross = w.blk(4, m.g1_keep.at[1], m.g1_far.at[1])
    m.dq[...] = dot(m.n1[...], m.gqkv[...], TN).astype(BF)
    q2g = [w.uly(k, m.dq.at[ds(flip(u, k) * 256, 256)], m.dq_u.at[k - 1]) for k in range(1, 4)]
    qv_sums = jnp.sum(m.gqkv[...].astype(F32), axis=0, keepdims=True)

    own = ds(chip2 * pair + c * rows, rows)
    swaps[0][1].wait_recv()
    out = m.mixed[...] + vec[5:6] + m.out_part[own].astype(F32) + m.out_sib[3].astype(F32)
    for i in range(3):
        out_sends[i].wait_recv()
        out = out + m.out_far[i].astype(F32)
    out_o[...] = out.astype(BF)
    for copy in pg2:
        copy.wait_recv()
    m.dpr_own[...] = (
        (m.dpr_keep[u].astype(F32) + m.dpr_u[0].astype(F32)) + (m.dpr_u[1].astype(F32) + m.dpr_u[2].astype(F32))
    ).astype(BF)
    pg3 = [w.blk(2 * k, m.dpr_own.at[flip(z, k)], m.dpr_z.at[k - 1]) for k in range(1, 4)]
    z1.wait_recv()
    down_o[...] = (m.dwn[y, zh].astype(F32) + m.dwn_y[zh].astype(F32)) + m.dwn_z[...].astype(F32)
    z2.wait_recv()
    m.dup_own[...] = (
        (m.dup[ds(y * 2, 2), zh].astype(F32) + m.dup_y[:, zh].astype(F32)) + m.dup_z[...].astype(F32)
    ).astype(BF).reshape(8, 32, hidden)
    up3g = [w.near(k // 4, k % 4, m.dup_own.at[flip(rank, k)], up_o.at[rank]) for k in range(1, 8)]
    up_o[rank] = m.dup_own[rank]
    for copy in q2g:
        copy.wait_recv()
    m.dq_own[...] = (
        (m.dq[ds(u * 256, 256)].astype(F32) + m.dq_u[0].astype(F32))
        + (m.dq_u[1].astype(F32) + m.dq_u[2].astype(F32))
    ).astype(BF).reshape(8, 32, 384)
    q3g = [w.blk(k, m.dq_own.at[flip(b, k)], qkv_o.at[b]) for k in range(1, 8)]
    qkv_o[b] = m.dq_own[b]

    n, inv = norm_parts(tok[...].astype(F32))
    g = chip_sum(0)
    g1_near.wait_recv()
    g1_cross.wait_recv()
    g = g + m.g1_far[0].astype(F32) + m.g1_far[1].astype(F32)
    lines = jnp.concatenate(
        [
            jnp.sum(g * n, axis=0, keepdims=True), jnp.sum(g, axis=0, keepdims=True),
            proj_bias_sum, ln2_gain_sum, ln2_bias_sum, down_bias_sum, jnp.zeros((2, width), F32),
        ],
        axis=0,
    )
    for d in range(32):
        m.sm[d] = lines[:, (d // 4) * 128:(d // 4 + 1) * 128]
    for at, line in ((2 * b, qv_sums[:, 0:128]), (16 + 2 * b, qv_sums[:, 256:384])):
        m.sm[at, 6:7] = line
        m.sm[at + 1, 6:7] = line
    for ch in range(4):
        m.sm[(ch // 2) * 16 + x * 8 + (ch % 2) * 4 + b % 4, 7:8] = up_bias_sum[:, ch * 128:(ch + 1) * 128]
    s1 = [w.uly(k, m.sm.at[ds(flip(u, k) * 8, 8)], m.sm_u.at[k - 1]) for k in range(1, 4)]
    e = g * vec[0:1]
    in_o[...] = (
        m.gmix[...]
        + inv * (e - jnp.mean(e, axis=-1, keepdims=True) - n * jnp.mean(e * n, axis=-1, keepdims=True))
    ).astype(BF)
    for copy in pg3:
        copy.wait_recv()
    proj_o[...] = (m.dpr_own[z].astype(F32) + m.dpr_z[0].astype(F32)) + (
        m.dpr_z[1].astype(F32) + m.dpr_z[2].astype(F32)
    )
    for copy in s1:
        copy.wait_recv()
    m.sm_keep[...] = (m.sm[ds(u * 8, 8)] + m.sm_u[0]) + (m.sm_u[1] + m.sm_u[2])
    s2 = [w.blk(k, m.sm_keep.at[flip(b, k)], m.sm_b.at[k - 1]) for k in range(1, 8)]
    for copy in up3g + q3g + s2:
        copy.wait_recv()
    total = m.sm_keep[b]
    for k in range(7):
        total = total + m.sm_b[k]
    line = lax.broadcasted_iota(jnp.int32, (8, 128), 0)
    by32 = pltpu.roll(total, (128 - 32 * (b % 4)) % 128, 1)
    by64 = pltpu.roll(total, (128 - 64 * (b % 2)) % 128, 1)
    vec_o[...] = jnp.where(line < 6, by32, jnp.where(line == 6, by64, total))

    for copy in g_sent:
        copy.wait_send()

    @pl.when(u < 3)
    def _():
        for copy in hand:
            copy.wait_send()

    @pl.when(u > 0)
    def _():
        for i in range(4):
            hand_back(i).wait_send()

    w.finish()


def finish_kernel(
    out, grad_in, down, up, qkv, proj, vec,
    out_o, in_o, g1_o, b1_o, qkv_o, qv_o, proj_o, pb_o, g2_o, b2_o, up_o, ub_o, down_o, db_o,
):
    out_o[...] = out[...]
    in_o[...] = grad_in[...]
    down_o[...] = down[...]
    proj_o[...] = proj[...]
    for r in range(8):
        for ch in range(4):
            to = ((ch // 2) * 16 + (r // 4) * 8 + (ch % 2) * 4 + r % 4) * 128
            up_o[:, to:to + 128] = up[r, :, ch * 128:(ch + 1) * 128].astype(F32)
        for part in range(3):
            to = part * 1024 + r * 128
            qkv_o[:, to:to + 128] = qkv[r, :, part * 128:(part + 1) * 128].astype(F32)
    for row, ref in enumerate((g1_o, b1_o, pb_o, g2_o, b2_o, db_o, qv_o, ub_o)):
        ref[...] = vec[row, 0:ref.shape[0]]


def fast_body(
    tokens, ln1_gain, ln1_bias, qkv_weight, qv_bias, proj_weight, proj_bias, ln2_gain, ln2_bias,
    up_weight, up_bias, down_weight, down_bias, alibi_slopes, doc_starts, cotangent,
):
    rows, width = tokens.shape
    shapes = buffer_shapes(rows, width, 512, 128)
    v = pl.BlockSpec(memory_space=pltpu.VMEM)
    s = pl.BlockSpec(memory_space=pltpu.SMEM)
    sds = jax.ShapeDtypeStruct
    parts = pl.pallas_call(
        functools.partial(block_kernel, shapes),
        name="transformer_block",
        out_shape=(
            sds((rows, width), BF),
            sds((rows, width), BF),
            sds((rows, width), F32),
            sds((8, 32, 512), BF),
            sds((8, 32, 384), BF),
            sds((32, width), F32),
            sds((8, 128), F32),
        ),
        in_specs=[v] * 14 + [s, s],
        out_specs=(v,) * 7,
        scratch_shapes=[pltpu.VMEM(shape, kind) for _, shape, kind in shapes]
        + [
            pltpu.SemaphoreType.DMA((SEMAPHORES,)),
            pltpu.SemaphoreType.DMA((SEMAPHORES,)),
            pltpu.SemaphoreType.DMA((4,)),
        ],
        compiler_params=pltpu.CompilerParams(
            collective_id=0, has_side_effects=True, vmem_limit_bytes=VMEM_LIMIT
        ),
    )(
        tokens, qkv_weight, proj_weight, up_weight, down_weight, cotangent,
        ln1_gain, ln1_bias, proj_bias, ln2_gain, ln2_bias, down_bias, qv_bias, up_bias,
        alibi_slopes, doc_starts,
    )
    vector = sds((32,), F32)
    return pl.pallas_call(
        finish_kernel,
        name="lay_out",
        out_shape=(
            sds((rows, width), BF), sds((rows, width), BF), vector, vector, sds((32, 3072), F32),
            sds((64,), F32), sds((32, width), F32), vector, vector, vector, sds((32, 4096), F32),
            sds((128,), F32), sds((rows, width), F32), vector,
        ),
        in_specs=[v] * 7,
        out_specs=(v,) * 14,
        compiler_params=pltpu.CompilerParams(vmem_limit_bytes=VMEM_LIMIT),
    )(*parts)


HEADS = 16
HEAD_DIM = 64


def layer_norm(values, norm_gain, norm_shift):
    center = jnp.mean(values, axis=-1, keepdims=True)
    offset = values - center
    spread = jnp.mean(offset * offset, axis=-1, keepdims=True)
    return offset * lax.rsqrt(spread + 1e-05) * norm_gain + norm_shift


def gelu_tanh(values):
    return (
        0.5
        * values
        * (1.0 + jnp.tanh(0.7978845608028654 * (values + 0.044715 * values * values * values)))
    )


def place_rows(local_rows, team_size, blk_count, tok_rows):
    team_span = team_size * tok_rows
    return (
        local_rows % team_span // tok_rows * blk_count + local_rows // team_span
    ) * tok_rows + local_rows % tok_rows


def doc_index(positions, doc_starts):
    return jnp.sum((positions[:, None] >= doc_starts[None, :]).astype(jnp.int32), axis=1) - 1


def split_rows(row_count, step_rows):
    return (row_count // step_rows, step_rows)


def score_block(queries, keys, query_pos, key_pos, query_doc, key_doc, slopes):
    raw_scores = jnp.einsum(
        "qhd,khd->hqk", queries, keys, preferred_element_type=jnp.float32
    ) * HEAD_DIM ** (-0.5)
    distance = (query_pos[:, None] - key_pos[None, :]).astype(jnp.float32)
    raw_scores = raw_scores - slopes[:, None, None] * distance[None]
    allowed = (key_pos[None, :] <= query_pos[:, None]) & (query_doc[:, None] == key_doc[None, :])
    return (jnp.where(allowed[None], raw_scores, -1e30), allowed[None])


def general_body(
    tokens,
    ln1_gain,
    ln1_bias,
    qkv_weight,
    qv_bias,
    proj_weight,
    proj_bias,
    ln2_gain,
    ln2_bias,
    up_weight,
    up_bias,
    down_weight,
    down_bias,
    alibi_slopes,
    doc_starts,
    cotangent,
):
    team_size = lax.axis_size("ulysses")
    blk_count = lax.axis_size("blk")
    tok_rows = tokens.shape[0]
    width_all = tokens.shape[1]
    head_rows = team_size * tok_rows
    heads_here = HEADS // team_size
    features = heads_here * HEAD_DIM
    scale_factor = HEAD_DIM ** (-0.5)
    gathered = (
        lax.all_gather(ln1_gain, ("ulysses", "blk"), axis=0, tiled=True),
        lax.all_gather(ln1_bias, ("ulysses", "blk"), axis=0, tiled=True),
        lax.all_gather(qkv_weight, ("ulysses", "blk"), axis=0, tiled=True),
        lax.all_gather(qv_bias, ("ulysses", "blk"), axis=0, tiled=True),
        lax.all_gather(proj_weight, ("ulysses", "blk"), axis=0, tiled=True),
        lax.all_gather(proj_bias, ("ulysses", "blk"), axis=0, tiled=True),
        lax.all_gather(ln2_gain, ("ulysses", "blk"), axis=0, tiled=True),
        lax.all_gather(ln2_bias, ("ulysses", "blk"), axis=0, tiled=True),
        lax.all_gather(up_weight, ("ulysses", "blk"), axis=0, tiled=True),
        lax.all_gather(up_bias, ("ulysses", "blk"), axis=0, tiled=True),
        lax.all_gather(down_weight, ("ulysses", "blk"), axis=0, tiled=True),
        lax.all_gather(down_bias, ("ulysses", "blk"), axis=0, tiled=True),
    )
    gain_one = gathered[0].astype(jnp.float32)
    shift_one = gathered[1].astype(jnp.float32)
    qkv_proj = gathered[2]
    qv_shift = gathered[3].astype(jnp.float32)
    proj_mat = gathered[4]
    proj_shift = gathered[5].astype(jnp.float32)
    gain_two = gathered[6].astype(jnp.float32)
    shift_two = gathered[7].astype(jnp.float32)
    up_mat = gathered[8]
    up_shift = gathered[9].astype(jnp.float32)
    down_mat = gathered[10]
    down_shift = gathered[11].astype(jnp.float32)
    inputs_f = tokens.astype(jnp.float32)
    normed_one = layer_norm(inputs_f, gain_one, shift_one).astype(jnp.bfloat16)
    joined_bias = jnp.concatenate(
        [qv_shift[:width_all], jnp.zeros((width_all,), jnp.float32), qv_shift[width_all:]]
    )
    joined = (
        jnp.dot(normed_one, qkv_proj, preferred_element_type=jnp.float32) + joined_bias
    ).astype(jnp.bfloat16)
    head_local = lax.all_to_all(
        joined.reshape(tok_rows, 3, team_size, features),
        "ulysses",
        split_axis=2,
        concat_axis=0,
        tiled=True,
    )
    queries_flat = head_local[:, 0, 0]
    queries = queries_flat.reshape(head_rows, heads_here, HEAD_DIM)
    key_value = head_local[:, 1:, 0]
    own_keys = key_value[:, 0].reshape(head_rows, heads_here, HEAD_DIM)
    own_values = key_value[:, 1].reshape(head_rows, heads_here, HEAD_DIM)
    slopes = lax.dynamic_slice_in_dim(
        alibi_slopes, lax.axis_index("ulysses") * heads_here, heads_here, 0
    )
    own_rows = lax.axis_index("blk") * head_rows + jnp.arange(head_rows, dtype=jnp.int32)
    own_pos = place_rows(own_rows, team_size, blk_count, tok_rows)
    own_doc = doc_index(own_pos, doc_starts)
    start_state = (
        jnp.full((heads_here, head_rows), -1e30, jnp.float32),
        jnp.zeros((heads_here, head_rows), jnp.float32),
        jnp.zeros((heads_here, head_rows, HEAD_DIM), jnp.float32),
    )
    carried = start_state
    piece_rows = lax.all_gather(key_value, "blk", axis=0, tiled=True)
    number, step_rows = split_rows(piece_rows.shape[0], head_rows)
    stacked = piece_rows.reshape(number, step_rows, 2, heads_here, HEAD_DIM)
    offsets = step_rows * jnp.arange(number, dtype=jnp.int32)

    def online_step(running, inputs_pair):
        best_now, norm_sum, accumulated = running
        kv_block, offset_now = inputs_pair
        key_pos = place_rows(
            offset_now + jnp.arange(step_rows, dtype=jnp.int32), team_size, blk_count, tok_rows
        )
        key_doc = doc_index(key_pos, doc_starts)
        masked, allowed = score_block(
            queries, kv_block[:, 0], own_pos, key_pos, own_doc, key_doc, slopes
        )
        best_next = jnp.maximum(best_now, jnp.max(masked, axis=-1))
        weights = jnp.where(allowed, jnp.exp(masked - best_next[..., None]), 0.0)
        shrink = jnp.exp(best_now - best_next)
        norm_sum = norm_sum * shrink + jnp.sum(weights, axis=-1)
        accumulated = accumulated * shrink[..., None] + jnp.einsum(
            "hqk,khd->hqd",
            weights.astype(jnp.bfloat16),
            kv_block[:, 1],
            preferred_element_type=jnp.float32,
        )
        return ((best_next, norm_sum, accumulated), None)

    carried, _ = lax.scan(online_step, carried, (stacked, offsets))
    best_all, norm_all, acc_all = carried
    attended_heads = acc_all / norm_all[..., None]
    log_norm = best_all + jnp.log(norm_all)
    attended_rows = (
        attended_heads.transpose(1, 0, 2).reshape(head_rows, 1, features).astype(jnp.bfloat16)
    )
    attended = lax.all_to_all(
        attended_rows, "ulysses", split_axis=0, concat_axis=1, tiled=True
    ).reshape(tok_rows, width_all)
    mixed = inputs_f + jnp.dot(attended, proj_mat, preferred_element_type=jnp.float32) + proj_shift
    normed_two = layer_norm(mixed, gain_two, shift_two).astype(jnp.bfloat16)
    up_values = jnp.dot(normed_two, up_mat, preferred_element_type=jnp.float32) + up_shift
    activated = gelu_tanh(up_values).astype(jnp.bfloat16)
    output = (
        mixed + jnp.dot(activated, down_mat, preferred_element_type=jnp.float32) + down_shift
    ).astype(jnp.bfloat16)
    contract_rows = (((0,), (0,)), ((), ()))
    contract_cols = (((1,), (1,)), ((), ()))
    grad_out = cotangent.astype(jnp.float32)
    down_grad = lax.dot_general(
        activated, cotangent, contract_rows, preferred_element_type=jnp.float32
    )
    down_bias_grad = jnp.sum(grad_out, axis=0)
    grad_act = lax.dot_general(
        cotangent, down_mat, contract_cols, preferred_element_type=jnp.float32
    )
    _, gelu_pull = jax.vjp(gelu_tanh, up_values)
    grad_up = gelu_pull(grad_act)[0].astype(jnp.bfloat16)
    up_grad = lax.dot_general(
        normed_two, grad_up, contract_rows, preferred_element_type=jnp.float32
    )
    up_bias_grad = jnp.sum(grad_up.astype(jnp.float32), axis=0)
    grad_norm_two = lax.dot_general(
        grad_up, up_mat, contract_cols, preferred_element_type=jnp.float32
    )
    _, norm_two_pull = jax.vjp(layer_norm, mixed, gain_two, shift_two)
    grad_mixed_part, ln2_gain_grad, ln2_bias_grad = norm_two_pull(grad_norm_two)
    grad_mixed = grad_out + grad_mixed_part
    grad_branch = grad_mixed.astype(jnp.bfloat16)
    proj_grad = lax.dot_general(
        attended, grad_branch, contract_rows, preferred_element_type=jnp.float32
    )
    proj_bias_grad = jnp.sum(grad_mixed, axis=0)
    grad_att = lax.dot_general(
        grad_branch, proj_mat, contract_cols, preferred_element_type=jnp.float32
    ).astype(jnp.bfloat16)
    grad_heads = lax.all_to_all(
        grad_att.reshape(tok_rows, team_size, features),
        "ulysses",
        split_axis=1,
        concat_axis=0,
        tiled=True,
    )
    grad_heads_flat = grad_heads[:, 0]
    grad_att_heads = grad_heads_flat.reshape(head_rows, heads_here, HEAD_DIM)
    delta = jnp.sum(grad_att_heads.astype(jnp.float32).transpose(1, 0, 2) * attended_heads, axis=-1)
    carried = jnp.zeros((heads_here, head_rows, HEAD_DIM), jnp.float32)
    piece_rows = lax.all_gather(key_value, "blk", axis=0, tiled=True)
    number, query_step_rows = split_rows(piece_rows.shape[0], head_rows)
    stacked = piece_rows.reshape(number, query_step_rows, 2, heads_here, HEAD_DIM)
    offsets = query_step_rows * jnp.arange(number, dtype=jnp.int32)

    def query_step(running, inputs_pair):
        kv_block, offset_now = inputs_pair
        key_pos = place_rows(
            offset_now + jnp.arange(query_step_rows, dtype=jnp.int32),
            team_size,
            blk_count,
            tok_rows,
        )
        key_doc = doc_index(key_pos, doc_starts)
        masked, allowed = score_block(
            queries, kv_block[:, 0], own_pos, key_pos, own_doc, key_doc, slopes
        )
        probs = jnp.where(allowed, jnp.exp(masked - log_norm[..., None]), 0.0)
        grad_probs = jnp.einsum(
            "qhd,khd->hqk", grad_att_heads, kv_block[:, 1], preferred_element_type=jnp.float32
        )
        grad_scores = (probs * (grad_probs - delta[..., None])).astype(jnp.bfloat16)
        running = running + jnp.einsum(
            "hqk,khd->hqd", grad_scores, kv_block[:, 0], preferred_element_type=jnp.float32
        )
        return (running, None)

    carried, _ = lax.scan(query_step, carried, (stacked, offsets))
    grad_queries = carried * scale_factor
    all_norms, all_deltas = (
        lax.all_gather(log_norm.T, "blk", axis=0, tiled=True),
        lax.all_gather(delta.T, "blk", axis=0, tiled=True),
    )
    empty_keys = jnp.zeros((head_rows, heads_here, HEAD_DIM), jnp.float32)
    carried = (empty_keys, empty_keys)
    pieces = (
        lax.all_gather(queries_flat, "blk", axis=0, tiled=True),
        lax.all_gather(grad_heads_flat, "blk", axis=0, tiled=True),
    )
    number, key_step_rows = split_rows(pieces[0].shape[0], head_rows)
    query_stack = pieces[0].reshape(number, key_step_rows, heads_here, HEAD_DIM)
    grad_stack = pieces[1].reshape(number, key_step_rows, heads_here, HEAD_DIM)
    offsets = key_step_rows * jnp.arange(number, dtype=jnp.int32)

    def key_step(running, inputs_triple):
        grad_keys_now, grad_values_now = running
        query_block, grad_block, offset_now = inputs_triple
        query_pos = place_rows(
            offset_now + jnp.arange(key_step_rows, dtype=jnp.int32), team_size, blk_count, tok_rows
        )
        query_doc = doc_index(query_pos, doc_starts)
        norm_block = lax.dynamic_slice_in_dim(all_norms, offset_now, key_step_rows, 0).T
        delta_block = lax.dynamic_slice_in_dim(all_deltas, offset_now, key_step_rows, 0).T
        masked, allowed = score_block(
            query_block, own_keys, query_pos, own_pos, query_doc, own_doc, slopes
        )
        probs = jnp.where(allowed, jnp.exp(masked - norm_block[..., None]), 0.0)
        grad_values_now = grad_values_now + jnp.einsum(
            "hqk,qhd->khd",
            probs.astype(jnp.bfloat16),
            grad_block,
            preferred_element_type=jnp.float32,
        )
        grad_probs = jnp.einsum(
            "qhd,khd->hqk", grad_block, own_values, preferred_element_type=jnp.float32
        )
        grad_scores = (probs * (grad_probs - delta_block[..., None])).astype(jnp.bfloat16)
        grad_keys_now = grad_keys_now + jnp.einsum(
            "hqk,qhd->khd", grad_scores, query_block, preferred_element_type=jnp.float32
        )
        return ((grad_keys_now, grad_values_now), None)

    carried, _ = lax.scan(key_step, carried, (query_stack, grad_stack, offsets))
    grad_keys, grad_values = carried
    grad_pack = jnp.stack(
        [
            grad_queries.transpose(1, 0, 2).reshape(head_rows, features),
            (grad_keys * scale_factor).reshape(head_rows, features),
            grad_values.reshape(head_rows, features),
        ],
        axis=1,
    ).astype(jnp.bfloat16)
    grad_joined = lax.all_to_all(
        grad_pack.reshape(head_rows, 3, 1, features),
        "ulysses",
        split_axis=0,
        concat_axis=2,
        tiled=True,
    ).reshape(tok_rows, 3 * width_all)
    qkv_grad = lax.dot_general(
        normed_one, grad_joined, contract_rows, preferred_element_type=jnp.float32
    )
    joined_sums = jnp.sum(grad_joined.astype(jnp.float32), axis=0)
    qv_bias_grad = jnp.concatenate([joined_sums[:width_all], joined_sums[2 * width_all :]])
    grad_norm_one = lax.dot_general(
        grad_joined, qkv_proj, contract_cols, preferred_element_type=jnp.float32
    )
    _, norm_one_pull = jax.vjp(layer_norm, inputs_f, gain_one, shift_one)
    grad_inputs_part, ln1_gain_grad, ln1_bias_grad = norm_one_pull(grad_norm_one)
    input_grad = (grad_mixed + grad_inputs_part).astype(jnp.bfloat16)
    shares = (
        lax.psum_scatter(ln1_gain_grad, ("ulysses", "blk"), scatter_dimension=0, tiled=True),
        lax.psum_scatter(ln1_bias_grad, ("ulysses", "blk"), scatter_dimension=0, tiled=True),
        lax.psum_scatter(qkv_grad, ("ulysses", "blk"), scatter_dimension=0, tiled=True),
        lax.psum_scatter(qv_bias_grad, ("ulysses", "blk"), scatter_dimension=0, tiled=True),
        lax.psum_scatter(proj_grad, ("ulysses", "blk"), scatter_dimension=0, tiled=True),
        lax.psum_scatter(proj_bias_grad, ("ulysses", "blk"), scatter_dimension=0, tiled=True),
        lax.psum_scatter(ln2_gain_grad, ("ulysses", "blk"), scatter_dimension=0, tiled=True),
        lax.psum_scatter(ln2_bias_grad, ("ulysses", "blk"), scatter_dimension=0, tiled=True),
        lax.psum_scatter(up_grad, ("ulysses", "blk"), scatter_dimension=0, tiled=True),
        lax.psum_scatter(up_bias_grad, ("ulysses", "blk"), scatter_dimension=0, tiled=True),
        lax.psum_scatter(down_grad, ("ulysses", "blk"), scatter_dimension=0, tiled=True),
        lax.psum_scatter(down_bias_grad, ("ulysses", "blk"), scatter_dimension=0, tiled=True),
    )
    return (
        output,
        input_grad,
        shares[0],
        shares[1],
        shares[2],
        shares[3],
        shares[4],
        shares[5],
        shares[6],
        shares[7],
        shares[8],
        shares[9],
        shares[10],
        shares[11],
    )


TOKEN_ROWS = P(("ulysses", "blk"), None)
VECTOR = P(("ulysses", "blk"))


def solution(mesh):
    whole = P()
    in_specs = (
        TOKEN_ROWS, VECTOR, VECTOR, TOKEN_ROWS, VECTOR, TOKEN_ROWS, VECTOR, VECTOR, VECTOR, TOKEN_ROWS,
        VECTOR, TOKEN_ROWS, VECTOR, whole, whole, TOKEN_ROWS,
    )
    out_specs = (
        TOKEN_ROWS, TOKEN_ROWS, VECTOR, VECTOR, TOKEN_ROWS, VECTOR, TOKEN_ROWS, VECTOR, VECTOR, VECTOR,
        TOKEN_ROWS, VECTOR, TOKEN_ROWS, VECTOR,
    )
    fits = mesh.shape["ulysses"] == 4 and mesh.shape["blk"] == 8
    return jax.shard_map(
        fast_body if fits else general_body,
        mesh=mesh, in_specs=in_specs, out_specs=out_specs, check_vma=False,
    )
```

```python
import collections
import functools

import jax
import jax.numpy as jnp
from jax import lax
from jax.experimental import pallas as pl
from jax.experimental.pallas import tpu as pltpu
from jax.sharding import PartitionSpec as P

BF = jnp.bfloat16
F32 = jnp.float32
MESH = pl.DeviceIdType.MESH
VMEM_LIMIT = 60 * 2**20
NT = (((1,), (1,)), ((), ()))
TN = (((0,), (0,)), ((), ()))
NN = (((1,), (0,)), ((), ()))


def dot(a, b, dims=NN):
    return lax.dot_general(a, b, dims, preferred_element_type=F32)


def flip(index, mask):
    out = index
    bit = 1
    while bit <= mask:
        if mask & bit:
            out = out + bit - 2 * bit * ((index // bit) % 2)
        bit *= 2
    return out


def ds(start, size, align=None):
    if not isinstance(start, int):
        start = pl.multiple_of(start, align or size)
    return pl.ds(start, size)


class Wire:
    def __init__(self, ssem, rsem, lsem=None):
        self.ssem, self.rsem, self.lsem = ssem, rsem, lsem
        self.used = 0
        self.local = 0
        self.u = lax.axis_index("ulysses")
        self.b = lax.axis_index("blk")
        self.sent = []

    def take(self, count):
        first = self.used
        self.used += count
        return first

    def make(self, src, dst, device, at, sent_at=None):
        return pltpu.make_async_remote_copy(
            src_ref=src,
            dst_ref=dst,
            send_sem=self.ssem.at[at if sent_at is None else sent_at],
            recv_sem=self.rsem.at[at],
            device_id=device,
            device_id_type=MESH,
        )

    def blk(self, k, src, dst):
        copy = self.make(src, dst, (self.u, flip(self.b, k)), self.take(1))
        copy.start()
        self.sent.append(copy)
        return copy

    def uly(self, k, src, dst):
        copy = self.make(src, dst, (flip(self.u, k), self.b), self.take(1))
        copy.start()
        self.sent.append(copy)
        return copy

    def near(self, ku, kb, src, dst):
        copy = self.make(src, dst, (flip(self.u, ku), flip(self.b, kb)), self.take(1))
        copy.start()
        self.sent.append(copy)
        return copy

    def here(self, src, dst):
        copy = pltpu.make_async_copy(src, dst, self.lsem.at[self.local])
        self.local += 1
        copy.start()
        return copy

    def finish(self):
        for copy in self.sent:
            copy.wait_send()


def partners(u, b):
    near = [(u, flip(b, k)) for k in range(1, 8)] + [(flip(u, k), b) for k in range(1, 4)]
    return near + [(flip(u, 1), flip(b, k)) for k in range(1, 4)]


def send_barrier(u, b):
    for device in partners(u, b):
        pl.semaphore_signal(pltpu.get_barrier_semaphore(), inc=1, device_id=device, device_id_type=MESH)


def wait_barrier():
    pl.semaphore_wait(pltpu.get_barrier_semaphore(), 13)


def norm_parts(values):
    center = jnp.mean(values, axis=-1, keepdims=True)
    offset = values - center
    spread = jnp.mean(offset * offset, axis=-1, keepdims=True)
    inv = lax.rsqrt(spread + 1e-05)
    return offset * inv, inv


def head_mask(shape, head):
    lane = lax.broadcasted_iota(jnp.int32, shape, len(shape) - 1)
    return (lane // 64) == head


def doc_begin(starts_ref, positions):
    begin = jnp.zeros_like(positions)
    for d in range(starts_ref.shape[0]):
        first = starts_ref[d]
        begin = jnp.where(positions >= first, jnp.full_like(positions, first), begin)
    return begin


def buffer_shapes(rows, width, hidden, heads):
    group = 8 * rows
    cols = 3 * heads
    third = hidden // 4
    return (
        ("x_all", (group, width), BF),
        ("n1", (group, width), BF),
        ("q_out", (8, 32, cols), BF),
        ("wqkv", (width, cols), BF),
        ("up_out", (8, 32, hidden), BF),
        ("wup", (4, 2, 128, hidden), BF),
        ("wdown", (2, 2, rows, width), BF),
        ("wproj", (4, 4, 2, 32, width), BF),
        ("q", (group, heads), BF),
        ("kv", (2 * group, 2 * heads), BF),
        ("lse", (2, group), F32),
        ("att_heads", (group, heads), BF),
        ("att", (rows, width), BF),
        ("par", (32, 8, 128), F32),
        ("vec", (8, width), F32),
        ("n2_all", (group, width), BF),
        ("c_all", (group, width), BF),
        ("act", (group, hidden), BF),
        ("gup", (group, hidden), BF),
        ("out_part", (group, width), BF),
        ("g2_part", (group, width), BF),
        ("out_sib", (4, rows, width), BF),
        ("g2_sib", (4, rows, width), BF),
        ("out_keep", (3, rows, width), BF),
        ("g2_keep", (3, rows, width), BF),
        ("out_far", (3, rows, width), BF),
        ("g2_far", (3, rows, width), BF),
        ("mixed", (rows, width), F32),
        ("gmix", (rows, width), F32),
        ("gbr", (rows, width), BF),
        ("gatt", (rows, width), BF),
        ("dwn", (2, 2, rows, width), BF),
        ("dup", (4, 2, 128, hidden), BF),
        ("dwn_y", (2, rows, width), BF),
        ("dup_y", (2, 2, 128, hidden), BF),
        ("dwn_keep", (rows, width), BF),
        ("dup_keep", (2, 128, hidden), BF),
        ("dwn_z", (rows, width), BF),
        ("dup_z", (2, 128, hidden), BF),
        ("dup_own", (8, 32, hidden), BF),
        ("gh", (group, heads), BF),
        ("dkv", (2 * group, 2 * heads), F32),
        ("halo_out", (group, 2 * heads), BF),
        ("halo_in", (group, 2 * heads), BF),
        ("gqkv", (group, cols), BF),
        ("g1_part", (group, width), BF),
        ("g1_sib", (4, rows, width), BF),
        ("g1_keep", (3, rows, width), BF),
        ("g1_far", (3, rows, width), BF),
        ("dpr", (4, 4, 2, 32, width), BF),
        ("dpr_sib", (4, 4, 32, width), BF),
        ("dpr_keep", (4, 4, 32, width), BF),
        ("dpr_u", (3, 4, 32, width), BF),
        ("dpr_own", (4, 32, width), BF),
        ("dpr_z", (3, 32, width), BF),
        ("dq", (width, cols), BF),
        ("dq_u", (3, 256, cols), BF),
        ("dq_own", (8, 32, cols), BF),
        ("sm", (32, 8, 128), F32),
        ("sm_u", (3, 8, 8, 128), F32),
        ("sm_keep", (8, 8, 128), F32),
        ("sm_b", (7, 8, 128), F32),
    )


SEMAPHORES = 161


def block_kernel(shapes, *refs):
    (
        tok, wqkv_in, wproj_in, wup_in, wdown_in, cot,
        ln1_gain, ln1_bias, proj_bias, ln2_gain, ln2_bias, down_bias, qv_bias, up_bias_in, slopes, starts,
    ) = refs[:16]
    out_o, in_o, down_o, up_o, qkv_o, proj_o, vec_o = refs[16:23]
    ssem, rsem, lsem = refs[23 + len(shapes):]
    m = collections.namedtuple("Buffers", [s[0] for s in shapes])(*refs[23:23 + len(shapes)])

    w = Wire(ssem, rsem, lsem)
    u, b = w.u, w.b
    z, c, zh = b // 2, b % 2, b // 4
    x, y = u % 2, u // 2
    rows, width = tok.shape
    group = 8 * rows
    pair = 2 * rows
    rank = x * 4 + b % 4
    chip2 = rank // 2
    mine_b = ds(b * rows, rows)
    mine_r = ds(rank * rows, rows)
    at = u * 8 + b
    send_barrier(u, b)
    m.par[at] = jnp.zeros((8, 128), F32)
    for row, v in enumerate((ln1_gain, ln1_bias, proj_bias, ln2_gain, ln2_bias, down_bias, qv_bias, up_bias_in)):
        m.par[at, row:row + 1, 0:v.shape[0]] = v[...].astype(F32).reshape(1, v.shape[0])
    for r in range(8):
        for part in range(3):
            m.q_out[r, :, part * 128:(part + 1) * 128] = wqkv_in[
                :, part * width + r * 128:part * width + (r + 1) * 128
            ]
    wrow = ds(at * 32, 32)
    m.wqkv[wrow] = m.q_out[b]
    for r in range(8):
        for ch in range(4):
            src = ((ch // 2) * 16 + (r // 4) * 8 + (ch % 2) * 4 + r % 4) * 128
            m.up_out[r, :, ch * 128:(ch + 1) * 128] = wup_in[:, src:src + 128]
    m.x_all[mine_b] = tok[...]
    m.c_all[mine_r] = cot[...]
    wait_barrier()

    q1 = [w.blk(k, m.q_out.at[flip(b, k)], m.wqkv.at[wrow]) for k in range(1, 8)]
    p1 = [w.blk(k, m.par.at[at], m.par.at[at]) for k in range(1, 8)]
    up_mine = m.wup.at[u, zh, ds((b % 4) * 32, 32)]
    pr1 = {k: w.blk(2 * k, wproj_in, m.wproj.at[u, z, c]) for k in (2, 1)}
    pr2 = [w.uly(k, wproj_in, m.wproj.at[u, z, c]) for k in range(1, 4)]

    def proj_on(k):
        pr1[k].wait_recv()
        slot = m.wproj.at[u, flip(z, k), c]
        pr2.extend([w.uly(j, slot, slot) for j in range(1, 4)])

    t_sib = w.blk(1, tok, m.x_all.at[mine_b])
    c_x = w.uly(1, cot, m.c_all.at[mine_r])
    d2 = [w.uly(2, wdown_in, m.wdown.at[y, zh])]
    c_sib = w.blk(1, cot, m.c_all.at[mine_r])
    l_up = w.here(m.up_out.at[rank], up_mine)
    l_down = w.here(wdown_in, m.wdown.at[y, zh])
    l_proj = w.here(wproj_in, m.wproj.at[u, z, c])

    for copy in p1:
        copy.wait_recv()
    mine = m.par.at[ds(u * 8, 8)]
    p2 = [w.uly(k, mine, mine) for k in range(1, 4)]
    for copy in q1:
        copy.wait_recv()
    mine = m.wqkv.at[ds(u * 256, 256)]
    q2 = [w.uly(k, mine, mine) for k in range(1, 4)]
    proj_on(2)
    slot = m.wproj.at[u, flip(z, 2), c]
    pr1[3] = w.blk(2, slot, slot)
    proj_on(1)
    slot = m.x_all.at[mine_b]
    t_z = {2: w.blk(4, tok, slot), 1: w.blk(2, tok, slot)}

    fwd = {}

    def to_sibling(k):
        slot = m.x_all.at[ds(flip(b, 2 * k) * rows, rows)]
        fwd[k] = w.blk(1, slot, slot)

    t_z[2].wait_recv()
    slot = m.x_all.at[ds(flip(b, 4) * rows, rows)]
    t_z[3] = w.blk(2, slot, slot)
    to_sibling(2)
    for copy in p2:
        copy.wait_recv()
    for t in range(8):
        tiles = [pltpu.roll(m.par[4 * t + k], 32 * k, 1) if k else m.par[4 * t] for k in range(4)]
        m.vec[:, t * 128:(t + 1) * 128] = (tiles[0] + tiles[1]) + (tiles[2] + tiles[3])
    vec = m.vec
    q_bias = (m.par[2 * b] + pltpu.roll(m.par[2 * b + 1], 64, 1))[6:7]
    v_bias = (m.par[16 + 2 * b] + pltpu.roll(m.par[17 + 2 * b], 64, 1))[6:7]
    bias = jnp.concatenate([q_bias, jnp.zeros_like(q_bias), v_bias], axis=1)
    up_bias = jnp.concatenate(
        [m.par[(ch // 2) * 16 + x * 8 + (ch % 2) * 4 + b % 4][7:8] for ch in range(4)], axis=1
    )

    def normalize(zc):
        at = ds(zc * pair, pair)
        n, _ = norm_parts(m.x_all[at].astype(F32))
        m.n1[at] = (n * vec[0:1] + vec[1:2]).astype(BF)

    halo = w.take(4)
    hand = []

    def project(zc):
        at = ds(zc * pair, pair)
        out = (dot(m.n1[at], m.wqkv[...]) + bias).astype(BF)
        m.q[at] = out[:, :128]
        own = ds(group + zc * pair, pair)
        m.kv[own] = out[:, 128:]
        copy = w.make(m.kv.at[own], m.kv.at[at], (jnp.minimum(u + 1, 3), b), halo + zc)

        @pl.when(u < 3)
        def _():
            copy.start()

        hand.append(copy)

    t_sib.wait_recv()
    normalize(z)
    t_z[1].wait_recv()
    to_sibling(1)
    up1 = [w.near(k // 4, k % 4, m.up_out.at[flip(rank, k)], up_mine) for k in range(1, 8)]
    proj_on(3)
    fwd[2].wait_recv()
    normalize(flip(z, 2))
    for copy in q2:
        copy.wait_recv()
    project(z)
    project(flip(z, 2))
    fwd[1].wait_recv()
    normalize(flip(z, 1))
    project(flip(z, 1))
    t_z[3].wait_recv()
    to_sibling(3)
    c_z = w.blk(2, cot, m.c_all.at[mine_r])
    d1 = w.blk(4, wdown_in, m.wdown.at[y, zh])
    c_x.wait_recv()
    slot = m.c_all.at[ds(flip(rank, 4) * rows, rows)]
    c_fwd = [w.blk(1, slot, slot)]
    fwd[3].wait_recv()
    normalize(flip(z, 3))
    project(flip(z, 3))
    for copy in up1:
        copy.wait_recv()
    l_up.wait()
    mine = m.wup.at[ds(y * 2, 2), zh]
    up2 = w.blk(4, mine, mine)
    up3 = [w.uly(2, mine, mine)]
    @pl.when(u == 0)
    def _():
        m.kv[0:group] = jnp.zeros((group, 256), BF)

    window = group + pair
    krow = lax.broadcasted_iota(jnp.int32, (window, pair), 0)
    qcol = lax.broadcasted_iota(jnp.int32, (window, pair), 1)
    causal = krow - group <= qcol
    kslope = (krow[:, :1] - group).astype(F32)
    att_at = w.take(8)
    lanes = ds(b * 128, 128)

    def allowed_pairs(i):
        qpos = lax.broadcasted_iota(jnp.int32, (1, pair), 1) + i * pair
        begin = doc_begin(starts, qpos + u * group) - u * group - i * pair + group
        return causal & (krow >= begin)

    def attend(i):
        @pl.when(u > 0)
        def _():
            w.make(
                m.kv.at[ds(i * pair, pair)], m.kv.at[ds(i * pair, pair)], (u, b), halo + i
            ).wait_recv()

        allowed = allowed_pairs(i)
        span = slice(i * pair, i * pair + window)
        keys = m.kv[span, 0:128]
        vals = m.kv[span, 128:256]
        at = slice(i * pair, (i + 1) * pair)
        query = m.q[at]
        out = None
        for h in range(2):
            qh = jnp.where(head_mask((pair, 128), h), query, jnp.zeros_like(query))
            s = dot(keys, qh, NT) * 0.125 + slopes[2 * b + h] * kslope
            s = jnp.where(allowed, s, -1e30)
            top = jnp.max(s, axis=0, keepdims=True)
            p = jnp.exp(s - top)
            total = jnp.sum(p, axis=0, keepdims=True)
            m.lse[h:h + 1, at] = top + jnp.log(total)
            o = dot(vals, p.astype(BF), TN) * (1.0 / total)
            if h == 0:
                out = o
            else:
                out = jnp.where(lax.broadcasted_iota(jnp.int32, o.shape, 0) < 64, out, o)
        m.att_heads[at] = out.T.astype(BF)
        for half in range(2):
            target = 2 * i + half
            piece = m.att_heads.at[ds(target * rows, rows)]

            @pl.when(target != b)
            def _():
                w.make(piece, m.att.at[:, lanes], (u, target), att_at + b, att_at + target).start()

    attend(3)
    l_proj.wait()
    for copy in pr2:
        copy.wait_recv()
    mine = m.wproj.at[:, :, c]
    pr3 = w.blk(1, mine, mine)
    attend(2)
    d1.wait_recv()
    slot = m.wdown.at[y, 1 - zh]
    d2.append(w.uly(2, slot, slot))
    c_z.wait_recv()
    slot = m.c_all.at[ds(flip(rank, 2) * rows, rows)]
    c_zx = w.uly(1, slot, slot)
    c_fwd.append(w.blk(1, slot, slot))
    attend(1)
    attend(0)
    m.att[:, lanes] = m.att_heads[mine_b]
    cot_f = cot[...].astype(F32)
    down_bias_sum = jnp.sum(cot_f, axis=0, keepdims=True)
    up2.wait_recv()
    mine = m.wup.at[ds(y * 2, 2), 1 - zh]
    up3.append(w.uly(2, mine, mine))
    for k in range(1, 8):
        other = flip(b, k)
        w.make(
            m.att_heads.at[ds(other * rows, rows)], m.att.at[:, ds(other * 128, 128)], (u, other), att_at + other
        ).wait_recv()
        w.make(
            m.att_heads.at[ds(other * rows, rows)], m.att.at[:, lanes], (u, other), att_at + b, att_at + other
        ).wait_send()
    pr3.wait_recv()

    wproj = m.wproj[...].reshape(width, width)
    mixed = tok[...].astype(F32) + dot(m.att[...], wproj) + vec[2:3]
    m.mixed[...] = mixed
    n2, inv2 = norm_parts(mixed)
    m.n2_all[mine_r] = (n2 * vec[3:4] + vec[4:5]).astype(BF)
    half_rows = rows // 2

    def halves(owner, h):
        return m.n2_all.at[ds(owner * rows + h * half_rows, half_rows)]

    n_z = [w.blk(2, halves(rank, 0), halves(rank, 0))]
    n_x = [w.uly(1, halves(rank, 1), halves(rank, 1))]
    n_z.append(w.blk(2, halves(rank, 1), halves(rank, 1)))
    n_x.append(w.uly(1, halves(rank, 0), halves(rank, 0)))
    n_sib = w.blk(1, m.n2_all.at[mine_r], m.n2_all.at[mine_r])
    for copy in up3 + d2:
        copy.wait_recv()
    l_down.wait()
    hidden = m.act.shape[1]
    wup = m.wup[...].reshape(width, hidden)
    wdown = m.wdown[...].reshape(hidden, width)

    hops = ((0, 2), (1, 0), (1, 2))

    def feed(chip):
        at = ds(chip * pair, pair)
        up = dot(m.n2_all[at], wup) + up_bias
        square = up * up
        th = jnp.tanh(0.7978845608028654 * (up + 0.044715 * square * up))
        act = (0.5 * up * (1.0 + th)).astype(BF)
        slope = 0.5 * (1.0 + th) + 0.5 * up * (1.0 - th * th) * (
            0.7978845608028654 * (1.0 + 3.0 * 0.044715 * square)
        )
        gup = (dot(m.c_all[at], wdown, NT) * slope).astype(BF)
        m.act[at] = act
        m.gup[at] = gup
        m.g2_part[at] = dot(gup, wup, NT).astype(BF)
        m.out_part[at] = dot(act, wdown).astype(BF)

    def swap(chip, i):
        other = ds(chip * pair + (1 - c) * rows, rows)
        return (
            w.blk(1, m.g2_part.at[other], m.g2_sib.at[i]),
            w.blk(1, m.out_part.at[other], m.out_sib.at[i]),
        )

    c_sib.wait_recv()
    n_sib.wait_recv()
    feed(chip2)
    swaps = [swap(chip2, 3)]
    g2_sends, out_sends = [], []

    def merge(i):
        ku, kb = hops[i]
        far = flip(chip2, (ku * 4 + kb) // 2)
        own = ds(far * pair + c * rows, rows)
        swaps[i + 1][0].wait_recv()
        m.g2_keep[i] = (m.g2_part[own].astype(F32) + m.g2_sib[i].astype(F32)).astype(BF)
        g2_sends.append(w.near(ku, kb, m.g2_keep.at[i], m.g2_far.at[i]))

    def merge_out(i):
        ku, kb = hops[i]
        far = flip(chip2, (ku * 4 + kb) // 2)
        own = ds(far * pair + c * rows, rows)
        swaps[i + 1][1].wait_recv()
        m.out_keep[i] = (m.out_part[own].astype(F32) + m.out_sib[i].astype(F32)).astype(BF)
        out_sends.append(w.near(ku, kb, m.out_keep.at[i], m.out_far.at[i]))

    n_z[0].wait_recv()
    n_diag = [w.uly(1, halves(flip(rank, 2), 0), halves(flip(rank, 2), 0))]
    n_x[0].wait_recv()
    n_diag.append(w.blk(2, halves(flip(rank, 4), 1), halves(flip(rank, 4), 1)))

    def n_forward(mask, copies):
        for copy in copies:
            copy.wait_recv()
        slot = m.n2_all.at[ds(flip(rank, mask) * rows, rows)]
        return w.blk(1, slot, slot)

    n_fwd = [n_forward(2, n_z[1:]), n_forward(4, n_x[1:])]
    for i, mask in enumerate((2, 4, 6)):
        if i == 2:
            n_fwd.append(n_forward(6, n_diag))
            c_zx.wait_recv()
            slot = m.c_all.at[ds(flip(rank, 6) * rows, rows)]
            c_fwd.append(w.blk(1, slot, slot))
        c_fwd[(1, 0, 2)[i]].wait_recv()
        n_fwd[i].wait_recv()
        far = flip(chip2, mask // 2)
        feed(far)
        swaps.append(swap(far, i))
        if i > 0:
            merge(i - 1)
    merge(2)
    half = hidden // 2
    for j in range(2):
        span = slice(j * half, (j + 1) * half)
        m.dwn[j] = dot(m.act[:, span], m.c_all[...], TN).astype(BF).reshape(2, rows, width)
    y_dwn = [w.uly(2, m.dwn.at[1 - y, 1 - zh], m.dwn_y.at[1 - zh])]
    for j in range(2):
        span = slice(j * half, (j + 1) * half)
        m.dup[:, :, :, span] = dot(m.n2_all[...], m.gup[:, span], TN).astype(BF).reshape(4, 2, 128, half)
    others = ds((1 - y) * 2, 2)
    y_dup = [w.uly(2, m.dup.at[others, 1 - zh], m.dup_y.at[:, 1 - zh])]
    y_dwn.append(w.uly(2, m.dwn.at[1 - y, zh], m.dwn_y.at[zh]))
    y_dup.append(w.uly(2, m.dup.at[others, zh], m.dup_y.at[:, zh]))
    up_bias_sum = jnp.sum(m.gup[...].astype(F32), axis=0, keepdims=True)

    own = ds(chip2 * pair + c * rows, rows)
    y_dwn[0].wait_recv()
    m.dwn_keep[...] = (m.dwn[y, 1 - zh].astype(F32) + m.dwn_y[1 - zh].astype(F32)).astype(BF)
    top, low = ds(0, half_rows), ds(half_rows, half_rows)
    z1 = [w.blk(4, m.dwn_keep.at[top], m.dwn_z.at[top])]
    swaps[0][0].wait_recv()
    g = m.g2_part[own].astype(F32) + m.g2_sib[3].astype(F32)
    for i in range(3):
        g2_sends[i].wait_recv()
        g = g + m.g2_far[i].astype(F32)
    ln2_gain_sum = jnp.sum(g * n2, axis=0, keepdims=True)
    ln2_bias_sum = jnp.sum(g, axis=0, keepdims=True)
    e = g * vec[3:4]
    gmix = cot_f + inv2 * (
        e - jnp.mean(e, axis=-1, keepdims=True) - n2 * jnp.mean(e * n2, axis=-1, keepdims=True)
    )
    m.gmix[...] = gmix
    proj_bias_sum = jnp.sum(gmix, axis=0, keepdims=True)
    gbr = gmix.astype(BF)
    m.gbr[...] = gbr
    m.gatt[...] = dot(gbr, wproj, NT).astype(BF)

    g_to = w.take(8)
    g_sent = []
    for k in range(1, 8):
        other = flip(b, k)
        copy = w.make(
            m.gatt.at[:, ds(other * 128, 128)], m.gh.at[mine_b], (u, other), g_to + b, g_to + other
        )
        copy.start()
        g_sent.append(copy)
    m.gh[mine_b] = m.gatt[:, ds(b * 128, 128)]
    for i in range(3):
        merge_out(i)
    for j in range(4):
        m.dpr[j] = dot(m.att[:, j * 256:(j + 1) * 256], gbr, TN).astype(BF).reshape(4, 2, 32, width)
    pg1 = w.blk(1, m.dpr.at[:, :, 1 - c], m.dpr_sib)
    m.dkv[...] = jnp.zeros_like(m.dkv)
    back = w.take(4)

    def hand_back(i):
        at = ds(i * pair, pair)
        return w.make(m.halo_out.at[at], m.halo_in.at[at], (jnp.maximum(u - 1, 0), b), back + i)

    def attend_back(i):
        for half in range(2):
            source = 2 * i + half

            @pl.when(source != b)
            def _():
                w.make(
                    m.gatt.at[:, lanes], m.gh.at[ds(source * rows, rows)], (u, b), g_to + source
                ).wait_recv()

        allowed = allowed_pairs(i)
        span = slice(i * pair, i * pair + window)
        at = slice(i * pair, (i + 1) * pair)
        keys = m.kv[span, 0:128]
        vals = m.kv[span, 128:256]
        query = m.q[at]
        grads = m.gh[at]
        dk = dv = dq = None
        for h in range(2):
            mask = head_mask((pair, 128), h)
            qh = jnp.where(mask, query, jnp.zeros_like(query))
            gr = jnp.where(mask, grads, jnp.zeros_like(grads))
            s = dot(keys, qh, NT) * 0.125 + slopes[2 * b + h] * kslope
            p = jnp.where(allowed, jnp.exp(s - m.lse[h:h + 1, at]), 0.0)
            dp = dot(vals, gr, NT)
            delta = jnp.sum(p * dp, axis=0, keepdims=True)
            gs = (p * (dp - delta)).astype(BF)
            dv_h = dot(p.astype(BF), gr)
            dk_h = dot(gs, qh)
            dq_h = dot(keys, gs, TN)
            if h == 0:
                dk, dv, dq = dk_h, dv_h, dq_h
            else:
                dk, dv = dk + dk_h, dv + dv_h
                dq = jnp.where(lax.broadcasted_iota(jnp.int32, dq.shape, 0) < 64, dq, dq_h)
        m.gqkv[at, 0:128] = (dq.T * 0.125).astype(BF)
        m.dkv[span, 0:128] += dk
        m.dkv[span, 128:256] += dv
        m.halo_out[at] = m.dkv[at].astype(BF)

        @pl.when(u > 0)
        def _():
            hand_back(i).start()

    attend_back(0)
    z1.append(w.blk(4, m.dwn_keep.at[low], m.dwn_z.at[low]))
    y_dup[0].wait_recv()
    m.dup_keep[...] = (m.dup[ds(y * 2, 2), 1 - zh].astype(F32) + m.dup_y[:, 1 - zh].astype(F32)).astype(BF)
    z2 = w.blk(4, m.dup_keep, m.dup_z)
    attend_back(1)
    attend_back(2)
    attend_back(3)
    def complete(i):
        @pl.when(u < 3)
        def _():
            at = ds(i * pair, pair)
            own = ds(group + i * pair, pair)
            w.make(m.halo_out.at[at], m.halo_in.at[at], (u, b), back + i).wait_recv()
            m.dkv[own] += m.halo_in[at].astype(F32)

        at = ds(i * pair, pair)
        own = ds(group + i * pair, pair)
        m.gqkv[at, 128:256] = (m.dkv[own, 0:128] * 0.125).astype(BF)
        m.gqkv[at, 256:384] = m.dkv[own, 128:256].astype(BF)

    swaps1 = {}

    def spread(k):
        chip = flip(z, k)
        complete(chip)
        at = ds(chip * pair, pair)
        m.g1_part[at] = dot(m.gqkv[at], m.wqkv[...], NT).astype(BF)
        other = ds(chip * pair + (1 - c) * rows, rows)
        swaps1[k] = w.blk(1, m.g1_part.at[other], m.g1_sib.at[k])

    def chip_sum(k):
        own = ds(flip(z, k) * pair + c * rows, rows)
        swaps1[k].wait_recv()
        return m.g1_part[own].astype(F32) + m.g1_sib[k].astype(F32)

    spread(3)
    spread(1)
    m.g1_keep[2] = chip_sum(3).astype(BF)
    via = [w.blk(2, m.g1_keep.at[2, part], m.g1_far.at[2, part]) for part in (top, low)]
    pg1.wait_recv()
    m.dpr_keep[...] = (m.dpr[:, :, c].astype(F32) + m.dpr_sib[...].astype(F32)).astype(BF)
    pg2 = [w.uly(k, m.dpr_keep.at[flip(u, k)], m.dpr_u.at[k - 1]) for k in range(1, 4)]
    spread(2)
    spread(0)
    m.dq[...] = dot(m.n1[...], m.gqkv[...], TN).astype(BF)
    q2g = [w.uly(k, m.dq.at[ds(flip(u, k) * 256, 256)], m.dq_u.at[k - 1]) for k in range(1, 4)]
    sum2 = chip_sum(2)
    g1_cross = []
    for h, part in enumerate((top, low)):
        via[h].wait_recv()
        m.g1_keep[1, part] = (
            sum2[h * half_rows:(h + 1) * half_rows] + m.g1_far[2, part].astype(F32)
        ).astype(BF)
        g1_cross.append(w.blk(4, m.g1_keep.at[1, part], m.g1_far.at[1, part]))
    m.g1_keep[0] = chip_sum(1).astype(BF)
    g1_near = w.blk(2, m.g1_keep.at[0], m.g1_far.at[0])
    qv_sums = jnp.sum(m.gqkv[...].astype(F32), axis=0, keepdims=True)

    own = ds(chip2 * pair + c * rows, rows)
    swaps[0][1].wait_recv()
    out = m.mixed[...] + vec[5:6] + m.out_part[own].astype(F32) + m.out_sib[3].astype(F32)
    for i in range(3):
        out_sends[i].wait_recv()
        out = out + m.out_far[i].astype(F32)
    out_o[...] = out.astype(BF)
    for copy in pg2:
        copy.wait_recv()
    m.dpr_own[...] = (
        (m.dpr_keep[u].astype(F32) + m.dpr_u[0].astype(F32)) + (m.dpr_u[1].astype(F32) + m.dpr_u[2].astype(F32))
    ).astype(BF)
    pg3 = [w.blk(2 * k, m.dpr_own.at[flip(z, k)], m.dpr_z.at[k - 1]) for k in range(1, 4)]
    for copy in z1:
        copy.wait_recv()
    y_dwn[1].wait_recv()
    down_o[...] = (m.dwn[y, zh].astype(F32) + m.dwn_y[zh].astype(F32)) + m.dwn_z[...].astype(F32)
    z2.wait_recv()
    y_dup[1].wait_recv()
    m.dup_own[...] = (
        (m.dup[ds(y * 2, 2), zh].astype(F32) + m.dup_y[:, zh].astype(F32)) + m.dup_z[...].astype(F32)
    ).astype(BF).reshape(8, 32, hidden)
    up3g = [w.near(k // 4, k % 4, m.dup_own.at[flip(rank, k)], up_o.at[rank]) for k in range(1, 8)]
    up_o[rank] = m.dup_own[rank]
    for copy in q2g:
        copy.wait_recv()
    m.dq_own[...] = (
        (m.dq[ds(u * 256, 256)].astype(F32) + m.dq_u[0].astype(F32))
        + (m.dq_u[1].astype(F32) + m.dq_u[2].astype(F32))
    ).astype(BF).reshape(8, 32, 384)
    q3g = [w.blk(k, m.dq_own.at[flip(b, k)], qkv_o.at[b]) for k in range(1, 8)]
    qkv_o[b] = m.dq_own[b]

    n, inv = norm_parts(tok[...].astype(F32))
    g = chip_sum(0)
    g1_near.wait_recv()
    for copy in g1_cross:
        copy.wait_recv()
    g = g + m.g1_far[0].astype(F32) + m.g1_far[1].astype(F32)
    lines = jnp.concatenate(
        [
            jnp.sum(g * n, axis=0, keepdims=True), jnp.sum(g, axis=0, keepdims=True),
            proj_bias_sum, ln2_gain_sum, ln2_bias_sum, down_bias_sum, jnp.zeros((2, width), F32),
        ],
        axis=0,
    )
    for d in range(32):
        m.sm[d] = lines[:, (d // 4) * 128:(d // 4 + 1) * 128]
    for at, line in ((2 * b, qv_sums[:, 0:128]), (16 + 2 * b, qv_sums[:, 256:384])):
        m.sm[at, 6:7] = line
        m.sm[at + 1, 6:7] = line
    for ch in range(4):
        m.sm[(ch // 2) * 16 + x * 8 + (ch % 2) * 4 + b % 4, 7:8] = up_bias_sum[:, ch * 128:(ch + 1) * 128]
    s1 = [w.uly(k, m.sm.at[ds(flip(u, k) * 8, 8)], m.sm_u.at[k - 1]) for k in range(1, 4)]
    e = g * vec[0:1]
    in_o[...] = (
        m.gmix[...]
        + inv * (e - jnp.mean(e, axis=-1, keepdims=True) - n * jnp.mean(e * n, axis=-1, keepdims=True))
    ).astype(BF)
    for copy in pg3:
        copy.wait_recv()
    proj_o[...] = (m.dpr_own[z].astype(F32) + m.dpr_z[0].astype(F32)) + (
        m.dpr_z[1].astype(F32) + m.dpr_z[2].astype(F32)
    )
    for copy in s1:
        copy.wait_recv()
    m.sm_keep[...] = (m.sm[ds(u * 8, 8)] + m.sm_u[0]) + (m.sm_u[1] + m.sm_u[2])
    s2 = [w.blk(k, m.sm_keep.at[flip(b, k)], m.sm_b.at[k - 1]) for k in range(1, 8)]
    for copy in up3g + q3g + s2:
        copy.wait_recv()
    total = m.sm_keep[b]
    for k in range(7):
        total = total + m.sm_b[k]
    line = lax.broadcasted_iota(jnp.int32, (8, 128), 0)
    by32 = pltpu.roll(total, (128 - 32 * (b % 4)) % 128, 1)
    by64 = pltpu.roll(total, (128 - 64 * (b % 2)) % 128, 1)
    vec_o[...] = jnp.where(line < 6, by32, jnp.where(line == 6, by64, total))

    for copy in g_sent:
        copy.wait_send()

    @pl.when(u < 3)
    def _():
        for copy in hand:
            copy.wait_send()

    @pl.when(u > 0)
    def _():
        for i in range(4):
            hand_back(i).wait_send()

    w.finish()


def finish_kernel(
    out, grad_in, down, up, qkv, proj, vec,
    out_o, in_o, g1_o, b1_o, qkv_o, qv_o, proj_o, pb_o, g2_o, b2_o, up_o, ub_o, down_o, db_o,
):
    out_o[...] = out[...]
    in_o[...] = grad_in[...]
    down_o[...] = down[...]
    proj_o[...] = proj[...]
    for r in range(8):
        for ch in range(4):
            to = ((ch // 2) * 16 + (r // 4) * 8 + (ch % 2) * 4 + r % 4) * 128
            up_o[:, to:to + 128] = up[r, :, ch * 128:(ch + 1) * 128].astype(F32)
        for part in range(3):
            to = part * 1024 + r * 128
            qkv_o[:, to:to + 128] = qkv[r, :, part * 128:(part + 1) * 128].astype(F32)
    for row, ref in enumerate((g1_o, b1_o, pb_o, g2_o, b2_o, db_o, qv_o, ub_o)):
        ref[...] = vec[row, 0:ref.shape[0]]


def fast_body(
    tokens, ln1_gain, ln1_bias, qkv_weight, qv_bias, proj_weight, proj_bias, ln2_gain, ln2_bias,
    up_weight, up_bias, down_weight, down_bias, alibi_slopes, doc_starts, cotangent,
):
    rows, width = tokens.shape
    shapes = buffer_shapes(rows, width, 512, 128)
    v = pl.BlockSpec(memory_space=pltpu.VMEM)
    s = pl.BlockSpec(memory_space=pltpu.SMEM)
    sds = jax.ShapeDtypeStruct
    parts = pl.pallas_call(
        functools.partial(block_kernel, shapes),
        name="transformer_block",
        out_shape=(
            sds((rows, width), BF),
            sds((rows, width), BF),
            sds((rows, width), F32),
            sds((8, 32, 512), BF),
            sds((8, 32, 384), BF),
            sds((32, width), F32),
            sds((8, 128), F32),
        ),
        in_specs=[v] * 14 + [s, s],
        out_specs=(v,) * 7,
        scratch_shapes=[pltpu.VMEM(shape, kind) for _, shape, kind in shapes]
        + [
            pltpu.SemaphoreType.DMA((SEMAPHORES,)),
            pltpu.SemaphoreType.DMA((SEMAPHORES,)),
            pltpu.SemaphoreType.DMA((4,)),
        ],
        compiler_params=pltpu.CompilerParams(
            collective_id=0, has_side_effects=True, vmem_limit_bytes=VMEM_LIMIT
        ),
    )(
        tokens, qkv_weight, proj_weight, up_weight, down_weight, cotangent,
        ln1_gain, ln1_bias, proj_bias, ln2_gain, ln2_bias, down_bias, qv_bias, up_bias,
        alibi_slopes, doc_starts,
    )
    vector = sds((32,), F32)
    return pl.pallas_call(
        finish_kernel,
        name="lay_out",
        out_shape=(
            sds((rows, width), BF), sds((rows, width), BF), vector, vector, sds((32, 3072), F32),
            sds((64,), F32), sds((32, width), F32), vector, vector, vector, sds((32, 4096), F32),
            sds((128,), F32), sds((rows, width), F32), vector,
        ),
        in_specs=[v] * 7,
        out_specs=(v,) * 14,
        compiler_params=pltpu.CompilerParams(vmem_limit_bytes=VMEM_LIMIT),
    )(*parts)


HEADS = 16
HEAD_DIM = 64


def layer_norm(values, norm_gain, norm_shift):
    center = jnp.mean(values, axis=-1, keepdims=True)
    offset = values - center
    spread = jnp.mean(offset * offset, axis=-1, keepdims=True)
    return offset * lax.rsqrt(spread + 1e-05) * norm_gain + norm_shift


def gelu_tanh(values):
    return (
        0.5
        * values
        * (1.0 + jnp.tanh(0.7978845608028654 * (values + 0.044715 * values * values * values)))
    )


def place_rows(local_rows, team_size, blk_count, tok_rows):
    team_span = team_size * tok_rows
    return (
        local_rows % team_span // tok_rows * blk_count + local_rows // team_span
    ) * tok_rows + local_rows % tok_rows


def doc_index(positions, doc_starts):
    return jnp.sum((positions[:, None] >= doc_starts[None, :]).astype(jnp.int32), axis=1) - 1


def split_rows(row_count, step_rows):
    return (row_count // step_rows, step_rows)


def score_block(queries, keys, query_pos, key_pos, query_doc, key_doc, slopes):
    raw_scores = jnp.einsum(
        "qhd,khd->hqk", queries, keys, preferred_element_type=jnp.float32
    ) * HEAD_DIM ** (-0.5)
    distance = (query_pos[:, None] - key_pos[None, :]).astype(jnp.float32)
    raw_scores = raw_scores - slopes[:, None, None] * distance[None]
    allowed = (key_pos[None, :] <= query_pos[:, None]) & (query_doc[:, None] == key_doc[None, :])
    return (jnp.where(allowed[None], raw_scores, -1e30), allowed[None])


def general_body(
    tokens,
    ln1_gain,
    ln1_bias,
    qkv_weight,
    qv_bias,
    proj_weight,
    proj_bias,
    ln2_gain,
    ln2_bias,
    up_weight,
    up_bias,
    down_weight,
    down_bias,
    alibi_slopes,
    doc_starts,
    cotangent,
):
    team_size = lax.axis_size("ulysses")
    blk_count = lax.axis_size("blk")
    tok_rows = tokens.shape[0]
    width_all = tokens.shape[1]
    head_rows = team_size * tok_rows
    heads_here = HEADS // team_size
    features = heads_here * HEAD_DIM
    scale_factor = HEAD_DIM ** (-0.5)
    gathered = (
        lax.all_gather(ln1_gain, ("ulysses", "blk"), axis=0, tiled=True),
        lax.all_gather(ln1_bias, ("ulysses", "blk"), axis=0, tiled=True),
        lax.all_gather(qkv_weight, ("ulysses", "blk"), axis=0, tiled=True),
        lax.all_gather(qv_bias, ("ulysses", "blk"), axis=0, tiled=True),
        lax.all_gather(proj_weight, ("ulysses", "blk"), axis=0, tiled=True),
        lax.all_gather(proj_bias, ("ulysses", "blk"), axis=0, tiled=True),
        lax.all_gather(ln2_gain, ("ulysses", "blk"), axis=0, tiled=True),
        lax.all_gather(ln2_bias, ("ulysses", "blk"), axis=0, tiled=True),
        lax.all_gather(up_weight, ("ulysses", "blk"), axis=0, tiled=True),
        lax.all_gather(up_bias, ("ulysses", "blk"), axis=0, tiled=True),
        lax.all_gather(down_weight, ("ulysses", "blk"), axis=0, tiled=True),
        lax.all_gather(down_bias, ("ulysses", "blk"), axis=0, tiled=True),
    )
    gain_one = gathered[0].astype(jnp.float32)
    shift_one = gathered[1].astype(jnp.float32)
    qkv_proj = gathered[2]
    qv_shift = gathered[3].astype(jnp.float32)
    proj_mat = gathered[4]
    proj_shift = gathered[5].astype(jnp.float32)
    gain_two = gathered[6].astype(jnp.float32)
    shift_two = gathered[7].astype(jnp.float32)
    up_mat = gathered[8]
    up_shift = gathered[9].astype(jnp.float32)
    down_mat = gathered[10]
    down_shift = gathered[11].astype(jnp.float32)
    inputs_f = tokens.astype(jnp.float32)
    normed_one = layer_norm(inputs_f, gain_one, shift_one).astype(jnp.bfloat16)
    joined_bias = jnp.concatenate(
        [qv_shift[:width_all], jnp.zeros((width_all,), jnp.float32), qv_shift[width_all:]]
    )
    joined = (
        jnp.dot(normed_one, qkv_proj, preferred_element_type=jnp.float32) + joined_bias
    ).astype(jnp.bfloat16)
    head_local = lax.all_to_all(
        joined.reshape(tok_rows, 3, team_size, features),
        "ulysses",
        split_axis=2,
        concat_axis=0,
        tiled=True,
    )
    queries_flat = head_local[:, 0, 0]
    queries = queries_flat.reshape(head_rows, heads_here, HEAD_DIM)
    key_value = head_local[:, 1:, 0]
    own_keys = key_value[:, 0].reshape(head_rows, heads_here, HEAD_DIM)
    own_values = key_value[:, 1].reshape(head_rows, heads_here, HEAD_DIM)
    slopes = lax.dynamic_slice_in_dim(
        alibi_slopes, lax.axis_index("ulysses") * heads_here, heads_here, 0
    )
    own_rows = lax.axis_index("blk") * head_rows + jnp.arange(head_rows, dtype=jnp.int32)
    own_pos = place_rows(own_rows, team_size, blk_count, tok_rows)
    own_doc = doc_index(own_pos, doc_starts)
    start_state = (
        jnp.full((heads_here, head_rows), -1e30, jnp.float32),
        jnp.zeros((heads_here, head_rows), jnp.float32),
        jnp.zeros((heads_here, head_rows, HEAD_DIM), jnp.float32),
    )
    carried = start_state
    piece_rows = lax.all_gather(key_value, "blk", axis=0, tiled=True)
    number, step_rows = split_rows(piece_rows.shape[0], head_rows)
    stacked = piece_rows.reshape(number, step_rows, 2, heads_here, HEAD_DIM)
    offsets = step_rows * jnp.arange(number, dtype=jnp.int32)

    def online_step(running, inputs_pair):
        best_now, norm_sum, accumulated = running
        kv_block, offset_now = inputs_pair
        key_pos = place_rows(
            offset_now + jnp.arange(step_rows, dtype=jnp.int32), team_size, blk_count, tok_rows
        )
        key_doc = doc_index(key_pos, doc_starts)
        masked, allowed = score_block(
            queries, kv_block[:, 0], own_pos, key_pos, own_doc, key_doc, slopes
        )
        best_next = jnp.maximum(best_now, jnp.max(masked, axis=-1))
        weights = jnp.where(allowed, jnp.exp(masked - best_next[..., None]), 0.0)
        shrink = jnp.exp(best_now - best_next)
        norm_sum = norm_sum * shrink + jnp.sum(weights, axis=-1)
        accumulated = accumulated * shrink[..., None] + jnp.einsum(
            "hqk,khd->hqd",
            weights.astype(jnp.bfloat16),
            kv_block[:, 1],
            preferred_element_type=jnp.float32,
        )
        return ((best_next, norm_sum, accumulated), None)

    carried, _ = lax.scan(online_step, carried, (stacked, offsets))
    best_all, norm_all, acc_all = carried
    attended_heads = acc_all / norm_all[..., None]
    log_norm = best_all + jnp.log(norm_all)
    attended_rows = (
        attended_heads.transpose(1, 0, 2).reshape(head_rows, 1, features).astype(jnp.bfloat16)
    )
    attended = lax.all_to_all(
        attended_rows, "ulysses", split_axis=0, concat_axis=1, tiled=True
    ).reshape(tok_rows, width_all)
    mixed = inputs_f + jnp.dot(attended, proj_mat, preferred_element_type=jnp.float32) + proj_shift
    normed_two = layer_norm(mixed, gain_two, shift_two).astype(jnp.bfloat16)
    up_values = jnp.dot(normed_two, up_mat, preferred_element_type=jnp.float32) + up_shift
    activated = gelu_tanh(up_values).astype(jnp.bfloat16)
    output = (
        mixed + jnp.dot(activated, down_mat, preferred_element_type=jnp.float32) + down_shift
    ).astype(jnp.bfloat16)
    contract_rows = (((0,), (0,)), ((), ()))
    contract_cols = (((1,), (1,)), ((), ()))
    grad_out = cotangent.astype(jnp.float32)
    down_grad = lax.dot_general(
        activated, cotangent, contract_rows, preferred_element_type=jnp.float32
    )
    down_bias_grad = jnp.sum(grad_out, axis=0)
    grad_act = lax.dot_general(
        cotangent, down_mat, contract_cols, preferred_element_type=jnp.float32
    )
    _, gelu_pull = jax.vjp(gelu_tanh, up_values)
    grad_up = gelu_pull(grad_act)[0].astype(jnp.bfloat16)
    up_grad = lax.dot_general(
        normed_two, grad_up, contract_rows, preferred_element_type=jnp.float32
    )
    up_bias_grad = jnp.sum(grad_up.astype(jnp.float32), axis=0)
    grad_norm_two = lax.dot_general(
        grad_up, up_mat, contract_cols, preferred_element_type=jnp.float32
    )
    _, norm_two_pull = jax.vjp(layer_norm, mixed, gain_two, shift_two)
    grad_mixed_part, ln2_gain_grad, ln2_bias_grad = norm_two_pull(grad_norm_two)
    grad_mixed = grad_out + grad_mixed_part
    grad_branch = grad_mixed.astype(jnp.bfloat16)
    proj_grad = lax.dot_general(
        attended, grad_branch, contract_rows, preferred_element_type=jnp.float32
    )
    proj_bias_grad = jnp.sum(grad_mixed, axis=0)
    grad_att = lax.dot_general(
        grad_branch, proj_mat, contract_cols, preferred_element_type=jnp.float32
    ).astype(jnp.bfloat16)
    grad_heads = lax.all_to_all(
        grad_att.reshape(tok_rows, team_size, features),
        "ulysses",
        split_axis=1,
        concat_axis=0,
        tiled=True,
    )
    grad_heads_flat = grad_heads[:, 0]
    grad_att_heads = grad_heads_flat.reshape(head_rows, heads_here, HEAD_DIM)
    delta = jnp.sum(grad_att_heads.astype(jnp.float32).transpose(1, 0, 2) * attended_heads, axis=-1)
    carried = jnp.zeros((heads_here, head_rows, HEAD_DIM), jnp.float32)
    piece_rows = lax.all_gather(key_value, "blk", axis=0, tiled=True)
    number, query_step_rows = split_rows(piece_rows.shape[0], head_rows)
    stacked = piece_rows.reshape(number, query_step_rows, 2, heads_here, HEAD_DIM)
    offsets = query_step_rows * jnp.arange(number, dtype=jnp.int32)

    def query_step(running, inputs_pair):
        kv_block, offset_now = inputs_pair
        key_pos = place_rows(
            offset_now + jnp.arange(query_step_rows, dtype=jnp.int32),
            team_size,
            blk_count,
            tok_rows,
        )
        key_doc = doc_index(key_pos, doc_starts)
        masked, allowed = score_block(
            queries, kv_block[:, 0], own_pos, key_pos, own_doc, key_doc, slopes
        )
        probs = jnp.where(allowed, jnp.exp(masked - log_norm[..., None]), 0.0)
        grad_probs = jnp.einsum(
            "qhd,khd->hqk", grad_att_heads, kv_block[:, 1], preferred_element_type=jnp.float32
        )
        grad_scores = (probs * (grad_probs - delta[..., None])).astype(jnp.bfloat16)
        running = running + jnp.einsum(
            "hqk,khd->hqd", grad_scores, kv_block[:, 0], preferred_element_type=jnp.float32
        )
        return (running, None)

    carried, _ = lax.scan(query_step, carried, (stacked, offsets))
    grad_queries = carried * scale_factor
    all_norms, all_deltas = (
        lax.all_gather(log_norm.T, "blk", axis=0, tiled=True),
        lax.all_gather(delta.T, "blk", axis=0, tiled=True),
    )
    empty_keys = jnp.zeros((head_rows, heads_here, HEAD_DIM), jnp.float32)
    carried = (empty_keys, empty_keys)
    pieces = (
        lax.all_gather(queries_flat, "blk", axis=0, tiled=True),
        lax.all_gather(grad_heads_flat, "blk", axis=0, tiled=True),
    )
    number, key_step_rows = split_rows(pieces[0].shape[0], head_rows)
    query_stack = pieces[0].reshape(number, key_step_rows, heads_here, HEAD_DIM)
    grad_stack = pieces[1].reshape(number, key_step_rows, heads_here, HEAD_DIM)
    offsets = key_step_rows * jnp.arange(number, dtype=jnp.int32)

    def key_step(running, inputs_triple):
        grad_keys_now, grad_values_now = running
        query_block, grad_block, offset_now = inputs_triple
        query_pos = place_rows(
            offset_now + jnp.arange(key_step_rows, dtype=jnp.int32), team_size, blk_count, tok_rows
        )
        query_doc = doc_index(query_pos, doc_starts)
        norm_block = lax.dynamic_slice_in_dim(all_norms, offset_now, key_step_rows, 0).T
        delta_block = lax.dynamic_slice_in_dim(all_deltas, offset_now, key_step_rows, 0).T
        masked, allowed = score_block(
            query_block, own_keys, query_pos, own_pos, query_doc, own_doc, slopes
        )
        probs = jnp.where(allowed, jnp.exp(masked - norm_block[..., None]), 0.0)
        grad_values_now = grad_values_now + jnp.einsum(
            "hqk,qhd->khd",
            probs.astype(jnp.bfloat16),
            grad_block,
            preferred_element_type=jnp.float32,
        )
        grad_probs = jnp.einsum(
            "qhd,khd->hqk", grad_block, own_values, preferred_element_type=jnp.float32
        )
        grad_scores = (probs * (grad_probs - delta_block[..., None])).astype(jnp.bfloat16)
        grad_keys_now = grad_keys_now + jnp.einsum(
            "hqk,qhd->khd", grad_scores, query_block, preferred_element_type=jnp.float32
        )
        return ((grad_keys_now, grad_values_now), None)

    carried, _ = lax.scan(key_step, carried, (query_stack, grad_stack, offsets))
    grad_keys, grad_values = carried
    grad_pack = jnp.stack(
        [
            grad_queries.transpose(1, 0, 2).reshape(head_rows, features),
            (grad_keys * scale_factor).reshape(head_rows, features),
            grad_values.reshape(head_rows, features),
        ],
        axis=1,
    ).astype(jnp.bfloat16)
    grad_joined = lax.all_to_all(
        grad_pack.reshape(head_rows, 3, 1, features),
        "ulysses",
        split_axis=0,
        concat_axis=2,
        tiled=True,
    ).reshape(tok_rows, 3 * width_all)
    qkv_grad = lax.dot_general(
        normed_one, grad_joined, contract_rows, preferred_element_type=jnp.float32
    )
    joined_sums = jnp.sum(grad_joined.astype(jnp.float32), axis=0)
    qv_bias_grad = jnp.concatenate([joined_sums[:width_all], joined_sums[2 * width_all :]])
    grad_norm_one = lax.dot_general(
        grad_joined, qkv_proj, contract_cols, preferred_element_type=jnp.float32
    )
    _, norm_one_pull = jax.vjp(layer_norm, inputs_f, gain_one, shift_one)
    grad_inputs_part, ln1_gain_grad, ln1_bias_grad = norm_one_pull(grad_norm_one)
    input_grad = (grad_mixed + grad_inputs_part).astype(jnp.bfloat16)
    shares = (
        lax.psum_scatter(ln1_gain_grad, ("ulysses", "blk"), scatter_dimension=0, tiled=True),
        lax.psum_scatter(ln1_bias_grad, ("ulysses", "blk"), scatter_dimension=0, tiled=True),
        lax.psum_scatter(qkv_grad, ("ulysses", "blk"), scatter_dimension=0, tiled=True),
        lax.psum_scatter(qv_bias_grad, ("ulysses", "blk"), scatter_dimension=0, tiled=True),
        lax.psum_scatter(proj_grad, ("ulysses", "blk"), scatter_dimension=0, tiled=True),
        lax.psum_scatter(proj_bias_grad, ("ulysses", "blk"), scatter_dimension=0, tiled=True),
        lax.psum_scatter(ln2_gain_grad, ("ulysses", "blk"), scatter_dimension=0, tiled=True),
        lax.psum_scatter(ln2_bias_grad, ("ulysses", "blk"), scatter_dimension=0, tiled=True),
        lax.psum_scatter(up_grad, ("ulysses", "blk"), scatter_dimension=0, tiled=True),
        lax.psum_scatter(up_bias_grad, ("ulysses", "blk"), scatter_dimension=0, tiled=True),
        lax.psum_scatter(down_grad, ("ulysses", "blk"), scatter_dimension=0, tiled=True),
        lax.psum_scatter(down_bias_grad, ("ulysses", "blk"), scatter_dimension=0, tiled=True),
    )
    return (
        output,
        input_grad,
        shares[0],
        shares[1],
        shares[2],
        shares[3],
        shares[4],
        shares[5],
        shares[6],
        shares[7],
        shares[8],
        shares[9],
        shares[10],
        shares[11],
    )


TOKEN_ROWS = P(("ulysses", "blk"), None)
VECTOR = P(("ulysses", "blk"))


def solution(mesh):
    whole = P()
    in_specs = (
        TOKEN_ROWS, VECTOR, VECTOR, TOKEN_ROWS, VECTOR, TOKEN_ROWS, VECTOR, VECTOR, VECTOR, TOKEN_ROWS,
        VECTOR, TOKEN_ROWS, VECTOR, whole, whole, TOKEN_ROWS,
    )
    out_specs = (
        TOKEN_ROWS, TOKEN_ROWS, VECTOR, VECTOR, TOKEN_ROWS, VECTOR, TOKEN_ROWS, VECTOR, VECTOR, VECTOR,
        TOKEN_ROWS, VECTOR, TOKEN_ROWS, VECTOR,
    )
    fits = mesh.shape["ulysses"] == 4 and mesh.shape["blk"] == 8
    return jax.shard_map(
        fast_body if fits else general_body,
        mesh=mesh, in_specs=in_specs, out_specs=out_specs, check_vma=False,
    )
```

```python
import collections
import functools

import jax
import jax.numpy as jnp
from jax import lax
from jax.experimental import pallas as pl
from jax.experimental.pallas import tpu as pltpu
from jax.sharding import PartitionSpec as P

BF = jnp.bfloat16
F32 = jnp.float32
MESH = pl.DeviceIdType.MESH
VMEM_LIMIT = 63 * 2**20
NT = (((1,), (1,)), ((), ()))
TN = (((0,), (0,)), ((), ()))
NN = (((1,), (0,)), ((), ()))


def dot(a, b, dims=NN):
    return lax.dot_general(a, b, dims, preferred_element_type=F32)


def flip(index, mask):
    out = index
    bit = 1
    while bit <= mask:
        if mask & bit:
            out = out + bit - 2 * bit * ((index // bit) % 2)
        bit *= 2
    return out


def ds(start, size, align=None):
    if not isinstance(start, int):
        start = pl.multiple_of(start, align or size)
    return pl.ds(start, size)


class Batch:
    def __init__(self, wire):
        self.wire = wire
        self.at = wire.take(1)
        self.size = 0

    def wait_recv(self):
        self.wire.await_bytes(self.wire.rsem.at[self.at], self.size)


class Wire:
    def __init__(self, ssem, rsem, lsem, measures):
        self.ssem, self.rsem, self.lsem = ssem, rsem, lsem
        self.measures = measures
        self.used = 0
        self.local = 0
        self.send_groups = []
        self.u = lax.axis_index("ulysses")
        self.b = lax.axis_index("blk")

    def take(self, count):
        first = self.used
        self.used += count
        assert self.used <= RECEIVES
        return first

    def take_send(self):
        self.send_groups.append([None, 0])
        assert len(self.send_groups) <= SENDS
        return len(self.send_groups) - 1

    def await_bytes(self, sem, size):
        for step, buffer, entries in self.measures:
            count = size // step * entries
            if size % step == 0 and count <= buffer.shape[0]:
                ref = buffer.at[pl.ds(0, count)]
                pltpu.make_async_copy(ref, ref, sem).wait()
                return
        assert False, size

    def send_slot(self, src, repeat=1):
        size = self.size_of(src)
        limit = max(step * (buffer.shape[0] // entries) for step, buffer, entries in self.measures if size % step == 0)
        for at, group in enumerate(self.send_groups):
            if group[0] == size and group[1] + size * repeat <= limit:
                group[1] += size * repeat
                return at
        self.send_groups.append([size, size * repeat])
        assert len(self.send_groups) <= SENDS
        return len(self.send_groups) - 1

    def make(self, src, dst, device, at, sent_at):
        return pltpu.make_async_remote_copy(
            src_ref=src,
            dst_ref=dst,
            send_sem=self.ssem.at[sent_at],
            recv_sem=self.rsem.at[at],
            device_id=device,
            device_id_type=MESH,
        )

    def near(self, ku, kb, src, dst, batch=None):
        at = self.take(1) if batch is None else batch.at
        copy = self.make(src, dst, (flip(self.u, ku), flip(self.b, kb)), at, self.send_slot(src))
        copy.start()
        if batch is not None:
            batch.size += self.size_of(src)
        return copy

    def size_of(self, src):
        size = src.dtype.itemsize
        for extent in src.shape:
            size *= extent
        return size

    def blk(self, k, src, dst, batch=None):
        return self.near(0, k, src, dst, batch)

    def uly(self, k, src, dst, batch=None):
        return self.near(k, 0, src, dst, batch)

    def here(self, src, dst):
        copy = pltpu.make_async_copy(src, dst, self.lsem.at[self.local])
        self.local += 1
        copy.start()
        return copy

    def finish(self):
        for at, (size, total) in enumerate(self.send_groups):
            if size is not None:
                self.await_bytes(self.ssem.at[at], total)


def partners(u, b):
    near = [(u, flip(b, k)) for k in range(1, 8)] + [(flip(u, k), b) for k in range(1, 4)]
    return near + [(flip(u, 1), flip(b, k)) for k in range(1, 4)]


def send_barrier(u, b):
    for device in partners(u, b):
        pl.semaphore_signal(pltpu.get_barrier_semaphore(), inc=1, device_id=device, device_id_type=MESH)


def wait_barrier():
    pl.semaphore_wait(pltpu.get_barrier_semaphore(), 13)


def norm_parts(values):
    center = jnp.mean(values, axis=-1, keepdims=True)
    offset = values - center
    spread = jnp.mean(offset * offset, axis=-1, keepdims=True)
    inv = lax.rsqrt(spread + 1e-05)
    return offset * inv, inv


def head_mask(shape, head):
    lane = lax.broadcasted_iota(jnp.int32, shape, len(shape) - 1)
    return (lane // 64) == head


def doc_begin(starts_ref, positions):
    begin = jnp.zeros_like(positions)
    for d in range(starts_ref.shape[0]):
        first = starts_ref[d]
        begin = jnp.where(positions >= first, jnp.full_like(positions, first), begin)
    return begin


def buffer_shapes(rows, width, hidden, heads):
    group = 8 * rows
    cols = 3 * heads
    third = hidden // 4
    return (
        ("x_all", (group, width), BF),
        ("n1", (group, width), BF),
        ("q_out", (8, 32, cols), BF),
        ("wqkv", (width, cols), BF),
        ("up_out", (8, 32, hidden), BF),
        ("wup", (2, 4, 2, 128, hidden), BF),
        ("wdown", (2, 2, 2, rows, width), BF),
        ("wproj", (4, 4, 2, 32, width), BF),
        ("q", (group, heads), BF),
        ("kv", (2 * group, 2 * heads), BF),
        ("lse", (2, group), F32),
        ("row_max", (2, group), F32),
        ("row_sum", (2, group), F32),
        ("o_rows", (heads, group), F32),
        ("att_heads", (group, heads), BF),
        ("att_in", (8, rows, heads), BF),
        ("att", (rows, width), BF),
        ("par", (32, 8, 128), F32),
        ("vec", (8, width), F32),
        ("n2_all", (4 * rows, width), BF),
        ("c_all", (4 * rows, width), BF),
        ("act", (2, 4 * rows, hidden), BF),
        ("gup", (2, 4 * rows, hidden), BF),
        ("out_part", (4 * rows, width), BF),
        ("g2_part", (4 * rows, width), BF),
        ("g2_far", (3, rows, width), BF),
        ("out_via", (2, rows // 2, width), BF),
        ("out_far", (2, rows, width), BF),
        ("mixed", (rows, width), F32),
        ("gmix", (rows, width), F32),
        ("gbr", (rows, width), BF),
        ("gatt", (8, rows, heads), BF),
        ("dwn", (2, 2, rows, width), BF),
        ("dup", (4, 2, 128, hidden), BF),
        ("dwn_out", (2, 2, rows, width), BF),
        ("dup_out", (4, 2, 128, hidden), BF),
        ("dwn_sib", (2, 2, rows, width), BF),
        ("dup_sib", (4, 2, 128, hidden), BF),
        ("dwn_y", (2, rows, width), BF),
        ("dup_y", (2, 2, 128, hidden), BF),
        ("dwn_keep", (rows, width), BF),
        ("dup_keep", (2, 128, hidden), BF),
        ("dwn_z", (rows, width), BF),
        ("dup_z", (2, 128, hidden), BF),
        ("dup_own", (8, 32, hidden), BF),
        ("gh", (group, heads), BF),
        ("delta", (2, group), F32),
        ("dq_rows", (heads, group), F32),
        ("dkv", (2 * group, 2 * heads), F32),
        ("halo_out", (group, 2 * heads), BF),
        ("halo_in", (group, 2 * heads), BF),
        ("gqkv", (group, cols), BF),
        ("g1_part", (group, width), BF),
        ("g1_sib", (4, rows, width), BF),
        ("g1_keep", (3, rows, width), BF),
        ("g1_far", (3, rows, width), BF),
        ("dpr", (4, 4, 2, 32, width), BF),
        ("dpr_sib", (4, 4, 32, width), BF),
        ("dpr_keep", (4, 4, 32, width), BF),
        ("dpr_via", (2, 2, 32, width), BF),
        ("dpr_u", (2, 2, 2, 32, width), BF),
        ("dpr_own", (4, 32, width), BF),
        ("dpr_z", (3, 32, width), BF),
        ("dq", (width, cols), BF),
        ("dq_via", (2, 128, cols), BF),
        ("dq_u", (2, 2, 128, cols), BF),
        ("dq_own", (8, 32, cols), BF),
        ("sm", (32, 8, 128), F32),
        ("sm_u", (3, 8, 8, 128), F32),
        ("sm_keep", (8, 8, 128), F32),
        ("sm_b", (7, 8, 128), F32),
    )


RECEIVES = 102
SENDS = 19


def block_kernel(shapes, *refs):
    (
        tok, wqkv_in, wproj_in, wup_in, wdown_in, cot,
        ln1_gain, ln1_bias, proj_bias, ln2_gain, ln2_bias, down_bias, qv_bias, up_bias_in, slopes, starts,
    ) = refs[:16]
    out_o, in_o, down_o, up_o, qkv_o, proj_o, vec_o = refs[16:23]
    ssem, rsem, lsem = refs[23 + len(shapes):]
    m = collections.namedtuple("Buffers", [s[0] for s in shapes])(*refs[23:23 + len(shapes)])

    w = Wire(
        ssem, rsem, lsem, ((32768, m.x_all, 16), (4096, m.sm, 1), (12288, m.wqkv, 16))
    )
    u, b = w.u, w.b
    z, c, zh = b // 2, b % 2, b // 4
    x, y = u % 2, u // 2
    rows, width = tok.shape
    group = 8 * rows
    pair = 2 * rows
    rank = x * 4 + b % 4
    chip2 = rank // 2
    mine_b = ds(b * rows, rows)
    mine_r = ds(chip2 * rows, rows)
    at = u * 8 + b
    send_barrier(u, b)
    m.par[at] = jnp.zeros((8, 128), F32)
    for row, v in enumerate((ln1_gain, ln1_bias, proj_bias, ln2_gain, ln2_bias, down_bias, qv_bias, up_bias_in)):
        m.par[at, row:row + 1, 0:v.shape[0]] = v[...].astype(F32).reshape(1, v.shape[0])
    for r in range(8):
        for part in range(3):
            m.q_out[r, :, part * 128:(part + 1) * 128] = wqkv_in[
                :, part * width + r * 128:part * width + (r + 1) * 128
            ]
    wrow = ds(at * 32, 32)
    m.wqkv[wrow] = m.q_out[b]
    for r in range(8):
        for ch in range(4):
            src = ((ch // 2) * 16 + (r // 4) * 8 + (ch % 2) * 4 + r % 4) * 128
            m.up_out[r, :, ch * 128:(ch + 1) * 128] = wup_in[:, src:src + 128]
    m.x_all[mine_b] = tok[...]
    m.c_all[mine_r] = cot[...]
    wait_barrier()

    q1 = Batch(w)
    for k in range(1, 8):
        w.blk(k, m.q_out.at[flip(b, k)], m.wqkv.at[wrow], batch=q1)
    p1 = Batch(w)
    for k in range(1, 8):
        w.blk(k, m.par.at[at], m.par.at[at], batch=p1)
    up_row = ds((b % 4) * 32, 32)
    pr1 = {k: w.blk(2 * k, wproj_in, m.wproj.at[u, z, c]) for k in (2, 1)}
    pr2 = Batch(w)
    for k in range(1, 4):
        w.uly(k, wproj_in, m.wproj.at[u, z, c], batch=pr2)

    def proj_on(k):
        pr1[k].wait_recv()
        slot = m.wproj.at[u, flip(z, k), c]
        for j in range(1, 4):
            w.uly(j, slot, slot, batch=pr2)

    t_sib = w.blk(1, tok, m.x_all.at[mine_b])
    c_x = w.uly(1, cot, m.c_all.at[mine_r])
    d2 = [w.uly(2, wdown_in, m.wdown.at[c, y, zh])]
    w_sib = [w.blk(1, wdown_in, m.wdown.at[c, y, zh])]

    def to_sib(piece):
        w_sib.append(w.blk(1, piece, piece))

    l_up = w.here(m.up_out.at[rank], m.wup.at[c, u, zh, up_row])
    l_down = w.here(wdown_in, m.wdown.at[c, y, zh])
    l_proj = w.here(wproj_in, m.wproj.at[u, z, c])

    p1.wait_recv()
    mine = m.par.at[ds(u * 8, 8)]
    p2 = Batch(w)
    for k in range(1, 4):
        w.uly(k, mine, mine, batch=p2)
    q1.wait_recv()
    mine = m.wqkv.at[ds(u * 256, 256)]
    q2 = Batch(w)
    for k in range(1, 4):
        w.uly(k, mine, mine, batch=q2)
    proj_on(2)
    slot = m.wproj.at[u, flip(z, 2), c]
    pr1[3] = w.blk(2, slot, slot)
    proj_on(1)
    slot = m.x_all.at[mine_b]
    t_z = {2: w.blk(4, tok, slot), 1: w.blk(2, tok, slot)}

    fwd = {}

    def to_sibling(k):
        slot = m.x_all.at[ds(flip(b, 2 * k) * rows, rows)]
        fwd[k] = w.blk(1, slot, slot)

    t_z[2].wait_recv()
    slot = m.x_all.at[ds(flip(b, 4) * rows, rows)]
    t_z[3] = w.blk(2, slot, slot)
    to_sibling(2)
    p2.wait_recv()
    for t in range(8):
        tiles = [pltpu.roll(m.par[4 * t + k], 32 * k, 1) if k else m.par[4 * t] for k in range(4)]
        m.vec[:, t * 128:(t + 1) * 128] = (tiles[0] + tiles[1]) + (tiles[2] + tiles[3])
    vec = m.vec
    q_bias = (m.par[2 * b] + pltpu.roll(m.par[2 * b + 1], 64, 1))[6:7]
    v_bias = (m.par[16 + 2 * b] + pltpu.roll(m.par[17 + 2 * b], 64, 1))[6:7]
    bias = jnp.concatenate([q_bias, jnp.zeros_like(q_bias), v_bias], axis=1)
    up_bias = [
        jnp.concatenate(
            [m.par[(ch // 2) * 16 + x * 8 + (ch % 2) * 4 + (b // 2) % 2 * 2 + core][7:8] for ch in range(4)], axis=1
        )
        for core in range(2)
    ]

    def normalize(zc):
        at = ds(zc * pair, pair)
        n, _ = norm_parts(m.x_all[at].astype(F32))
        m.n1[at] = (n * vec[0:1] + vec[1:2]).astype(BF)

    halo = w.take(4)
    halo_sent = w.take_send()

    def project(zc):
        at = ds(zc * pair, pair)
        out = (dot(m.n1[at], m.wqkv[...]) + bias).astype(BF)
        m.q[at] = out[:, :128]
        own = ds(group + zc * pair, pair)
        m.kv[own] = out[:, 128:]
        copy = w.make(m.kv.at[own], m.kv.at[at], (jnp.minimum(u + 1, 3), b), halo + zc, halo_sent)

        @pl.when(u < 3)
        def _():
            copy.start()

    t_sib.wait_recv()
    normalize(z)
    t_z[1].wait_recv()
    to_sibling(1)
    up1 = Batch(w)
    for k in range(1, 8):
        w.near(k // 4, k % 4, m.up_out.at[flip(rank, k)], m.wup.at[flip(c, k % 2), u, zh, up_row], batch=up1)
    proj_on(3)
    fwd[2].wait_recv()
    normalize(flip(z, 2))
    q2.wait_recv()
    project(z)
    project(flip(z, 2))
    fwd[1].wait_recv()
    normalize(flip(z, 1))
    project(flip(z, 1))
    t_z[3].wait_recv()
    to_sibling(3)
    c_z = w.blk(2, cot, m.c_all.at[mine_r])
    d1 = w.blk(4, wdown_in, m.wdown.at[c, y, zh])
    d2[0].wait_recv()
    to_sib(m.wdown.at[c, 1 - y, zh])
    fwd[3].wait_recv()
    normalize(flip(z, 3))
    project(flip(z, 3))
    up1.wait_recv()
    l_up.wait()
    mine = m.wup.at[c, ds(y * 2, 2), zh]
    up2 = w.blk(4, mine, mine)
    up3 = [w.uly(2, mine, mine)]
    to_sib(mine)
    @pl.when(u == 0)
    def _():
        m.kv[0:group] = jnp.zeros((group, 256), BF)

    att_at = w.take(1)
    att_sent = w.take_send()

    def stretch(i, own):
        count = (i + 1) * pair if own else group - i * pair
        first = 0 if own else i * pair - group
        place = lax.broadcasted_iota(jnp.int32, (count, pair), 0) + first
        qpos = lax.broadcasted_iota(jnp.int32, (1, pair), 1) + i * pair
        allowed = place >= doc_begin(starts, qpos + u * group) - u * group
        if own:
            allowed = allowed & (place <= qpos)
        return slice(group + first, group + first + count), allowed, (place[:, :1] - i * pair).astype(F32)

    def one_head(rows_of, h):
        return jnp.where(head_mask((pair, 128), h), rows_of, jnp.zeros_like(rows_of))

    def scores(keys, query, h, place):
        return dot(keys, one_head(query, h), NT) * 0.125 + slopes[2 * b + h] * place

    def by_head(first, second):
        line = lax.broadcasted_iota(jnp.int32, (128, pair), 0)
        return jnp.where(line < 64, first, second)

    def attend_own(i):
        span, allowed, place = stretch(i, True)
        at = slice(i * pair, (i + 1) * pair)
        out = []
        for h in range(2):
            s = jnp.where(allowed, scores(m.kv[span, 0:128], m.q[at], h, place), -1e30)
            top = jnp.max(s, axis=0, keepdims=True)
            p = jnp.exp(s - top)
            m.row_max[h:h + 1, at] = top
            m.row_sum[h:h + 1, at] = jnp.sum(p, axis=0, keepdims=True)
            out.append(dot(m.kv[span, 128:256], p.astype(BF), TN))
        m.o_rows[:, at] = by_head(*out)

    def attend(i):
        @pl.when(u > 0)
        def _():
            w.make(
                m.kv.at[ds(i * pair, pair)], m.kv.at[ds(i * pair, pair)], (u, b), halo + i, halo_sent
            ).wait_recv()

        span, allowed, place = stretch(i, False)
        at = slice(i * pair, (i + 1) * pair)
        out, shrinks, inverses = [], [], []
        for h in range(2):
            s = jnp.where(allowed, scores(m.kv[span, 0:128], m.q[at], h, place), -1e30)
            old = m.row_max[h:h + 1, at]
            top = jnp.maximum(old, jnp.max(s, axis=0, keepdims=True))
            p = jnp.exp(s - top)
            shrink = jnp.exp(old - top)
            total = m.row_sum[h:h + 1, at] * shrink + jnp.sum(p, axis=0, keepdims=True)
            m.lse[h:h + 1, at] = top + jnp.log(total)
            out.append(dot(m.kv[span, 128:256], p.astype(BF), TN))
            shrinks.append(shrink)
            inverses.append(1.0 / total)
        mixed_rows = (m.o_rows[:, at] * by_head(*shrinks) + by_head(*out)) * by_head(*inverses)
        m.o_rows[:, at] = mixed_rows
        m.att_heads[at] = mixed_rows.T.astype(BF)
        for half in range(2):
            target = 2 * i + half
            piece = m.att_heads.at[ds(target * rows, rows)]

            @pl.when(target != b)
            def _():
                w.make(piece, m.att_in.at[b], (u, target), att_at, att_sent).start()

    for i in range(4):
        attend_own(i)
    attend(3)
    l_proj.wait()
    pr2.wait_recv()
    mine = m.wproj.at[:, :, c]
    pr3 = w.blk(1, mine, mine)
    attend(2)
    d1.wait_recv()
    slot = m.wdown.at[c, y, 1 - zh]
    d2.append(w.uly(2, slot, slot))
    to_sib(slot)
    c_z.wait_recv()
    slot = m.c_all.at[ds(flip(chip2, 1) * rows, rows)]
    c_zx = w.uly(1, slot, slot)
    up3[0].wait_recv()
    to_sib(m.wup.at[c, ds((1 - y) * 2, 2), zh])
    attend(1)
    attend(0)
    m.att_in[b] = m.att_heads[mine_b]
    cot_f = cot[...].astype(F32)
    down_bias_sum = jnp.sum(cot_f, axis=0, keepdims=True)
    up2.wait_recv()
    mine = m.wup.at[c, ds(y * 2, 2), 1 - zh]
    up3.append(w.uly(2, mine, mine))
    to_sib(mine)
    att_bytes = 7 * w.size_of(m.att_in.at[0])
    w.await_bytes(w.rsem.at[att_at], att_bytes)
    w.await_bytes(w.ssem.at[att_sent], att_bytes)
    pr3.wait_recv()

    wproj = m.wproj[...].reshape(width, width)
    for r in range(8):
        m.att[:, r * 128:(r + 1) * 128] = m.att_in[r]
    mixed = tok[...].astype(F32) + dot(m.att[...], wproj) + vec[2:3]
    m.mixed[...] = mixed
    n2, inv2 = norm_parts(mixed)
    m.n2_all[mine_r] = (n2 * vec[3:4] + vec[4:5]).astype(BF)
    half_rows = rows // 2
    top, low = ds(0, half_rows), ds(half_rows, half_rows)

    def halves(owner, h):
        return m.n2_all.at[ds(owner * rows + h * half_rows, half_rows)]

    n_z = [w.blk(2, halves(chip2, 0), halves(chip2, 0))]
    n_x = [w.uly(1, halves(chip2, 1), halves(chip2, 1))]
    n_z.append(w.blk(2, halves(chip2, 1), halves(chip2, 1)))
    n_x.append(w.uly(1, halves(chip2, 0), halves(chip2, 0)))
    d2[1].wait_recv()
    to_sib(m.wdown.at[c, 1 - y, 1 - zh])
    up3[1].wait_recv()
    to_sib(m.wup.at[c, ds((1 - y) * 2, 2), 1 - zh])
    l_down.wait()
    hidden = m.act.shape[2]

    def feed(chip):
        at = ds(chip * rows, rows)
        out = g2 = 0.0
        for core in range(2):
            up = dot(m.n2_all[at], m.wup[core].reshape(width, hidden)) + up_bias[core]
            square = up * up
            th = jnp.tanh(0.7978845608028654 * (up + 0.044715 * square * up))
            act = (0.5 * up * (1.0 + th)).astype(BF)
            slope = 0.5 * (1.0 + th) + 0.5 * up * (1.0 - th * th) * (
                0.7978845608028654 * (1.0 + 3.0 * 0.044715 * square)
            )
            gup = (dot(m.c_all[at], m.wdown[core].reshape(hidden, width), NT) * slope).astype(BF)
            m.act[core, at] = act
            m.gup[core, at] = gup
            g2 = g2 + dot(gup, m.wup[core].reshape(width, hidden), NT)
            out = out + dot(act, m.wdown[core].reshape(hidden, width))
        m.g2_part[at] = g2.astype(BF)
        m.out_part[at] = out.astype(BF)

    hops = ((0, 2), (1, 0), (1, 2))
    g2_sends = []

    def return_g2(i):
        ku, kb = hops[i]
        far = flip(chip2, ku * 2 + kb // 2)
        g2_sends.append(w.near(ku, kb, m.g2_part.at[ds(far * rows, rows)], m.g2_far.at[i]))

    for copy in w_sib:
        copy.wait_recv()
    feed(chip2)
    n_z[0].wait_recv()
    n_diag = [w.uly(1, halves(flip(chip2, 1), 0), halves(flip(chip2, 1), 0))]
    n_x[0].wait_recv()
    n_diag.append(w.blk(2, halves(flip(chip2, 2), 1), halves(flip(chip2, 2), 1)))
    n_z[1].wait_recv()
    feed(flip(chip2, 1))
    return_g2(0)
    n_x[1].wait_recv()
    c_x.wait_recv()
    feed(flip(chip2, 2))
    return_g2(1)
    for copy in n_diag:
        copy.wait_recv()
    c_zx.wait_recv()
    feed(flip(chip2, 3))
    return_g2(2)
    other = 1 - c
    m.dwn_out[...] = dot(m.act[other], m.c_all[...], TN).astype(BF).reshape(2, 2, rows, width)
    s_dwn = w.blk(1, m.dwn_out, m.dwn_sib)
    m.dup_out[...] = dot(m.n2_all[...], m.gup[other], TN).astype(BF).reshape(4, 2, 128, hidden)
    s_dup = w.blk(1, m.dup_out, m.dup_sib)
    m.dwn[...] = dot(m.act[c], m.c_all[...], TN).astype(BF).reshape(2, 2, rows, width)
    m.dup[...] = dot(m.n2_all[...], m.gup[c], TN).astype(BF).reshape(4, 2, 128, hidden)
    up_bias_sums = [jnp.sum(m.gup[core].astype(F32), axis=0, keepdims=True) for core in range(2)]
    others = ds((1 - y) * 2, 2)
    s_dwn.wait_recv()
    m.dwn[...] = (m.dwn[...].astype(F32) + m.dwn_sib[...].astype(F32)).astype(BF)
    y_dwn = [w.uly(2, m.dwn.at[1 - y, 1 - zh], m.dwn_y.at[1 - zh])]
    s_dup.wait_recv()
    m.dup[...] = (m.dup[...].astype(F32) + m.dup_sib[...].astype(F32)).astype(BF)
    y_dup = [w.uly(2, m.dup.at[others, 1 - zh], m.dup_y.at[:, 1 - zh])]
    y_dwn.append(w.uly(2, m.dwn.at[1 - y, zh], m.dwn_y.at[zh]))
    y_dup.append(w.uly(2, m.dup.at[others, zh], m.dup_y.at[:, zh]))
    y_dwn[0].wait_recv()
    m.dwn_keep[...] = (m.dwn[y, 1 - zh].astype(F32) + m.dwn_y[1 - zh].astype(F32)).astype(BF)
    z1 = [w.blk(4, m.dwn_keep.at[top], m.dwn_z.at[top])]
    g = m.g2_part[mine_r].astype(F32)
    for i in range(3):
        g2_sends[i].wait_recv()
        g = g + m.g2_far[i].astype(F32)
    ln2_gain_sum = jnp.sum(g * n2, axis=0, keepdims=True)
    ln2_bias_sum = jnp.sum(g, axis=0, keepdims=True)
    e = g * vec[3:4]
    gmix = cot_f + inv2 * (
        e - jnp.mean(e, axis=-1, keepdims=True) - n2 * jnp.mean(e * n2, axis=-1, keepdims=True)
    )
    m.gmix[...] = gmix
    proj_bias_sum = jnp.sum(gmix, axis=0, keepdims=True)
    gbr = gmix.astype(BF)
    m.gbr[...] = gbr
    gatt = dot(gbr, wproj, NT).astype(BF)
    for r in range(8):
        m.gatt[r] = gatt[:, r * 128:(r + 1) * 128]

    g_to = w.take(8)
    g_sent = w.take_send()
    for k in range(1, 8):
        other = flip(b, k)
        w.make(m.gatt.at[other], m.gh.at[mine_b], (u, other), g_to + b, g_sent).start()
    m.gh[mine_b] = m.gatt[b]
    def out_rows(mask, part):
        return m.out_part.at[ds(flip(chip2, mask) * rows + part * half_rows, half_rows)]

    out_via = [w.blk(2, out_rows(3, 0), m.out_via.at[0]), w.uly(1, out_rows(3, 1), m.out_via.at[1])]
    out_sends = [w.blk(2, out_rows(1, 0), m.out_far.at[0, top]), w.uly(1, out_rows(2, 1), m.out_far.at[1, low])]
    for j in range(4):
        m.dpr[j] = dot(m.att[:, j * 256:(j + 1) * 256], gbr, TN).astype(BF).reshape(4, 2, 32, width)
    pg1 = w.blk(1, m.dpr.at[:, :, 1 - c], m.dpr_sib)
    m.dkv[...] = jnp.zeros_like(m.dkv)
    back = w.take(4)
    back_sent = w.take_send()

    def hand_back(i):
        at = ds(i * pair, pair)
        return w.make(m.halo_out.at[at], m.halo_in.at[at], (jnp.maximum(u - 1, 0), b), back + i, back_sent)

    def gradients(i, own):
        span, allowed, place = stretch(i, own)
        at = slice(i * pair, (i + 1) * pair)
        keys, vals = m.kv[span, 0:128], m.kv[span, 128:256]
        dk = dv = 0.0
        dq = []
        for h in range(2):
            gr = one_head(m.gh[at], h)
            s = scores(keys, m.q[at], h, place)
            p = jnp.where(allowed, jnp.exp(s - m.lse[h:h + 1, at]), 0.0)
            gs = (p * (dot(vals, gr, NT) - m.delta[h:h + 1, at])).astype(BF)
            dv = dv + dot(p.astype(BF), gr)
            dk = dk + dot(gs, one_head(m.q[at], h))
            dq.append(dot(keys, gs, TN))
        m.dkv[span, 0:128] += dk
        m.dkv[span, 128:256] += dv
        return by_head(*dq)

    def attend_back(i):
        for half in range(2):
            source = 2 * i + half

            @pl.when(source != b)
            def _():
                w.make(
                    m.gatt.at[b], m.gh.at[ds(source * rows, rows)], (u, b), g_to + source, g_sent
                ).wait_recv()

        at = slice(i * pair, (i + 1) * pair)
        products = m.gh[at].astype(F32).T * m.o_rows[:, at]
        m.delta[0:1, at] = jnp.sum(products[:64], axis=0, keepdims=True)
        m.delta[1:2, at] = jnp.sum(products[64:], axis=0, keepdims=True)
        m.dq_rows[:, at] = gradients(i, False)
        m.halo_out[at] = m.dkv[at].astype(BF)

        @pl.when(u > 0)
        def _():
            hand_back(i).start()

    class Fold:
        def __init__(self, part, via, far):
            self.part, self.via, self.far = part, via, far
            self.first = [w.uly(1, part(3, 0), via.at[0]), w.uly(2, part(3, 1), via.at[1])]
            self.all = [w.uly(1, part(1, 0), far.at[0, 0]), w.uly(2, part(2, 1), far.at[1, 1])]

        def second(self):
            for h, mask in enumerate((2, 1)):
                self.first[h].wait_recv()
                ref = self.part(mask, h)
                ref[...] = (ref[...].astype(F32) + self.via[h].astype(F32)).astype(BF)
                self.all.append(w.uly(mask, ref, self.far.at[mask - 1, h]))

        def total(self):
            for copy in self.all:
                copy.wait_recv()
            return [
                self.part(0, h)[...].astype(F32) + (self.far[0, h].astype(F32) + self.far[1, h].astype(F32))
                for h in range(2)
            ]

    attend_back(0)
    z1.append(w.blk(4, m.dwn_keep.at[low], m.dwn_z.at[low]))
    y_dup[0].wait_recv()
    m.dup_keep[...] = (m.dup[ds(y * 2, 2), 1 - zh].astype(F32) + m.dup_y[:, 1 - zh].astype(F32)).astype(BF)
    z2 = w.blk(4, m.dup_keep, m.dup_z)
    attend_back(1)
    attend_back(2)
    attend_back(3)
    for h, mask in enumerate((2, 1)):
        out_via[h].wait_recv()
        at = ds(flip(chip2, mask) * rows + h * half_rows, half_rows)
        m.out_part[at] = (m.out_part[at].astype(F32) + m.out_via[h].astype(F32)).astype(BF)
    out_sends += [w.uly(1, out_rows(2, 0), m.out_far.at[1, top]), w.blk(2, out_rows(1, 1), m.out_far.at[0, low])]
    for i in range(4):
        at = slice(i * pair, (i + 1) * pair)
        m.gqkv[at, 0:128] = ((m.dq_rows[:, at] + gradients(i, True)).T * 0.125).astype(BF)
    def complete(i):
        @pl.when(u < 3)
        def _():
            at = ds(i * pair, pair)
            own = ds(group + i * pair, pair)
            w.make(m.halo_out.at[at], m.halo_in.at[at], (u, b), back + i, back_sent).wait_recv()
            m.dkv[own] += m.halo_in[at].astype(F32)

        at = ds(i * pair, pair)
        own = ds(group + i * pair, pair)
        m.gqkv[at, 128:256] = (m.dkv[own, 0:128] * 0.125).astype(BF)
        m.gqkv[at, 256:384] = m.dkv[own, 128:256].astype(BF)

    swaps1 = {}

    def spread(k):
        chip = flip(z, k)
        complete(chip)
        at = ds(chip * pair, pair)
        m.g1_part[at] = dot(m.gqkv[at], m.wqkv[...], NT).astype(BF)
        other = ds(chip * pair + (1 - c) * rows, rows)
        swaps1[k] = w.blk(1, m.g1_part.at[other], m.g1_sib.at[k])

    def chip_sum(k):
        own = ds(flip(z, k) * pair + c * rows, rows)
        swaps1[k].wait_recv()
        return m.g1_part[own].astype(F32) + m.g1_sib[k].astype(F32)

    spread(3)
    n, inv = norm_parts(tok[...].astype(F32))
    m.g1_keep[2] = chip_sum(3).astype(BF)
    via = [w.blk(2, m.g1_keep.at[2, part], m.g1_far.at[2, part]) for part in (top, low)]
    spread(1)
    pg1.wait_recv()
    m.dpr_keep[...] = (m.dpr[:, :, c].astype(F32) + m.dpr_sib[...].astype(F32)).astype(BF)
    pg2 = Fold(lambda mask, h: m.dpr_keep.at[flip(u, mask), ds(2 * h, 2)], m.dpr_via, m.dpr_u)
    spread(2)
    spread(0)
    m.dq[...] = dot(m.n1[...], m.gqkv[...], TN).astype(BF)
    q2g = Fold(lambda mask, h: m.dq.at[ds(flip(u, mask) * 256 + h * 128, 128)], m.dq_via, m.dq_u)
    gain_sum = bias_sum = 0.0
    for i in range(4):
        at = slice(i * pair, (i + 1) * pair)
        part = m.g1_part[at].astype(F32)
        bias_sum = bias_sum + jnp.sum(part, axis=0, keepdims=True)
        gain_sum = gain_sum + jnp.sum(part * norm_parts(m.x_all[at].astype(F32))[0], axis=0, keepdims=True)
    qv_sums = jnp.sum(m.gqkv[...].astype(F32), axis=0, keepdims=True)
    lines = jnp.concatenate(
        [gain_sum, bias_sum, proj_bias_sum, ln2_gain_sum, ln2_bias_sum, down_bias_sum, jnp.zeros((2, width), F32)],
        axis=0,
    )
    for d in range(32):
        m.sm[d] = lines[:, (d // 4) * 128:(d // 4 + 1) * 128]
    for at, line in ((2 * b, qv_sums[:, 0:128]), (16 + 2 * b, qv_sums[:, 256:384])):
        m.sm[at, 6:7] = line
        m.sm[at + 1, 6:7] = line
    for core in range(2):
        for ch in range(4):
            at = (ch // 2) * 16 + x * 8 + (ch % 2) * 4 + (b // 2) % 2 * 2 + core
            m.sm[at, 7:8] = up_bias_sums[core][:, ch * 128:(ch + 1) * 128]
    s1 = Batch(w)
    for k in range(1, 4):
        w.uly(k, m.sm.at[ds(flip(u, k) * 8, 8)], m.sm_u.at[k - 1], batch=s1)
    pg2.second()
    sum2 = chip_sum(2)
    g1_cross = []
    for h, part in enumerate((top, low)):
        via[h].wait_recv()
        m.g1_keep[1, part] = (
            sum2[h * half_rows:(h + 1) * half_rows] + m.g1_far[2, part].astype(F32)
        ).astype(BF)
        g1_cross.append(w.blk(4, m.g1_keep.at[1, part], m.g1_far.at[1, part]))
    m.g1_keep[0] = chip_sum(1).astype(BF)
    g1_near = w.blk(2, m.g1_keep.at[0], m.g1_far.at[0])

    q2g.second()
    s1.wait_recv()
    m.sm_keep[...] = (m.sm[ds(u * 8, 8)] + m.sm_u[0]) + (m.sm_u[1] + m.sm_u[2])
    s2 = Batch(w)
    for k in range(1, 8):
        w.blk(k, m.sm_keep.at[flip(b, k)], m.sm_b.at[k - 1], batch=s2)
    for copy in z1:
        copy.wait_recv()
    y_dwn[1].wait_recv()
    down_o[...] = (m.dwn[y, zh].astype(F32) + m.dwn_y[zh].astype(F32)) + m.dwn_z[...].astype(F32)
    z2.wait_recv()
    y_dup[1].wait_recv()
    m.dup_own[...] = (
        (m.dup[ds(y * 2, 2), zh].astype(F32) + m.dup_y[:, zh].astype(F32)) + m.dup_z[...].astype(F32)
    ).astype(BF).reshape(8, 32, hidden)
    up3g = Batch(w)
    for k in range(1, 8):
        w.near(k // 4, k % 4, m.dup_own.at[flip(rank, k)], up_o.at[rank], batch=up3g)
    up_o[rank] = m.dup_own[rank]
    out = m.mixed[...] + vec[5:6] + m.out_part[mine_r].astype(F32)
    for copy in out_sends:
        copy.wait_recv()
    for i in range(2):
        out = out + m.out_far[i].astype(F32)
    out_o[...] = out.astype(BF)
    for h, total in enumerate(pg2.total()):
        m.dpr_own[2 * h:2 * h + 2] = total.astype(BF)
    pg3 = Batch(w)
    for k in range(1, 4):
        w.blk(2 * k, m.dpr_own.at[flip(z, k)], m.dpr_z.at[k - 1], batch=pg3)
    for h, total in enumerate(q2g.total()):
        m.dq_own[4 * h:4 * h + 4] = total.astype(BF).reshape(4, 32, 384)
    q3g = Batch(w)
    for k in range(1, 8):
        w.blk(k, m.dq_own.at[flip(b, k)], qkv_o.at[b], batch=q3g)
    qkv_o[b] = m.dq_own[b]

    g = chip_sum(0)
    g1_near.wait_recv()
    for copy in g1_cross:
        copy.wait_recv()
    g = g + m.g1_far[0].astype(F32) + m.g1_far[1].astype(F32)
    e = g * vec[0:1]
    in_o[...] = (
        m.gmix[...]
        + inv * (e - jnp.mean(e, axis=-1, keepdims=True) - n * jnp.mean(e * n, axis=-1, keepdims=True))
    ).astype(BF)
    pg3.wait_recv()
    proj_o[...] = (m.dpr_own[z].astype(F32) + m.dpr_z[0].astype(F32)) + (
        m.dpr_z[1].astype(F32) + m.dpr_z[2].astype(F32)
    )
    for batch in (up3g, q3g, s2):
        batch.wait_recv()
    total = m.sm_keep[b]
    for k in range(7):
        total = total + m.sm_b[k]
    line = lax.broadcasted_iota(jnp.int32, (8, 128), 0)
    by32 = pltpu.roll(total, (128 - 32 * (b % 4)) % 128, 1)
    by64 = pltpu.roll(total, (128 - 64 * (b % 2)) % 128, 1)
    vec_o[...] = jnp.where(line < 6, by32, jnp.where(line == 6, by64, total))

    w.await_bytes(w.ssem.at[g_sent], 7 * w.size_of(m.gatt.at[0]))

    @pl.when(u < 3)
    def _():
        w.await_bytes(w.ssem.at[halo_sent], w.size_of(m.halo_in))

    @pl.when(u > 0)
    def _():
        w.await_bytes(w.ssem.at[back_sent], w.size_of(m.halo_in))

    w.finish()


def finish_kernel(
    out, grad_in, down, up, qkv, proj, vec,
    out_o, in_o, g1_o, b1_o, qkv_o, qv_o, proj_o, pb_o, g2_o, b2_o, up_o, ub_o, down_o, db_o,
):
    out_o[...] = out[...]
    in_o[...] = grad_in[...]
    down_o[...] = down[...]
    proj_o[...] = proj[...]
    for r in range(8):
        for ch in range(4):
            to = ((ch // 2) * 16 + (r // 4) * 8 + (ch % 2) * 4 + r % 4) * 128
            up_o[:, to:to + 128] = up[r, :, ch * 128:(ch + 1) * 128].astype(F32)
        for part in range(3):
            to = part * 1024 + r * 128
            qkv_o[:, to:to + 128] = qkv[r, :, part * 128:(part + 1) * 128].astype(F32)
    for row, ref in enumerate((g1_o, b1_o, pb_o, g2_o, b2_o, db_o, qv_o, ub_o)):
        ref[...] = vec[row, 0:ref.shape[0]]


def fast_body(
    tokens, ln1_gain, ln1_bias, qkv_weight, qv_bias, proj_weight, proj_bias, ln2_gain, ln2_bias,
    up_weight, up_bias, down_weight, down_bias, alibi_slopes, doc_starts, cotangent,
):
    rows, width = tokens.shape
    shapes = buffer_shapes(rows, width, 512, 128)
    v = pl.BlockSpec(memory_space=pltpu.VMEM)
    s = pl.BlockSpec(memory_space=pltpu.SMEM)
    sds = jax.ShapeDtypeStruct
    parts = pl.pallas_call(
        functools.partial(block_kernel, shapes),
        name="transformer_block",
        out_shape=(
            sds((rows, width), BF),
            sds((rows, width), BF),
            sds((rows, width), F32),
            sds((8, 32, 512), BF),
            sds((8, 32, 384), BF),
            sds((32, width), F32),
            sds((8, 128), F32),
        ),
        in_specs=[v] * 14 + [s, s],
        out_specs=(v,) * 7,
        scratch_shapes=[pltpu.VMEM(shape, kind) for _, shape, kind in shapes]
        + [
            pltpu.SemaphoreType.DMA((SENDS,)),
            pltpu.SemaphoreType.DMA((RECEIVES,)),
            pltpu.SemaphoreType.DMA((3,)),
        ],
        compiler_params=pltpu.CompilerParams(
            collective_id=0, has_side_effects=True, vmem_limit_bytes=VMEM_LIMIT
        ),
    )(
        tokens, qkv_weight, proj_weight, up_weight, down_weight, cotangent,
        ln1_gain, ln1_bias, proj_bias, ln2_gain, ln2_bias, down_bias, qv_bias, up_bias,
        alibi_slopes, doc_starts,
    )
    vector = sds((32,), F32)
    return pl.pallas_call(
        finish_kernel,
        name="lay_out",
        out_shape=(
            sds((rows, width), BF), sds((rows, width), BF), vector, vector, sds((32, 3072), F32),
            sds((64,), F32), sds((32, width), F32), vector, vector, vector, sds((32, 4096), F32),
            sds((128,), F32), sds((rows, width), F32), vector,
        ),
        in_specs=[v] * 7,
        out_specs=(v,) * 14,
        compiler_params=pltpu.CompilerParams(vmem_limit_bytes=VMEM_LIMIT),
    )(*parts)


HEADS = 16
HEAD_DIM = 64


def layer_norm(values, norm_gain, norm_shift):
    center = jnp.mean(values, axis=-1, keepdims=True)
    offset = values - center
    spread = jnp.mean(offset * offset, axis=-1, keepdims=True)
    return offset * lax.rsqrt(spread + 1e-05) * norm_gain + norm_shift


def gelu_tanh(values):
    return (
        0.5
        * values
        * (1.0 + jnp.tanh(0.7978845608028654 * (values + 0.044715 * values * values * values)))
    )


def place_rows(local_rows, team_size, blk_count, tok_rows):
    team_span = team_size * tok_rows
    return (
        local_rows % team_span // tok_rows * blk_count + local_rows // team_span
    ) * tok_rows + local_rows % tok_rows


def doc_index(positions, doc_starts):
    return jnp.sum((positions[:, None] >= doc_starts[None, :]).astype(jnp.int32), axis=1) - 1


def split_rows(row_count, step_rows):
    return (row_count // step_rows, step_rows)


def score_block(queries, keys, query_pos, key_pos, query_doc, key_doc, slopes):
    raw_scores = jnp.einsum(
        "qhd,khd->hqk", queries, keys, preferred_element_type=jnp.float32
    ) * HEAD_DIM ** (-0.5)
    distance = (query_pos[:, None] - key_pos[None, :]).astype(jnp.float32)
    raw_scores = raw_scores - slopes[:, None, None] * distance[None]
    allowed = (key_pos[None, :] <= query_pos[:, None]) & (query_doc[:, None] == key_doc[None, :])
    return (jnp.where(allowed[None], raw_scores, -1e30), allowed[None])


def general_body(
    tokens,
    ln1_gain,
    ln1_bias,
    qkv_weight,
    qv_bias,
    proj_weight,
    proj_bias,
    ln2_gain,
    ln2_bias,
    up_weight,
    up_bias,
    down_weight,
    down_bias,
    alibi_slopes,
    doc_starts,
    cotangent,
):
    team_size = lax.axis_size("ulysses")
    blk_count = lax.axis_size("blk")
    tok_rows = tokens.shape[0]
    width_all = tokens.shape[1]
    head_rows = team_size * tok_rows
    heads_here = HEADS // team_size
    features = heads_here * HEAD_DIM
    scale_factor = HEAD_DIM ** (-0.5)
    gathered = (
        lax.all_gather(ln1_gain, ("ulysses", "blk"), axis=0, tiled=True),
        lax.all_gather(ln1_bias, ("ulysses", "blk"), axis=0, tiled=True),
        lax.all_gather(qkv_weight, ("ulysses", "blk"), axis=0, tiled=True),
        lax.all_gather(qv_bias, ("ulysses", "blk"), axis=0, tiled=True),
        lax.all_gather(proj_weight, ("ulysses", "blk"), axis=0, tiled=True),
        lax.all_gather(proj_bias, ("ulysses", "blk"), axis=0, tiled=True),
        lax.all_gather(ln2_gain, ("ulysses", "blk"), axis=0, tiled=True),
        lax.all_gather(ln2_bias, ("ulysses", "blk"), axis=0, tiled=True),
        lax.all_gather(up_weight, ("ulysses", "blk"), axis=0, tiled=True),
        lax.all_gather(up_bias, ("ulysses", "blk"), axis=0, tiled=True),
        lax.all_gather(down_weight, ("ulysses", "blk"), axis=0, tiled=True),
        lax.all_gather(down_bias, ("ulysses", "blk"), axis=0, tiled=True),
    )
    gain_one = gathered[0].astype(jnp.float32)
    shift_one = gathered[1].astype(jnp.float32)
    qkv_proj = gathered[2]
    qv_shift = gathered[3].astype(jnp.float32)
    proj_mat = gathered[4]
    proj_shift = gathered[5].astype(jnp.float32)
    gain_two = gathered[6].astype(jnp.float32)
    shift_two = gathered[7].astype(jnp.float32)
    up_mat = gathered[8]
    up_shift = gathered[9].astype(jnp.float32)
    down_mat = gathered[10]
    down_shift = gathered[11].astype(jnp.float32)
    inputs_f = tokens.astype(jnp.float32)
    normed_one = layer_norm(inputs_f, gain_one, shift_one).astype(jnp.bfloat16)
    joined_bias = jnp.concatenate(
        [qv_shift[:width_all], jnp.zeros((width_all,), jnp.float32), qv_shift[width_all:]]
    )
    joined = (
        jnp.dot(normed_one, qkv_proj, preferred_element_type=jnp.float32) + joined_bias
    ).astype(jnp.bfloat16)
    head_local = lax.all_to_all(
        joined.reshape(tok_rows, 3, team_size, features),
        "ulysses",
        split_axis=2,
        concat_axis=0,
        tiled=True,
    )
    queries_flat = head_local[:, 0, 0]
    queries = queries_flat.reshape(head_rows, heads_here, HEAD_DIM)
    key_value = head_local[:, 1:, 0]
    own_keys = key_value[:, 0].reshape(head_rows, heads_here, HEAD_DIM)
    own_values = key_value[:, 1].reshape(head_rows, heads_here, HEAD_DIM)
    slopes = lax.dynamic_slice_in_dim(
        alibi_slopes, lax.axis_index("ulysses") * heads_here, heads_here, 0
    )
    own_rows = lax.axis_index("blk") * head_rows + jnp.arange(head_rows, dtype=jnp.int32)
    own_pos = place_rows(own_rows, team_size, blk_count, tok_rows)
    own_doc = doc_index(own_pos, doc_starts)
    start_state = (
        jnp.full((heads_here, head_rows), -1e30, jnp.float32),
        jnp.zeros((heads_here, head_rows), jnp.float32),
        jnp.zeros((heads_here, head_rows, HEAD_DIM), jnp.float32),
    )
    carried = start_state
    piece_rows = lax.all_gather(key_value, "blk", axis=0, tiled=True)
    number, step_rows = split_rows(piece_rows.shape[0], head_rows)
    stacked = piece_rows.reshape(number, step_rows, 2, heads_here, HEAD_DIM)
    offsets = step_rows * jnp.arange(number, dtype=jnp.int32)

    def online_step(running, inputs_pair):
        best_now, norm_sum, accumulated = running
        kv_block, offset_now = inputs_pair
        key_pos = place_rows(
            offset_now + jnp.arange(step_rows, dtype=jnp.int32), team_size, blk_count, tok_rows
        )
        key_doc = doc_index(key_pos, doc_starts)
        masked, allowed = score_block(
            queries, kv_block[:, 0], own_pos, key_pos, own_doc, key_doc, slopes
        )
        best_next = jnp.maximum(best_now, jnp.max(masked, axis=-1))
        weights = jnp.where(allowed, jnp.exp(masked - best_next[..., None]), 0.0)
        shrink = jnp.exp(best_now - best_next)
        norm_sum = norm_sum * shrink + jnp.sum(weights, axis=-1)
        accumulated = accumulated * shrink[..., None] + jnp.einsum(
            "hqk,khd->hqd",
            weights.astype(jnp.bfloat16),
            kv_block[:, 1],
            preferred_element_type=jnp.float32,
        )
        return ((best_next, norm_sum, accumulated), None)

    carried, _ = lax.scan(online_step, carried, (stacked, offsets))
    best_all, norm_all, acc_all = carried
    attended_heads = acc_all / norm_all[..., None]
    log_norm = best_all + jnp.log(norm_all)
    attended_rows = (
        attended_heads.transpose(1, 0, 2).reshape(head_rows, 1, features).astype(jnp.bfloat16)
    )
    attended = lax.all_to_all(
        attended_rows, "ulysses", split_axis=0, concat_axis=1, tiled=True
    ).reshape(tok_rows, width_all)
    mixed = inputs_f + jnp.dot(attended, proj_mat, preferred_element_type=jnp.float32) + proj_shift
    normed_two = layer_norm(mixed, gain_two, shift_two).astype(jnp.bfloat16)
    up_values = jnp.dot(normed_two, up_mat, preferred_element_type=jnp.float32) + up_shift
    activated = gelu_tanh(up_values).astype(jnp.bfloat16)
    output = (
        mixed + jnp.dot(activated, down_mat, preferred_element_type=jnp.float32) + down_shift
    ).astype(jnp.bfloat16)
    contract_rows = (((0,), (0,)), ((), ()))
    contract_cols = (((1,), (1,)), ((), ()))
    grad_out = cotangent.astype(jnp.float32)
    down_grad = lax.dot_general(
        activated, cotangent, contract_rows, preferred_element_type=jnp.float32
    )
    down_bias_grad = jnp.sum(grad_out, axis=0)
    grad_act = lax.dot_general(
        cotangent, down_mat, contract_cols, preferred_element_type=jnp.float32
    )
    _, gelu_pull = jax.vjp(gelu_tanh, up_values)
    grad_up = gelu_pull(grad_act)[0].astype(jnp.bfloat16)
    up_grad = lax.dot_general(
        normed_two, grad_up, contract_rows, preferred_element_type=jnp.float32
    )
    up_bias_grad = jnp.sum(grad_up.astype(jnp.float32), axis=0)
    grad_norm_two = lax.dot_general(
        grad_up, up_mat, contract_cols, preferred_element_type=jnp.float32
    )
    _, norm_two_pull = jax.vjp(layer_norm, mixed, gain_two, shift_two)
    grad_mixed_part, ln2_gain_grad, ln2_bias_grad = norm_two_pull(grad_norm_two)
    grad_mixed = grad_out + grad_mixed_part
    grad_branch = grad_mixed.astype(jnp.bfloat16)
    proj_grad = lax.dot_general(
        attended, grad_branch, contract_rows, preferred_element_type=jnp.float32
    )
    proj_bias_grad = jnp.sum(grad_mixed, axis=0)
    grad_att = lax.dot_general(
        grad_branch, proj_mat, contract_cols, preferred_element_type=jnp.float32
    ).astype(jnp.bfloat16)
    grad_heads = lax.all_to_all(
        grad_att.reshape(tok_rows, team_size, features),
        "ulysses",
        split_axis=1,
        concat_axis=0,
        tiled=True,
    )
    grad_heads_flat = grad_heads[:, 0]
    grad_att_heads = grad_heads_flat.reshape(head_rows, heads_here, HEAD_DIM)
    delta = jnp.sum(grad_att_heads.astype(jnp.float32).transpose(1, 0, 2) * attended_heads, axis=-1)
    carried = jnp.zeros((heads_here, head_rows, HEAD_DIM), jnp.float32)
    piece_rows = lax.all_gather(key_value, "blk", axis=0, tiled=True)
    number, query_step_rows = split_rows(piece_rows.shape[0], head_rows)
    stacked = piece_rows.reshape(number, query_step_rows, 2, heads_here, HEAD_DIM)
    offsets = query_step_rows * jnp.arange(number, dtype=jnp.int32)

    def query_step(running, inputs_pair):
        kv_block, offset_now = inputs_pair
        key_pos = place_rows(
            offset_now + jnp.arange(query_step_rows, dtype=jnp.int32),
            team_size,
            blk_count,
            tok_rows,
        )
        key_doc = doc_index(key_pos, doc_starts)
        masked, allowed = score_block(
            queries, kv_block[:, 0], own_pos, key_pos, own_doc, key_doc, slopes
        )
        probs = jnp.where(allowed, jnp.exp(masked - log_norm[..., None]), 0.0)
        grad_probs = jnp.einsum(
            "qhd,khd->hqk", grad_att_heads, kv_block[:, 1], preferred_element_type=jnp.float32
        )
        grad_scores = (probs * (grad_probs - delta[..., None])).astype(jnp.bfloat16)
        running = running + jnp.einsum(
            "hqk,khd->hqd", grad_scores, kv_block[:, 0], preferred_element_type=jnp.float32
        )
        return (running, None)

    carried, _ = lax.scan(query_step, carried, (stacked, offsets))
    grad_queries = carried * scale_factor
    all_norms, all_deltas = (
        lax.all_gather(log_norm.T, "blk", axis=0, tiled=True),
        lax.all_gather(delta.T, "blk", axis=0, tiled=True),
    )
    empty_keys = jnp.zeros((head_rows, heads_here, HEAD_DIM), jnp.float32)
    carried = (empty_keys, empty_keys)
    pieces = (
        lax.all_gather(queries_flat, "blk", axis=0, tiled=True),
        lax.all_gather(grad_heads_flat, "blk", axis=0, tiled=True),
    )
    number, key_step_rows = split_rows(pieces[0].shape[0], head_rows)
    query_stack = pieces[0].reshape(number, key_step_rows, heads_here, HEAD_DIM)
    grad_stack = pieces[1].reshape(number, key_step_rows, heads_here, HEAD_DIM)
    offsets = key_step_rows * jnp.arange(number, dtype=jnp.int32)

    def key_step(running, inputs_triple):
        grad_keys_now, grad_values_now = running
        query_block, grad_block, offset_now = inputs_triple
        query_pos = place_rows(
            offset_now + jnp.arange(key_step_rows, dtype=jnp.int32), team_size, blk_count, tok_rows
        )
        query_doc = doc_index(query_pos, doc_starts)
        norm_block = lax.dynamic_slice_in_dim(all_norms, offset_now, key_step_rows, 0).T
        delta_block = lax.dynamic_slice_in_dim(all_deltas, offset_now, key_step_rows, 0).T
        masked, allowed = score_block(
            query_block, own_keys, query_pos, own_pos, query_doc, own_doc, slopes
        )
        probs = jnp.where(allowed, jnp.exp(masked - norm_block[..., None]), 0.0)
        grad_values_now = grad_values_now + jnp.einsum(
            "hqk,qhd->khd",
            probs.astype(jnp.bfloat16),
            grad_block,
            preferred_element_type=jnp.float32,
        )
        grad_probs = jnp.einsum(
            "qhd,khd->hqk", grad_block, own_values, preferred_element_type=jnp.float32
        )
        grad_scores = (probs * (grad_probs - delta_block[..., None])).astype(jnp.bfloat16)
        grad_keys_now = grad_keys_now + jnp.einsum(
            "hqk,qhd->khd", grad_scores, query_block, preferred_element_type=jnp.float32
        )
        return ((grad_keys_now, grad_values_now), None)

    carried, _ = lax.scan(key_step, carried, (query_stack, grad_stack, offsets))
    grad_keys, grad_values = carried
    grad_pack = jnp.stack(
        [
            grad_queries.transpose(1, 0, 2).reshape(head_rows, features),
            (grad_keys * scale_factor).reshape(head_rows, features),
            grad_values.reshape(head_rows, features),
        ],
        axis=1,
    ).astype(jnp.bfloat16)
    grad_joined = lax.all_to_all(
        grad_pack.reshape(head_rows, 3, 1, features),
        "ulysses",
        split_axis=0,
        concat_axis=2,
        tiled=True,
    ).reshape(tok_rows, 3 * width_all)
    qkv_grad = lax.dot_general(
        normed_one, grad_joined, contract_rows, preferred_element_type=jnp.float32
    )
    joined_sums = jnp.sum(grad_joined.astype(jnp.float32), axis=0)
    qv_bias_grad = jnp.concatenate([joined_sums[:width_all], joined_sums[2 * width_all :]])
    grad_norm_one = lax.dot_general(
        grad_joined, qkv_proj, contract_cols, preferred_element_type=jnp.float32
    )
    _, norm_one_pull = jax.vjp(layer_norm, inputs_f, gain_one, shift_one)
    grad_inputs_part, ln1_gain_grad, ln1_bias_grad = norm_one_pull(grad_norm_one)
    input_grad = (grad_mixed + grad_inputs_part).astype(jnp.bfloat16)
    shares = (
        lax.psum_scatter(ln1_gain_grad, ("ulysses", "blk"), scatter_dimension=0, tiled=True),
        lax.psum_scatter(ln1_bias_grad, ("ulysses", "blk"), scatter_dimension=0, tiled=True),
        lax.psum_scatter(qkv_grad, ("ulysses", "blk"), scatter_dimension=0, tiled=True),
        lax.psum_scatter(qv_bias_grad, ("ulysses", "blk"), scatter_dimension=0, tiled=True),
        lax.psum_scatter(proj_grad, ("ulysses", "blk"), scatter_dimension=0, tiled=True),
        lax.psum_scatter(proj_bias_grad, ("ulysses", "blk"), scatter_dimension=0, tiled=True),
        lax.psum_scatter(ln2_gain_grad, ("ulysses", "blk"), scatter_dimension=0, tiled=True),
        lax.psum_scatter(ln2_bias_grad, ("ulysses", "blk"), scatter_dimension=0, tiled=True),
        lax.psum_scatter(up_grad, ("ulysses", "blk"), scatter_dimension=0, tiled=True),
        lax.psum_scatter(up_bias_grad, ("ulysses", "blk"), scatter_dimension=0, tiled=True),
        lax.psum_scatter(down_grad, ("ulysses", "blk"), scatter_dimension=0, tiled=True),
        lax.psum_scatter(down_bias_grad, ("ulysses", "blk"), scatter_dimension=0, tiled=True),
    )
    return (
        output,
        input_grad,
        shares[0],
        shares[1],
        shares[2],
        shares[3],
        shares[4],
        shares[5],
        shares[6],
        shares[7],
        shares[8],
        shares[9],
        shares[10],
        shares[11],
    )


TOKEN_ROWS = P(("ulysses", "blk"), None)
VECTOR = P(("ulysses", "blk"))


def solution(mesh):
    whole = P()
    in_specs = (
        TOKEN_ROWS, VECTOR, VECTOR, TOKEN_ROWS, VECTOR, TOKEN_ROWS, VECTOR, VECTOR, VECTOR, TOKEN_ROWS,
        VECTOR, TOKEN_ROWS, VECTOR, whole, whole, TOKEN_ROWS,
    )
    out_specs = (
        TOKEN_ROWS, TOKEN_ROWS, VECTOR, VECTOR, TOKEN_ROWS, VECTOR, TOKEN_ROWS, VECTOR, VECTOR, VECTOR,
        TOKEN_ROWS, VECTOR, TOKEN_ROWS, VECTOR,
    )
    fits = mesh.shape["ulysses"] == 4 and mesh.shape["blk"] == 8
    return jax.shard_map(
        fast_body if fits else general_body,
        mesh=mesh, in_specs=in_specs, out_specs=out_specs, check_vma=False,
    )
```

```python
import collections
import functools

import jax
import jax.numpy as jnp
from jax import lax
from jax.experimental import pallas as pl
from jax.experimental.pallas import tpu as pltpu
from jax.sharding import PartitionSpec as P

BF = jnp.bfloat16
F32 = jnp.float32
MESH = pl.DeviceIdType.MESH
VMEM_LIMIT = 63 * 2**20
NT = (((1,), (1,)), ((), ()))
TN = (((0,), (0,)), ((), ()))
NN = (((1,), (0,)), ((), ()))


def dot(a, b, dims=NN):
    return lax.dot_general(a, b, dims, preferred_element_type=F32)


def flip(index, mask):
    out = index
    bit = 1
    while bit <= mask:
        if mask & bit:
            out = out + bit - 2 * bit * ((index // bit) % 2)
        bit *= 2
    return out


def ds(start, size, align=None):
    if not isinstance(start, int):
        start = pl.multiple_of(start, align or size)
    return pl.ds(start, size)


class Batch:
    def __init__(self, wire):
        self.wire = wire
        self.at = wire.take(1)
        self.size = 0

    def wait_recv(self):
        self.wire.await_bytes(self.wire.rsem.at[self.at], self.size)


class Wire:
    def __init__(self, ssem, rsem, lsem, measures):
        self.ssem, self.rsem, self.lsem = ssem, rsem, lsem
        self.measures = measures
        self.used = 0
        self.local = 0
        self.send_groups = []
        self.u = lax.axis_index("ulysses")
        self.b = lax.axis_index("blk")

    def take(self, count):
        first = self.used
        self.used += count
        assert self.used <= RECEIVES
        return first

    def take_send(self):
        self.send_groups.append([None, 0])
        assert len(self.send_groups) <= SENDS
        return len(self.send_groups) - 1

    def await_bytes(self, sem, size):
        for step, buffer, entries in self.measures:
            count = size // step * entries
            if size % step == 0 and count <= buffer.shape[0]:
                ref = buffer.at[pl.ds(0, count)]
                pltpu.make_async_copy(ref, ref, sem).wait()
                return
        assert False, size

    def send_slot(self, src, repeat=1):
        size = self.size_of(src)
        limit = max(step * (buffer.shape[0] // entries) for step, buffer, entries in self.measures if size % step == 0)
        for at, group in enumerate(self.send_groups):
            if group[0] == size and group[1] + size * repeat <= limit:
                group[1] += size * repeat
                return at
        self.send_groups.append([size, size * repeat])
        assert len(self.send_groups) <= SENDS
        return len(self.send_groups) - 1

    def make(self, src, dst, device, at, sent_at):
        return pltpu.make_async_remote_copy(
            src_ref=src,
            dst_ref=dst,
            send_sem=self.ssem.at[sent_at],
            recv_sem=self.rsem.at[at],
            device_id=device,
            device_id_type=MESH,
        )

    def near(self, ku, kb, src, dst, batch=None):
        at = self.take(1) if batch is None else batch.at
        copy = self.make(src, dst, (flip(self.u, ku), flip(self.b, kb)), at, self.send_slot(src))
        copy.start()
        if batch is not None:
            batch.size += self.size_of(src)
        return copy

    def size_of(self, src):
        size = src.dtype.itemsize
        for extent in src.shape:
            size *= extent
        return size

    def blk(self, k, src, dst, batch=None):
        return self.near(0, k, src, dst, batch)

    def uly(self, k, src, dst, batch=None):
        return self.near(k, 0, src, dst, batch)

    def here(self, src, dst):
        copy = pltpu.make_async_copy(src, dst, self.lsem.at[self.local])
        self.local += 1
        copy.start()
        return copy

    def finish(self):
        for at, (size, total) in enumerate(self.send_groups):
            if size is not None:
                self.await_bytes(self.ssem.at[at], total)


def partners(u, b):
    near = [(u, flip(b, k)) for k in range(1, 8)] + [(flip(u, k), b) for k in range(1, 4)]
    return near + [(flip(u, 1), flip(b, k)) for k in range(1, 4)]


def send_barrier(u, b):
    for device in partners(u, b):
        pl.semaphore_signal(pltpu.get_barrier_semaphore(), inc=1, device_id=device, device_id_type=MESH)


def wait_barrier():
    pl.semaphore_wait(pltpu.get_barrier_semaphore(), 13)


def norm_parts(values):
    center = jnp.mean(values, axis=-1, keepdims=True)
    offset = values - center
    spread = jnp.mean(offset * offset, axis=-1, keepdims=True)
    inv = lax.rsqrt(spread + 1e-05)
    return offset * inv, inv


def head_mask(shape, head):
    lane = lax.broadcasted_iota(jnp.int32, shape, len(shape) - 1)
    return (lane // 64) == head


def doc_begin(starts_ref, positions):
    begin = jnp.zeros_like(positions)
    for d in range(starts_ref.shape[0]):
        first = starts_ref[d]
        begin = jnp.where(positions >= first, jnp.full_like(positions, first), begin)
    return begin


def buffer_shapes(rows, width, hidden, heads):
    group = 8 * rows
    cols = 3 * heads
    third = hidden // 4
    return (
        ("x_all", (group, width), BF),
        ("n1", (group, width), BF),
        ("q_out", (8, 32, cols), BF),
        ("wqkv", (width, cols), BF),
        ("up_out", (8, 32, hidden), BF),
        ("wup", (2, 4, 2, 128, hidden), BF),
        ("wdown", (2, 2, 2, rows, width), BF),
        ("wproj", (4, 4, 2, 32, width), BF),
        ("q", (group, heads), BF),
        ("kv", (2 * group, 2 * heads), BF),
        ("lse", (2, group), F32),
        ("row_max", (2, group), F32),
        ("row_sum", (2, group), F32),
        ("o_rows", (heads, group), F32),
        ("att_heads", (group, heads), BF),
        ("att_in", (8, rows, heads), BF),
        ("att", (rows, width), BF),
        ("par", (32, 8, 128), F32),
        ("vec", (8, width), F32),
        ("n2_all", (4 * rows, width), BF),
        ("c_all", (4 * rows, width), BF),
        ("act", (2, 4 * rows, hidden), BF),
        ("gup", (2, 4 * rows, hidden), BF),
        ("out_part", (4 * rows, width), BF),
        ("g2_part", (4 * rows, width), BF),
        ("g2_far", (3, rows, width), BF),
        ("out_via", (2, rows // 2, width), BF),
        ("out_far", (2, rows, width), BF),
        ("mixed", (rows, width), F32),
        ("gmix", (rows, width), F32),
        ("gbr", (rows, width), BF),
        ("gatt", (8, rows, heads), BF),
        ("dwn", (2, 2, rows, width), BF),
        ("dup", (4, 2, 128, hidden), BF),
        ("dwn_out", (2, 2, rows, width), BF),
        ("dup_out", (4, 2, 128, hidden), BF),
        ("dwn_sib", (2, 2, rows, width), BF),
        ("dup_sib", (4, 2, 128, hidden), BF),
        ("dwn_y", (2, rows, width), BF),
        ("dup_y", (2, 2, 128, hidden), BF),
        ("dwn_keep", (rows, width), BF),
        ("dup_keep", (2, 128, hidden), BF),
        ("dwn_z", (rows, width), BF),
        ("dup_z", (2, 128, hidden), BF),
        ("dup_own", (8, 32, hidden), BF),
        ("gh", (group, heads), BF),
        ("delta", (2, group), F32),
        ("dq_rows", (heads, group), F32),
        ("dkv", (2 * group, 2 * heads), F32),
        ("halo_out", (group, 2 * heads), BF),
        ("halo_in", (group, 2 * heads), BF),
        ("gqkv", (group, cols), BF),
        ("g1_part", (group, width), BF),
        ("g1_sib", (4, rows, width), BF),
        ("g1_keep", (3, rows, width), BF),
        ("g1_far", (3, rows, width), BF),
        ("dpr", (4, 4, 2, 32, width), BF),
        ("dpr_sib", (4, 4, 32, width), BF),
        ("dpr_keep", (4, 4, 32, width), BF),
        ("dpr_via", (2, 2, 32, width), BF),
        ("dpr_u", (2, 2, 2, 32, width), BF),
        ("dpr_own", (4, 32, width), BF),
        ("dpr_z", (3, 32, width), BF),
        ("dq", (width, cols), BF),
        ("dq_via", (2, 128, cols), BF),
        ("dq_u", (2, 2, 128, cols), BF),
        ("dq_own", (8, 32, cols), BF),
        ("sm", (32, 8, 128), F32),
        ("sm_u", (3, 8, 8, 128), F32),
        ("sm_keep", (8, 8, 128), F32),
        ("sm_b", (7, 8, 128), F32),
    )


RECEIVES = 101
SENDS = 19


def block_kernel(shapes, *refs):
    (
        tok, wqkv_in, wproj_in, wup_in, wdown_in, cot,
        ln1_gain, ln1_bias, proj_bias, ln2_gain, ln2_bias, down_bias, qv_bias, up_bias_in, slopes, starts,
    ) = refs[:16]
    out_o, in_o, down_o, up_o, qkv_o, proj_o, vec_o = refs[16:23]
    ssem, rsem, lsem = refs[23 + len(shapes):]
    m = collections.namedtuple("Buffers", [s[0] for s in shapes])(*refs[23:23 + len(shapes)])

    w = Wire(
        ssem, rsem, lsem, ((32768, m.x_all, 16), (4096, m.sm, 1), (12288, m.wqkv, 16))
    )
    u, b = w.u, w.b
    z, c, zh = b // 2, b % 2, b // 4
    x, y = u % 2, u // 2
    rows, width = tok.shape
    group = 8 * rows
    pair = 2 * rows
    rank = x * 4 + b % 4
    mine_b = ds(b * rows, rows)
    own_rows = ds(0, rows)
    at = u * 8 + b
    send_barrier(u, b)
    m.par[at] = jnp.zeros((8, 128), F32)
    for row, v in enumerate((ln1_gain, ln1_bias, proj_bias, ln2_gain, ln2_bias, down_bias, qv_bias, up_bias_in)):
        m.par[at, row:row + 1, 0:v.shape[0]] = v[...].astype(F32).reshape(1, v.shape[0])
    for r in range(8):
        for part in range(3):
            m.q_out[r, :, part * 128:(part + 1) * 128] = wqkv_in[
                :, part * width + r * 128:part * width + (r + 1) * 128
            ]
    wrow = ds(at * 32, 32)
    m.wqkv[wrow] = m.q_out[b]
    for r in range(8):
        for ch in range(4):
            src = ((ch // 2) * 16 + (r // 4) * 8 + (ch % 2) * 4 + r % 4) * 128
            m.up_out[r, :, ch * 128:(ch + 1) * 128] = wup_in[:, src:src + 128]
    m.x_all[mine_b] = tok[...]
    m.c_all[own_rows] = cot[...]
    wait_barrier()

    q1 = Batch(w)
    for k in range(1, 8):
        w.blk(k, m.q_out.at[flip(b, k)], m.wqkv.at[wrow], batch=q1)
    p1 = Batch(w)
    for k in range(1, 8):
        w.blk(k, m.par.at[at], m.par.at[at], batch=p1)
    up_row = ds((b % 4) * 32, 32)
    pr1 = {k: w.blk(2 * k, wproj_in, m.wproj.at[u, z, c]) for k in (2, 1)}
    pr2 = Batch(w)
    for k in range(1, 4):
        w.uly(k, wproj_in, m.wproj.at[u, z, c], batch=pr2)

    def proj_on(k):
        pr1[k].wait_recv()
        slot = m.wproj.at[u, flip(z, k), c]
        for j in range(1, 4):
            w.uly(j, slot, slot, batch=pr2)

    slot = m.x_all.at[mine_b]
    t_z = {2: w.blk(4, tok, slot), 1: w.blk(2, tok, slot)}
    t_sib = w.blk(1, tok, m.x_all.at[mine_b])
    c_x = w.uly(1, cot, m.c_all.at[ds(2 * rows, rows)])
    d2 = [w.uly(2, wdown_in, m.wdown.at[c, y, zh])]
    w_sib = [w.blk(1, wdown_in, m.wdown.at[c, y, zh])]

    def to_sib(piece):
        w_sib.append(w.blk(1, piece, piece))

    l_up = w.here(m.up_out.at[rank], m.wup.at[c, u, zh, up_row])
    l_down = w.here(wdown_in, m.wdown.at[c, y, zh])
    l_proj = w.here(wproj_in, m.wproj.at[u, z, c])

    p1.wait_recv()
    mine = m.par.at[ds(u * 8, 8)]
    p2 = Batch(w)
    for k in range(1, 4):
        w.uly(k, mine, mine, batch=p2)
    q1.wait_recv()
    mine = m.wqkv.at[ds(u * 256, 256)]
    q2 = Batch(w)
    for k in range(1, 4):
        w.uly(k, mine, mine, batch=q2)
    proj_on(2)
    slot = m.wproj.at[u, flip(z, 2), c]
    pr1[3] = w.blk(2, slot, slot)
    proj_on(1)

    fwd = {}

    def to_sibling(k):
        slot = m.x_all.at[ds(flip(b, 2 * k) * rows, rows)]
        fwd[k] = w.blk(1, slot, slot)

    t_z[2].wait_recv()
    slot = m.x_all.at[ds(flip(b, 4) * rows, rows)]
    t_z[3] = w.blk(2, slot, slot)
    to_sibling(2)
    p2.wait_recv()
    for t in range(8):
        tiles = [pltpu.roll(m.par[4 * t + k], 32 * k, 1) if k else m.par[4 * t] for k in range(4)]
        m.vec[:, t * 128:(t + 1) * 128] = (tiles[0] + tiles[1]) + (tiles[2] + tiles[3])
    vec = m.vec
    q_bias = (m.par[2 * b] + pltpu.roll(m.par[2 * b + 1], 64, 1))[6:7]
    v_bias = (m.par[16 + 2 * b] + pltpu.roll(m.par[17 + 2 * b], 64, 1))[6:7]
    bias = jnp.concatenate([q_bias, jnp.zeros_like(q_bias), v_bias], axis=1)
    up_bias = [
        jnp.concatenate(
            [m.par[(ch // 2) * 16 + x * 8 + (ch % 2) * 4 + (b // 2) % 2 * 2 + core][7:8] for ch in range(4)], axis=1
        )
        for core in range(2)
    ]

    def normalize(zc):
        at = ds(zc * pair, pair)
        n, _ = norm_parts(m.x_all[at].astype(F32))
        m.n1[at] = (n * vec[0:1] + vec[1:2]).astype(BF)

    halo = w.take(4)
    halo_sent = w.take_send()

    def project(zc):
        at = ds(zc * pair, pair)
        out = (dot(m.n1[at], m.wqkv[...]) + bias).astype(BF)
        m.q[at] = out[:, :128]
        own = ds(group + zc * pair, pair)
        m.kv[own] = out[:, 128:]
        copy = w.make(m.kv.at[own], m.kv.at[at], (jnp.minimum(u + 1, 3), b), halo + zc, halo_sent)

        @pl.when(u < 3)
        def _():
            copy.start()

    t_sib.wait_recv()
    normalize(z)
    t_z[1].wait_recv()
    to_sibling(1)
    up1 = Batch(w)
    for k in range(1, 8):
        w.near(k // 4, k % 4, m.up_out.at[flip(rank, k)], m.wup.at[flip(c, k % 2), u, zh, up_row], batch=up1)
    proj_on(3)
    fwd[2].wait_recv()
    normalize(flip(z, 2))
    q2.wait_recv()
    project(z)
    project(flip(z, 2))
    fwd[1].wait_recv()
    normalize(flip(z, 1))
    project(flip(z, 1))
    t_z[3].wait_recv()
    to_sibling(3)
    c_z = w.blk(2, cot, m.c_all.at[ds(rows, rows)])
    d1 = w.blk(4, wdown_in, m.wdown.at[c, y, zh])
    d2[0].wait_recv()
    to_sib(m.wdown.at[c, 1 - y, zh])
    fwd[3].wait_recv()
    normalize(flip(z, 3))
    project(flip(z, 3))
    up1.wait_recv()
    l_up.wait()
    mine = m.wup.at[c, ds(y * 2, 2), zh]
    up2 = w.blk(4, mine, mine)
    up3 = [w.uly(2, mine, mine)]
    to_sib(mine)
    @pl.when(u == 0)
    def _():
        m.kv[0:group] = jnp.zeros((group, 256), BF)

    att_at = w.take(1)
    att_sent = w.take_send()

    def stretch(i, own):
        count = (i + 1) * pair if own else group - i * pair
        first = 0 if own else i * pair - group
        place = lax.broadcasted_iota(jnp.int32, (count, pair), 0) + first
        qpos = lax.broadcasted_iota(jnp.int32, (1, pair), 1) + i * pair
        allowed = place >= doc_begin(starts, qpos + u * group) - u * group
        if own:
            allowed = allowed & (place <= qpos)
        return slice(group + first, group + first + count), allowed, (place[:, :1] - i * pair).astype(F32)

    def one_head(rows_of, h):
        return jnp.where(head_mask((pair, 128), h), rows_of, jnp.zeros_like(rows_of))

    def scores(keys, query, h, place):
        return dot(keys, one_head(query, h), NT) * 0.125 + slopes[2 * b + h] * place

    def by_head(first, second):
        line = lax.broadcasted_iota(jnp.int32, (128, pair), 0)
        return jnp.where(line < 64, first, second)

    def attend_own(i):
        span, allowed, place = stretch(i, True)
        at = slice(i * pair, (i + 1) * pair)
        out = []
        for h in range(2):
            s = jnp.where(allowed, scores(m.kv[span, 0:128], m.q[at], h, place), -1e30)
            top = jnp.max(s, axis=0, keepdims=True)
            p = jnp.exp(s - top)
            m.row_max[h:h + 1, at] = top
            m.row_sum[h:h + 1, at] = jnp.sum(p, axis=0, keepdims=True)
            out.append(dot(m.kv[span, 128:256], p.astype(BF), TN))
        m.o_rows[:, at] = by_head(*out)

    def attend(i):
        @pl.when(u > 0)
        def _():
            w.make(
                m.kv.at[ds(i * pair, pair)], m.kv.at[ds(i * pair, pair)], (u, b), halo + i, halo_sent
            ).wait_recv()

        span, allowed, place = stretch(i, False)
        at = slice(i * pair, (i + 1) * pair)
        out, shrinks, inverses = [], [], []
        for h in range(2):
            s = jnp.where(allowed, scores(m.kv[span, 0:128], m.q[at], h, place), -1e30)
            old = m.row_max[h:h + 1, at]
            top = jnp.maximum(old, jnp.max(s, axis=0, keepdims=True))
            p = jnp.exp(s - top)
            shrink = jnp.exp(old - top)
            total = m.row_sum[h:h + 1, at] * shrink + jnp.sum(p, axis=0, keepdims=True)
            m.lse[h:h + 1, at] = top + jnp.log(total)
            out.append(dot(m.kv[span, 128:256], p.astype(BF), TN))
            shrinks.append(shrink)
            inverses.append(1.0 / total)
        mixed_rows = (m.o_rows[:, at] * by_head(*shrinks) + by_head(*out)) * by_head(*inverses)
        m.o_rows[:, at] = mixed_rows
        m.att_heads[at] = mixed_rows.T.astype(BF)
        for half in range(2):
            target = 2 * i + half
            piece = m.att_heads.at[ds(target * rows, rows)]

            @pl.when(target != b)
            def _():
                w.make(piece, m.att_in.at[b], (u, target), att_at, att_sent).start()

    for i in range(4):
        attend_own(i)
    attend(3)
    l_proj.wait()
    pr2.wait_recv()
    mine = m.wproj.at[:, :, c]
    pr3 = w.blk(1, mine, mine)
    attend(2)
    d1.wait_recv()
    slot = m.wdown.at[c, y, 1 - zh]
    d2.append(w.uly(2, slot, slot))
    to_sib(slot)
    c_z.wait_recv()
    c_zx = w.uly(1, m.c_all.at[ds(rows, rows)], m.c_all.at[ds(3 * rows, rows)])
    up3[0].wait_recv()
    to_sib(m.wup.at[c, ds((1 - y) * 2, 2), zh])
    attend(1)
    attend(0)
    m.att_in[b] = m.att_heads[mine_b]
    cot_f = cot[...].astype(F32)
    down_bias_sum = jnp.sum(cot_f, axis=0, keepdims=True)
    up2.wait_recv()
    mine = m.wup.at[c, ds(y * 2, 2), 1 - zh]
    up3.append(w.uly(2, mine, mine))
    to_sib(mine)
    att_bytes = 7 * w.size_of(m.att_in.at[0])
    w.await_bytes(w.rsem.at[att_at], att_bytes)
    w.await_bytes(w.ssem.at[att_sent], att_bytes)
    pr3.wait_recv()

    wproj = m.wproj[...].reshape(width, width)
    for r in range(8):
        m.att[:, r * 128:(r + 1) * 128] = m.att_in[r]
    mixed = tok[...].astype(F32) + dot(m.att[...], wproj) + vec[2:3]
    m.mixed[...] = mixed
    n2, inv2 = norm_parts(mixed)
    m.n2_all[own_rows] = (n2 * vec[3:4] + vec[4:5]).astype(BF)
    half_rows = rows // 2
    top, low = ds(0, half_rows), ds(half_rows, half_rows)

    def halves(owner, h):
        return m.n2_all.at[ds(owner * rows + h * half_rows, half_rows)]

    n_z = [w.blk(2, halves(0, 0), halves(1, 0))]
    n_x = [w.uly(1, halves(0, 1), halves(2, 1))]
    n_z.append(w.blk(2, halves(0, 1), halves(1, 1)))
    n_x.append(w.uly(1, halves(0, 0), halves(2, 0)))
    d2[1].wait_recv()
    to_sib(m.wdown.at[c, 1 - y, 1 - zh])
    up3[1].wait_recv()
    to_sib(m.wup.at[c, ds((1 - y) * 2, 2), 1 - zh])
    l_down.wait()
    hidden = m.act.shape[2]

    def feed(first, count):
        at = ds(first * rows, count * rows)
        out = g2 = 0.0
        for core in range(2):
            up = dot(m.n2_all[at], m.wup[core].reshape(width, hidden)) + up_bias[core]
            square = up * up
            th = jnp.tanh(0.7978845608028654 * (up + 0.044715 * square * up))
            act = (0.5 * up * (1.0 + th)).astype(BF)
            slope = 0.5 * (1.0 + th) + 0.5 * up * (1.0 - th * th) * (
                0.7978845608028654 * (1.0 + 3.0 * 0.044715 * square)
            )
            gup = (dot(m.c_all[at], m.wdown[core].reshape(hidden, width), NT) * slope).astype(BF)
            m.act[core, at] = act
            m.gup[core, at] = gup
            g2 = g2 + dot(gup, m.wup[core].reshape(width, hidden), NT)
            out = out + dot(act, m.wdown[core].reshape(hidden, width))
        m.g2_part[at] = g2.astype(BF)
        m.out_part[at] = out.astype(BF)

    hops = ((0, 2), (1, 0), (1, 2))
    g2_sends = []

    def return_g2(i):
        ku, kb = hops[i]
        far = ku * 2 + kb // 2
        g2_sends.append(w.near(ku, kb, m.g2_part.at[ds(far * rows, rows)], m.g2_far.at[i]))

    for copy in w_sib:
        copy.wait_recv()
    feed(0, 1)
    n_z[0].wait_recv()
    n_diag = [w.uly(1, halves(1, 0), halves(3, 0))]
    n_x[0].wait_recv()
    n_diag.append(w.blk(2, halves(2, 1), halves(3, 1)))
    n_z[1].wait_recv()
    n_x[1].wait_recv()
    c_x.wait_recv()
    feed(1, 2)
    return_g2(0)
    return_g2(1)
    for copy in n_diag:
        copy.wait_recv()
    c_zx.wait_recv()
    feed(3, 1)
    return_g2(2)
    other = 1 - c
    m.dwn_out[...] = dot(m.act[other], m.c_all[...], TN).astype(BF).reshape(2, 2, rows, width)
    s_dwn = w.blk(1, m.dwn_out, m.dwn_sib)
    m.dwn[...] = dot(m.act[c], m.c_all[...], TN).astype(BF).reshape(2, 2, rows, width)
    m.dup_out[...] = dot(m.n2_all[...], m.gup[other], TN).astype(BF).reshape(4, 2, 128, hidden)
    s_dup = w.blk(1, m.dup_out, m.dup_sib)
    others = ds((1 - y) * 2, 2)
    s_dwn.wait_recv()
    m.dwn[...] = (m.dwn[...].astype(F32) + m.dwn_sib[...].astype(F32)).astype(BF)
    y_dwn = [w.uly(2, m.dwn.at[1 - y, 1 - zh], m.dwn_y.at[1 - zh])]
    m.dup[...] = dot(m.n2_all[...], m.gup[c], TN).astype(BF).reshape(4, 2, 128, hidden)
    s_dup.wait_recv()
    m.dup[...] = (m.dup[...].astype(F32) + m.dup_sib[...].astype(F32)).astype(BF)
    y_dup = [w.uly(2, m.dup.at[others, 1 - zh], m.dup_y.at[:, 1 - zh])]
    y_dwn.append(w.uly(2, m.dwn.at[1 - y, zh], m.dwn_y.at[zh]))
    y_dup.append(w.uly(2, m.dup.at[others, zh], m.dup_y.at[:, zh]))
    up_bias_sums = [jnp.sum(m.gup[core].astype(F32), axis=0, keepdims=True) for core in range(2)]
    y_dwn[0].wait_recv()
    m.dwn_keep[...] = (m.dwn[y, 1 - zh].astype(F32) + m.dwn_y[1 - zh].astype(F32)).astype(BF)
    g = m.g2_part[own_rows].astype(F32)
    for i in range(3):
        g2_sends[i].wait_recv()
        g = g + m.g2_far[i].astype(F32)
    ln2_gain_sum = jnp.sum(g * n2, axis=0, keepdims=True)
    ln2_bias_sum = jnp.sum(g, axis=0, keepdims=True)
    e = g * vec[3:4]
    gmix = cot_f + inv2 * (
        e - jnp.mean(e, axis=-1, keepdims=True) - n2 * jnp.mean(e * n2, axis=-1, keepdims=True)
    )
    m.gmix[...] = gmix
    proj_bias_sum = jnp.sum(gmix, axis=0, keepdims=True)
    gbr = gmix.astype(BF)
    m.gbr[...] = gbr
    gatt = dot(gbr, wproj, NT).astype(BF)
    for r in range(8):
        m.gatt[r] = gatt[:, r * 128:(r + 1) * 128]

    g_to = w.take(8)
    g_sent = w.take_send()
    for k in range(1, 8):
        other = flip(b, k)
        w.make(m.gatt.at[other], m.gh.at[mine_b], (u, other), g_to + b, g_sent).start()
    m.gh[mine_b] = m.gatt[b]
    def out_rows(mask, part):
        return m.out_part.at[ds(mask * rows + part * half_rows, half_rows)]

    out_via = [w.blk(2, out_rows(3, 0), m.out_via.at[0]), w.uly(1, out_rows(3, 1), m.out_via.at[1])]
    out_sends = [w.blk(2, out_rows(1, 0), m.out_far.at[0, top]), w.uly(1, out_rows(2, 1), m.out_far.at[1, low])]
    for j in range(4):
        m.dpr[j] = dot(m.att[:, j * 256:(j + 1) * 256], gbr, TN).astype(BF).reshape(4, 2, 32, width)
    pg1 = w.blk(1, m.dpr.at[:, :, 1 - c], m.dpr_sib)
    m.dkv[...] = jnp.zeros_like(m.dkv)
    back = w.take(4)
    back_sent = w.take_send()

    def hand_back(i):
        at = ds(i * pair, pair)
        return w.make(m.halo_out.at[at], m.halo_in.at[at], (jnp.maximum(u - 1, 0), b), back + i, back_sent)

    def gradients(i, own):
        span, allowed, place = stretch(i, own)
        at = slice(i * pair, (i + 1) * pair)
        keys, vals = m.kv[span, 0:128], m.kv[span, 128:256]
        dk = dv = 0.0
        dq = []
        for h in range(2):
            gr = one_head(m.gh[at], h)
            s = scores(keys, m.q[at], h, place)
            p = jnp.where(allowed, jnp.exp(s - m.lse[h:h + 1, at]), 0.0)
            gs = (p * (dot(vals, gr, NT) - m.delta[h:h + 1, at])).astype(BF)
            dv = dv + dot(p.astype(BF), gr)
            dk = dk + dot(gs, one_head(m.q[at], h))
            dq.append(dot(keys, gs, TN))
        m.dkv[span, 0:128] += dk
        m.dkv[span, 128:256] += dv
        return by_head(*dq)

    def attend_back(i):
        for half in range(2):
            source = 2 * i + half

            @pl.when(source != b)
            def _():
                w.make(
                    m.gatt.at[b], m.gh.at[ds(source * rows, rows)], (u, b), g_to + source, g_sent
                ).wait_recv()

        at = slice(i * pair, (i + 1) * pair)
        products = m.gh[at].astype(F32).T * m.o_rows[:, at]
        m.delta[0:1, at] = jnp.sum(products[:64], axis=0, keepdims=True)
        m.delta[1:2, at] = jnp.sum(products[64:], axis=0, keepdims=True)
        m.dq_rows[:, at] = gradients(i, False)
        m.halo_out[at] = m.dkv[at].astype(BF)

        @pl.when(u > 0)
        def _():
            hand_back(i).start()

    class Fold:
        def __init__(self, part, via, far):
            self.part, self.via, self.far = part, via, far
            self.first = [w.uly(1, part(3, 0), via.at[0]), w.uly(2, part(3, 1), via.at[1])]
            self.all = [w.uly(1, part(1, 0), far.at[0, 0]), w.uly(2, part(2, 1), far.at[1, 1])]

        def second(self):
            for h, mask in enumerate((2, 1)):
                self.first[h].wait_recv()
                ref = self.part(mask, h)
                ref[...] = (ref[...].astype(F32) + self.via[h].astype(F32)).astype(BF)
                self.all.append(w.uly(mask, ref, self.far.at[mask - 1, h]))

        def total(self):
            for copy in self.all:
                copy.wait_recv()
            return [
                self.part(0, h)[...].astype(F32) + (self.far[0, h].astype(F32) + self.far[1, h].astype(F32))
                for h in range(2)
            ]

    attend_back(0)
    z1 = [w.blk(4, m.dwn_keep, m.dwn_z)]
    attend_back(1)
    attend_back(2)
    attend_back(3)
    for h, mask in enumerate((2, 1)):
        out_via[h].wait_recv()
        at = ds(mask * rows + h * half_rows, half_rows)
        m.out_part[at] = (m.out_part[at].astype(F32) + m.out_via[h].astype(F32)).astype(BF)
    out_sends += [w.uly(1, out_rows(2, 0), m.out_far.at[1, top]), w.blk(2, out_rows(1, 1), m.out_far.at[0, low])]
    y_dup[0].wait_recv()
    m.dup_keep[...] = (m.dup[ds(y * 2, 2), 1 - zh].astype(F32) + m.dup_y[:, 1 - zh].astype(F32)).astype(BF)
    z2 = w.blk(4, m.dup_keep, m.dup_z)
    for i in range(4):
        at = slice(i * pair, (i + 1) * pair)
        m.gqkv[at, 0:128] = ((m.dq_rows[:, at] + gradients(i, True)).T * 0.125).astype(BF)
    def complete(i):
        @pl.when(u < 3)
        def _():
            at = ds(i * pair, pair)
            own = ds(group + i * pair, pair)
            w.make(m.halo_out.at[at], m.halo_in.at[at], (u, b), back + i, back_sent).wait_recv()
            m.dkv[own] += m.halo_in[at].astype(F32)

        at = ds(i * pair, pair)
        own = ds(group + i * pair, pair)
        m.gqkv[at, 128:256] = (m.dkv[own, 0:128] * 0.125).astype(BF)
        m.gqkv[at, 256:384] = m.dkv[own, 128:256].astype(BF)

    swaps1 = {}

    def spread(k):
        chip = flip(z, k)
        complete(chip)
        at = ds(chip * pair, pair)
        m.g1_part[at] = dot(m.gqkv[at], m.wqkv[...], NT).astype(BF)
        other = ds(chip * pair + (1 - c) * rows, rows)
        swaps1[k] = w.blk(1, m.g1_part.at[other], m.g1_sib.at[k])

    def chip_sum(k):
        own = ds(flip(z, k) * pair + c * rows, rows)
        swaps1[k].wait_recv()
        return m.g1_part[own].astype(F32) + m.g1_sib[k].astype(F32)

    spread(3)
    n, inv = norm_parts(tok[...].astype(F32))
    m.g1_keep[2] = chip_sum(3).astype(BF)
    via = [w.blk(2, m.g1_keep.at[2, part], m.g1_far.at[2, part]) for part in (top, low)]
    spread(1)
    pg1.wait_recv()
    m.dpr_keep[...] = (m.dpr[:, :, c].astype(F32) + m.dpr_sib[...].astype(F32)).astype(BF)
    pg2 = Fold(lambda mask, h: m.dpr_keep.at[flip(u, mask), ds(2 * h, 2)], m.dpr_via, m.dpr_u)
    spread(2)
    spread(0)
    m.dq[...] = dot(m.n1[...], m.gqkv[...], TN).astype(BF)
    q2g = Fold(lambda mask, h: m.dq.at[ds(flip(u, mask) * 256 + h * 128, 128)], m.dq_via, m.dq_u)
    gain_sum = bias_sum = 0.0
    for i in range(4):
        at = slice(i * pair, (i + 1) * pair)
        part = m.g1_part[at].astype(F32)
        bias_sum = bias_sum + jnp.sum(part, axis=0, keepdims=True)
        gain_sum = gain_sum + jnp.sum(part * norm_parts(m.x_all[at].astype(F32))[0], axis=0, keepdims=True)
    qv_sums = jnp.sum(m.gqkv[...].astype(F32), axis=0, keepdims=True)
    lines = jnp.concatenate(
        [gain_sum, bias_sum, proj_bias_sum, ln2_gain_sum, ln2_bias_sum, down_bias_sum, jnp.zeros((2, width), F32)],
        axis=0,
    )
    for d in range(32):
        m.sm[d] = lines[:, (d // 4) * 128:(d // 4 + 1) * 128]
    for at, line in ((2 * b, qv_sums[:, 0:128]), (16 + 2 * b, qv_sums[:, 256:384])):
        m.sm[at, 6:7] = line
        m.sm[at + 1, 6:7] = line
    for core in range(2):
        for ch in range(4):
            at = (ch // 2) * 16 + x * 8 + (ch % 2) * 4 + (b // 2) % 2 * 2 + core
            m.sm[at, 7:8] = up_bias_sums[core][:, ch * 128:(ch + 1) * 128]
    s1 = Batch(w)
    for k in range(1, 4):
        w.uly(k, m.sm.at[ds(flip(u, k) * 8, 8)], m.sm_u.at[k - 1], batch=s1)
    pg2.second()
    sum2 = chip_sum(2)
    g1_cross = []
    def cross(h):
        part = (top, low)[h]
        via[h].wait_recv()
        m.g1_keep[1, part] = (
            sum2[h * half_rows:(h + 1) * half_rows] + m.g1_far[2, part].astype(F32)
        ).astype(BF)
        g1_cross.append(w.blk(4, m.g1_keep.at[1, part], m.g1_far.at[1, part]))

    cross(0)
    q2g.second()
    cross(1)
    m.g1_keep[0] = chip_sum(1).astype(BF)
    g1_near = w.blk(2, m.g1_keep.at[0], m.g1_far.at[0])

    s1.wait_recv()
    m.sm_keep[...] = (m.sm[ds(u * 8, 8)] + m.sm_u[0]) + (m.sm_u[1] + m.sm_u[2])
    s2 = Batch(w)
    for k in range(1, 8):
        w.blk(k, m.sm_keep.at[flip(b, k)], m.sm_b.at[k - 1], batch=s2)
    for copy in z1:
        copy.wait_recv()
    y_dwn[1].wait_recv()
    down_o[...] = (m.dwn[y, zh].astype(F32) + m.dwn_y[zh].astype(F32)) + m.dwn_z[...].astype(F32)
    z2.wait_recv()
    y_dup[1].wait_recv()
    m.dup_own[...] = (
        (m.dup[ds(y * 2, 2), zh].astype(F32) + m.dup_y[:, zh].astype(F32)) + m.dup_z[...].astype(F32)
    ).astype(BF).reshape(8, 32, hidden)
    up3g = Batch(w)
    for k in range(1, 8):
        w.near(k // 4, k % 4, m.dup_own.at[flip(rank, k)], up_o.at[rank], batch=up3g)
    up_o[rank] = m.dup_own[rank]
    out = m.mixed[...] + vec[5:6] + m.out_part[own_rows].astype(F32)
    for copy in out_sends:
        copy.wait_recv()
    for i in range(2):
        out = out + m.out_far[i].astype(F32)
    out_o[...] = out.astype(BF)
    for h, total in enumerate(pg2.total()):
        m.dpr_own[2 * h:2 * h + 2] = total.astype(BF)
    pg3 = Batch(w)
    for k in range(1, 4):
        w.blk(2 * k, m.dpr_own.at[flip(z, k)], m.dpr_z.at[k - 1], batch=pg3)
    for h, total in enumerate(q2g.total()):
        m.dq_own[4 * h:4 * h + 4] = total.astype(BF).reshape(4, 32, 384)
    q3g = Batch(w)
    for k in range(1, 8):
        w.blk(k, m.dq_own.at[flip(b, k)], qkv_o.at[b], batch=q3g)
    qkv_o[b] = m.dq_own[b]

    g = chip_sum(0)
    g1_near.wait_recv()
    for copy in g1_cross:
        copy.wait_recv()
    g = g + m.g1_far[0].astype(F32) + m.g1_far[1].astype(F32)
    e = g * vec[0:1]
    in_o[...] = (
        m.gmix[...]
        + inv * (e - jnp.mean(e, axis=-1, keepdims=True) - n * jnp.mean(e * n, axis=-1, keepdims=True))
    ).astype(BF)
    pg3.wait_recv()
    proj_o[...] = (m.dpr_own[z].astype(F32) + m.dpr_z[0].astype(F32)) + (
        m.dpr_z[1].astype(F32) + m.dpr_z[2].astype(F32)
    )
    for batch in (up3g, q3g, s2):
        batch.wait_recv()
    total = m.sm_keep[b]
    for k in range(7):
        total = total + m.sm_b[k]
    line = lax.broadcasted_iota(jnp.int32, (8, 128), 0)
    by32 = pltpu.roll(total, (128 - 32 * (b % 4)) % 128, 1)
    by64 = pltpu.roll(total, (128 - 64 * (b % 2)) % 128, 1)
    vec_o[...] = jnp.where(line < 6, by32, jnp.where(line == 6, by64, total))

    w.await_bytes(w.ssem.at[g_sent], 7 * w.size_of(m.gatt.at[0]))

    @pl.when(u < 3)
    def _():
        w.await_bytes(w.ssem.at[halo_sent], w.size_of(m.halo_in))

    @pl.when(u > 0)
    def _():
        w.await_bytes(w.ssem.at[back_sent], w.size_of(m.halo_in))

    w.finish()


def finish_kernel(
    out, grad_in, down, up, qkv, proj, vec,
    out_o, in_o, g1_o, b1_o, qkv_o, qv_o, proj_o, pb_o, g2_o, b2_o, up_o, ub_o, down_o, db_o,
):
    out_o[...] = out[...]
    in_o[...] = grad_in[...]
    down_o[...] = down[...]
    proj_o[...] = proj[...]
    for r in range(8):
        for ch in range(4):
            to = ((ch // 2) * 16 + (r // 4) * 8 + (ch % 2) * 4 + r % 4) * 128
            up_o[:, to:to + 128] = up[r, :, ch * 128:(ch + 1) * 128].astype(F32)
        for part in range(3):
            to = part * 1024 + r * 128
            qkv_o[:, to:to + 128] = qkv[r, :, part * 128:(part + 1) * 128].astype(F32)
    for row, ref in enumerate((g1_o, b1_o, pb_o, g2_o, b2_o, db_o, qv_o, ub_o)):
        ref[...] = vec[row, 0:ref.shape[0]]


def fast_body(
    tokens, ln1_gain, ln1_bias, qkv_weight, qv_bias, proj_weight, proj_bias, ln2_gain, ln2_bias,
    up_weight, up_bias, down_weight, down_bias, alibi_slopes, doc_starts, cotangent,
):
    rows, width = tokens.shape
    shapes = buffer_shapes(rows, width, 512, 128)
    v = pl.BlockSpec(memory_space=pltpu.VMEM)
    s = pl.BlockSpec(memory_space=pltpu.SMEM)
    sds = jax.ShapeDtypeStruct
    parts = pl.pallas_call(
        functools.partial(block_kernel, shapes),
        name="transformer_block",
        out_shape=(
            sds((rows, width), BF),
            sds((rows, width), BF),
            sds((rows, width), F32),
            sds((8, 32, 512), BF),
            sds((8, 32, 384), BF),
            sds((32, width), F32),
            sds((8, 128), F32),
        ),
        in_specs=[v] * 14 + [s, s],
        out_specs=(v,) * 7,
        scratch_shapes=[pltpu.VMEM(shape, kind) for _, shape, kind in shapes]
        + [
            pltpu.SemaphoreType.DMA((SENDS,)),
            pltpu.SemaphoreType.DMA((RECEIVES,)),
            pltpu.SemaphoreType.DMA((3,)),
        ],
        compiler_params=pltpu.CompilerParams(
            collective_id=0, has_side_effects=True, vmem_limit_bytes=VMEM_LIMIT
        ),
    )(
        tokens, qkv_weight, proj_weight, up_weight, down_weight, cotangent,
        ln1_gain, ln1_bias, proj_bias, ln2_gain, ln2_bias, down_bias, qv_bias, up_bias,
        alibi_slopes, doc_starts,
    )
    vector = sds((32,), F32)
    return pl.pallas_call(
        finish_kernel,
        name="lay_out",
        out_shape=(
            sds((rows, width), BF), sds((rows, width), BF), vector, vector, sds((32, 3072), F32),
            sds((64,), F32), sds((32, width), F32), vector, vector, vector, sds((32, 4096), F32),
            sds((128,), F32), sds((rows, width), F32), vector,
        ),
        in_specs=[v] * 7,
        out_specs=(v,) * 14,
        compiler_params=pltpu.CompilerParams(vmem_limit_bytes=VMEM_LIMIT),
    )(*parts)


HEADS = 16
HEAD_DIM = 64


def layer_norm(values, norm_gain, norm_shift):
    center = jnp.mean(values, axis=-1, keepdims=True)
    offset = values - center
    spread = jnp.mean(offset * offset, axis=-1, keepdims=True)
    return offset * lax.rsqrt(spread + 1e-05) * norm_gain + norm_shift


def gelu_tanh(values):
    return (
        0.5
        * values
        * (1.0 + jnp.tanh(0.7978845608028654 * (values + 0.044715 * values * values * values)))
    )


def place_rows(local_rows, team_size, blk_count, tok_rows):
    team_span = team_size * tok_rows
    return (
        local_rows % team_span // tok_rows * blk_count + local_rows // team_span
    ) * tok_rows + local_rows % tok_rows


def doc_index(positions, doc_starts):
    return jnp.sum((positions[:, None] >= doc_starts[None, :]).astype(jnp.int32), axis=1) - 1


def split_rows(row_count, step_rows):
    return (row_count // step_rows, step_rows)


def score_block(queries, keys, query_pos, key_pos, query_doc, key_doc, slopes):
    raw_scores = jnp.einsum(
        "qhd,khd->hqk", queries, keys, preferred_element_type=jnp.float32
    ) * HEAD_DIM ** (-0.5)
    distance = (query_pos[:, None] - key_pos[None, :]).astype(jnp.float32)
    raw_scores = raw_scores - slopes[:, None, None] * distance[None]
    allowed = (key_pos[None, :] <= query_pos[:, None]) & (query_doc[:, None] == key_doc[None, :])
    return (jnp.where(allowed[None], raw_scores, -1e30), allowed[None])


def general_body(
    tokens,
    ln1_gain,
    ln1_bias,
    qkv_weight,
    qv_bias,
    proj_weight,
    proj_bias,
    ln2_gain,
    ln2_bias,
    up_weight,
    up_bias,
    down_weight,
    down_bias,
    alibi_slopes,
    doc_starts,
    cotangent,
):
    team_size = lax.axis_size("ulysses")
    blk_count = lax.axis_size("blk")
    tok_rows = tokens.shape[0]
    width_all = tokens.shape[1]
    head_rows = team_size * tok_rows
    heads_here = HEADS // team_size
    features = heads_here * HEAD_DIM
    scale_factor = HEAD_DIM ** (-0.5)
    gathered = (
        lax.all_gather(ln1_gain, ("ulysses", "blk"), axis=0, tiled=True),
        lax.all_gather(ln1_bias, ("ulysses", "blk"), axis=0, tiled=True),
        lax.all_gather(qkv_weight, ("ulysses", "blk"), axis=0, tiled=True),
        lax.all_gather(qv_bias, ("ulysses", "blk"), axis=0, tiled=True),
        lax.all_gather(proj_weight, ("ulysses", "blk"), axis=0, tiled=True),
        lax.all_gather(proj_bias, ("ulysses", "blk"), axis=0, tiled=True),
        lax.all_gather(ln2_gain, ("ulysses", "blk"), axis=0, tiled=True),
        lax.all_gather(ln2_bias, ("ulysses", "blk"), axis=0, tiled=True),
        lax.all_gather(up_weight, ("ulysses", "blk"), axis=0, tiled=True),
        lax.all_gather(up_bias, ("ulysses", "blk"), axis=0, tiled=True),
        lax.all_gather(down_weight, ("ulysses", "blk"), axis=0, tiled=True),
        lax.all_gather(down_bias, ("ulysses", "blk"), axis=0, tiled=True),
    )
    gain_one = gathered[0].astype(jnp.float32)
    shift_one = gathered[1].astype(jnp.float32)
    qkv_proj = gathered[2]
    qv_shift = gathered[3].astype(jnp.float32)
    proj_mat = gathered[4]
    proj_shift = gathered[5].astype(jnp.float32)
    gain_two = gathered[6].astype(jnp.float32)
    shift_two = gathered[7].astype(jnp.float32)
    up_mat = gathered[8]
    up_shift = gathered[9].astype(jnp.float32)
    down_mat = gathered[10]
    down_shift = gathered[11].astype(jnp.float32)
    inputs_f = tokens.astype(jnp.float32)
    normed_one = layer_norm(inputs_f, gain_one, shift_one).astype(jnp.bfloat16)
    joined_bias = jnp.concatenate(
        [qv_shift[:width_all], jnp.zeros((width_all,), jnp.float32), qv_shift[width_all:]]
    )
    joined = (
        jnp.dot(normed_one, qkv_proj, preferred_element_type=jnp.float32) + joined_bias
    ).astype(jnp.bfloat16)
    head_local = lax.all_to_all(
        joined.reshape(tok_rows, 3, team_size, features),
        "ulysses",
        split_axis=2,
        concat_axis=0,
        tiled=True,
    )
    queries_flat = head_local[:, 0, 0]
    queries = queries_flat.reshape(head_rows, heads_here, HEAD_DIM)
    key_value = head_local[:, 1:, 0]
    own_keys = key_value[:, 0].reshape(head_rows, heads_here, HEAD_DIM)
    own_values = key_value[:, 1].reshape(head_rows, heads_here, HEAD_DIM)
    slopes = lax.dynamic_slice_in_dim(
        alibi_slopes, lax.axis_index("ulysses") * heads_here, heads_here, 0
    )
    own_rows = lax.axis_index("blk") * head_rows + jnp.arange(head_rows, dtype=jnp.int32)
    own_pos = place_rows(own_rows, team_size, blk_count, tok_rows)
    own_doc = doc_index(own_pos, doc_starts)
    start_state = (
        jnp.full((heads_here, head_rows), -1e30, jnp.float32),
        jnp.zeros((heads_here, head_rows), jnp.float32),
        jnp.zeros((heads_here, head_rows, HEAD_DIM), jnp.float32),
    )
    carried = start_state
    piece_rows = lax.all_gather(key_value, "blk", axis=0, tiled=True)
    number, step_rows = split_rows(piece_rows.shape[0], head_rows)
    stacked = piece_rows.reshape(number, step_rows, 2, heads_here, HEAD_DIM)
    offsets = step_rows * jnp.arange(number, dtype=jnp.int32)

    def online_step(running, inputs_pair):
        best_now, norm_sum, accumulated = running
        kv_block, offset_now = inputs_pair
        key_pos = place_rows(
            offset_now + jnp.arange(step_rows, dtype=jnp.int32), team_size, blk_count, tok_rows
        )
        key_doc = doc_index(key_pos, doc_starts)
        masked, allowed = score_block(
            queries, kv_block[:, 0], own_pos, key_pos, own_doc, key_doc, slopes
        )
        best_next = jnp.maximum(best_now, jnp.max(masked, axis=-1))
        weights = jnp.where(allowed, jnp.exp(masked - best_next[..., None]), 0.0)
        shrink = jnp.exp(best_now - best_next)
        norm_sum = norm_sum * shrink + jnp.sum(weights, axis=-1)
        accumulated = accumulated * shrink[..., None] + jnp.einsum(
            "hqk,khd->hqd",
            weights.astype(jnp.bfloat16),
            kv_block[:, 1],
            preferred_element_type=jnp.float32,
        )
        return ((best_next, norm_sum, accumulated), None)

    carried, _ = lax.scan(online_step, carried, (stacked, offsets))
    best_all, norm_all, acc_all = carried
    attended_heads = acc_all / norm_all[..., None]
    log_norm = best_all + jnp.log(norm_all)
    attended_rows = (
        attended_heads.transpose(1, 0, 2).reshape(head_rows, 1, features).astype(jnp.bfloat16)
    )
    attended = lax.all_to_all(
        attended_rows, "ulysses", split_axis=0, concat_axis=1, tiled=True
    ).reshape(tok_rows, width_all)
    mixed = inputs_f + jnp.dot(attended, proj_mat, preferred_element_type=jnp.float32) + proj_shift
    normed_two = layer_norm(mixed, gain_two, shift_two).astype(jnp.bfloat16)
    up_values = jnp.dot(normed_two, up_mat, preferred_element_type=jnp.float32) + up_shift
    activated = gelu_tanh(up_values).astype(jnp.bfloat16)
    output = (
        mixed + jnp.dot(activated, down_mat, preferred_element_type=jnp.float32) + down_shift
    ).astype(jnp.bfloat16)
    contract_rows = (((0,), (0,)), ((), ()))
    contract_cols = (((1,), (1,)), ((), ()))
    grad_out = cotangent.astype(jnp.float32)
    down_grad = lax.dot_general(
        activated, cotangent, contract_rows, preferred_element_type=jnp.float32
    )
    down_bias_grad = jnp.sum(grad_out, axis=0)
    grad_act = lax.dot_general(
        cotangent, down_mat, contract_cols, preferred_element_type=jnp.float32
    )
    _, gelu_pull = jax.vjp(gelu_tanh, up_values)
    grad_up = gelu_pull(grad_act)[0].astype(jnp.bfloat16)
    up_grad = lax.dot_general(
        normed_two, grad_up, contract_rows, preferred_element_type=jnp.float32
    )
    up_bias_grad = jnp.sum(grad_up.astype(jnp.float32), axis=0)
    grad_norm_two = lax.dot_general(
        grad_up, up_mat, contract_cols, preferred_element_type=jnp.float32
    )
    _, norm_two_pull = jax.vjp(layer_norm, mixed, gain_two, shift_two)
    grad_mixed_part, ln2_gain_grad, ln2_bias_grad = norm_two_pull(grad_norm_two)
    grad_mixed = grad_out + grad_mixed_part
    grad_branch = grad_mixed.astype(jnp.bfloat16)
    proj_grad = lax.dot_general(
        attended, grad_branch, contract_rows, preferred_element_type=jnp.float32
    )
    proj_bias_grad = jnp.sum(grad_mixed, axis=0)
    grad_att = lax.dot_general(
        grad_branch, proj_mat, contract_cols, preferred_element_type=jnp.float32
    ).astype(jnp.bfloat16)
    grad_heads = lax.all_to_all(
        grad_att.reshape(tok_rows, team_size, features),
        "ulysses",
        split_axis=1,
        concat_axis=0,
        tiled=True,
    )
    grad_heads_flat = grad_heads[:, 0]
    grad_att_heads = grad_heads_flat.reshape(head_rows, heads_here, HEAD_DIM)
    delta = jnp.sum(grad_att_heads.astype(jnp.float32).transpose(1, 0, 2) * attended_heads, axis=-1)
    carried = jnp.zeros((heads_here, head_rows, HEAD_DIM), jnp.float32)
    piece_rows = lax.all_gather(key_value, "blk", axis=0, tiled=True)
    number, query_step_rows = split_rows(piece_rows.shape[0], head_rows)
    stacked = piece_rows.reshape(number, query_step_rows, 2, heads_here, HEAD_DIM)
    offsets = query_step_rows * jnp.arange(number, dtype=jnp.int32)

    def query_step(running, inputs_pair):
        kv_block, offset_now = inputs_pair
        key_pos = place_rows(
            offset_now + jnp.arange(query_step_rows, dtype=jnp.int32),
            team_size,
            blk_count,
            tok_rows,
        )
        key_doc = doc_index(key_pos, doc_starts)
        masked, allowed = score_block(
            queries, kv_block[:, 0], own_pos, key_pos, own_doc, key_doc, slopes
        )
        probs = jnp.where(allowed, jnp.exp(masked - log_norm[..., None]), 0.0)
        grad_probs = jnp.einsum(
            "qhd,khd->hqk", grad_att_heads, kv_block[:, 1], preferred_element_type=jnp.float32
        )
        grad_scores = (probs * (grad_probs - delta[..., None])).astype(jnp.bfloat16)
        running = running + jnp.einsum(
            "hqk,khd->hqd", grad_scores, kv_block[:, 0], preferred_element_type=jnp.float32
        )
        return (running, None)

    carried, _ = lax.scan(query_step, carried, (stacked, offsets))
    grad_queries = carried * scale_factor
    all_norms, all_deltas = (
        lax.all_gather(log_norm.T, "blk", axis=0, tiled=True),
        lax.all_gather(delta.T, "blk", axis=0, tiled=True),
    )
    empty_keys = jnp.zeros((head_rows, heads_here, HEAD_DIM), jnp.float32)
    carried = (empty_keys, empty_keys)
    pieces = (
        lax.all_gather(queries_flat, "blk", axis=0, tiled=True),
        lax.all_gather(grad_heads_flat, "blk", axis=0, tiled=True),
    )
    number, key_step_rows = split_rows(pieces[0].shape[0], head_rows)
    query_stack = pieces[0].reshape(number, key_step_rows, heads_here, HEAD_DIM)
    grad_stack = pieces[1].reshape(number, key_step_rows, heads_here, HEAD_DIM)
    offsets = key_step_rows * jnp.arange(number, dtype=jnp.int32)

    def key_step(running, inputs_triple):
        grad_keys_now, grad_values_now = running
        query_block, grad_block, offset_now = inputs_triple
        query_pos = place_rows(
            offset_now + jnp.arange(key_step_rows, dtype=jnp.int32), team_size, blk_count, tok_rows
        )
        query_doc = doc_index(query_pos, doc_starts)
        norm_block = lax.dynamic_slice_in_dim(all_norms, offset_now, key_step_rows, 0).T
        delta_block = lax.dynamic_slice_in_dim(all_deltas, offset_now, key_step_rows, 0).T
        masked, allowed = score_block(
            query_block, own_keys, query_pos, own_pos, query_doc, own_doc, slopes
        )
        probs = jnp.where(allowed, jnp.exp(masked - norm_block[..., None]), 0.0)
        grad_values_now = grad_values_now + jnp.einsum(
            "hqk,qhd->khd",
            probs.astype(jnp.bfloat16),
            grad_block,
            preferred_element_type=jnp.float32,
        )
        grad_probs = jnp.einsum(
            "qhd,khd->hqk", grad_block, own_values, preferred_element_type=jnp.float32
        )
        grad_scores = (probs * (grad_probs - delta_block[..., None])).astype(jnp.bfloat16)
        grad_keys_now = grad_keys_now + jnp.einsum(
            "hqk,qhd->khd", grad_scores, query_block, preferred_element_type=jnp.float32
        )
        return ((grad_keys_now, grad_values_now), None)

    carried, _ = lax.scan(key_step, carried, (query_stack, grad_stack, offsets))
    grad_keys, grad_values = carried
    grad_pack = jnp.stack(
        [
            grad_queries.transpose(1, 0, 2).reshape(head_rows, features),
            (grad_keys * scale_factor).reshape(head_rows, features),
            grad_values.reshape(head_rows, features),
        ],
        axis=1,
    ).astype(jnp.bfloat16)
    grad_joined = lax.all_to_all(
        grad_pack.reshape(head_rows, 3, 1, features),
        "ulysses",
        split_axis=0,
        concat_axis=2,
        tiled=True,
    ).reshape(tok_rows, 3 * width_all)
    qkv_grad = lax.dot_general(
        normed_one, grad_joined, contract_rows, preferred_element_type=jnp.float32
    )
    joined_sums = jnp.sum(grad_joined.astype(jnp.float32), axis=0)
    qv_bias_grad = jnp.concatenate([joined_sums[:width_all], joined_sums[2 * width_all :]])
    grad_norm_one = lax.dot_general(
        grad_joined, qkv_proj, contract_cols, preferred_element_type=jnp.float32
    )
    _, norm_one_pull = jax.vjp(layer_norm, inputs_f, gain_one, shift_one)
    grad_inputs_part, ln1_gain_grad, ln1_bias_grad = norm_one_pull(grad_norm_one)
    input_grad = (grad_mixed + grad_inputs_part).astype(jnp.bfloat16)
    shares = (
        lax.psum_scatter(ln1_gain_grad, ("ulysses", "blk"), scatter_dimension=0, tiled=True),
        lax.psum_scatter(ln1_bias_grad, ("ulysses", "blk"), scatter_dimension=0, tiled=True),
        lax.psum_scatter(qkv_grad, ("ulysses", "blk"), scatter_dimension=0, tiled=True),
        lax.psum_scatter(qv_bias_grad, ("ulysses", "blk"), scatter_dimension=0, tiled=True),
        lax.psum_scatter(proj_grad, ("ulysses", "blk"), scatter_dimension=0, tiled=True),
        lax.psum_scatter(proj_bias_grad, ("ulysses", "blk"), scatter_dimension=0, tiled=True),
        lax.psum_scatter(ln2_gain_grad, ("ulysses", "blk"), scatter_dimension=0, tiled=True),
        lax.psum_scatter(ln2_bias_grad, ("ulysses", "blk"), scatter_dimension=0, tiled=True),
        lax.psum_scatter(up_grad, ("ulysses", "blk"), scatter_dimension=0, tiled=True),
        lax.psum_scatter(up_bias_grad, ("ulysses", "blk"), scatter_dimension=0, tiled=True),
        lax.psum_scatter(down_grad, ("ulysses", "blk"), scatter_dimension=0, tiled=True),
        lax.psum_scatter(down_bias_grad, ("ulysses", "blk"), scatter_dimension=0, tiled=True),
    )
    return (
        output,
        input_grad,
        shares[0],
        shares[1],
        shares[2],
        shares[3],
        shares[4],
        shares[5],
        shares[6],
        shares[7],
        shares[8],
        shares[9],
        shares[10],
        shares[11],
    )


TOKEN_ROWS = P(("ulysses", "blk"), None)
VECTOR = P(("ulysses", "blk"))


def solution(mesh):
    whole = P()
    in_specs = (
        TOKEN_ROWS, VECTOR, VECTOR, TOKEN_ROWS, VECTOR, TOKEN_ROWS, VECTOR, VECTOR, VECTOR, TOKEN_ROWS,
        VECTOR, TOKEN_ROWS, VECTOR, whole, whole, TOKEN_ROWS,
    )
    out_specs = (
        TOKEN_ROWS, TOKEN_ROWS, VECTOR, VECTOR, TOKEN_ROWS, VECTOR, TOKEN_ROWS, VECTOR, VECTOR, VECTOR,
        TOKEN_ROWS, VECTOR, TOKEN_ROWS, VECTOR,
    )
    fits = mesh.shape["ulysses"] == 4 and mesh.shape["blk"] == 8
    return jax.shard_map(
        fast_body if fits else general_body,
        mesh=mesh, in_specs=in_specs, out_specs=out_specs, check_vma=False,
    )
```

```python
import collections
import functools

import jax
import jax.numpy as jnp
from jax import lax
from jax.experimental import pallas as pl
from jax.experimental.pallas import tpu as pltpu
from jax.sharding import PartitionSpec as P

BF = jnp.bfloat16
F32 = jnp.float32
MESH = pl.DeviceIdType.MESH
VMEM_LIMIT = 63 * 2**20
NT = (((1,), (1,)), ((), ()))
TN = (((0,), (0,)), ((), ()))
NN = (((1,), (0,)), ((), ()))


def dot(a, b, dims=NN):
    return lax.dot_general(a, b, dims, preferred_element_type=F32)


def flip(index, mask):
    out = index
    bit = 1
    while bit <= mask:
        if mask & bit:
            out = out + bit - 2 * bit * ((index // bit) % 2)
        bit *= 2
    return out


def ds(start, size, align=None):
    if not isinstance(start, int):
        start = pl.multiple_of(start, align or size)
    return pl.ds(start, size)


class Batch:
    def __init__(self, wire):
        self.wire = wire
        self.at = wire.take(1)
        self.size = 0

    def wait_recv(self):
        self.wire.await_bytes(self.wire.rsem.at[self.at], self.size)


class Wire:
    def __init__(self, ssem, rsem, lsem, measures):
        self.ssem, self.rsem, self.lsem = ssem, rsem, lsem
        self.measures = measures
        self.used = 0
        self.local = 0
        self.send_groups = []
        self.u = lax.axis_index("ulysses")
        self.b = lax.axis_index("blk")

    def take(self, count):
        first = self.used
        self.used += count
        assert self.used <= RECEIVES
        return first

    def take_send(self):
        self.send_groups.append([None, 0])
        assert len(self.send_groups) <= SENDS
        return len(self.send_groups) - 1

    def await_bytes(self, sem, size):
        for step, buffer, entries in self.measures:
            count = size // step * entries
            if size % step == 0 and count <= buffer.shape[0]:
                ref = buffer.at[pl.ds(0, count)]
                pltpu.make_async_copy(ref, ref, sem).wait()
                return
        assert False, size

    def send_slot(self, src, repeat=1):
        size = self.size_of(src)
        limit = max(step * (buffer.shape[0] // entries) for step, buffer, entries in self.measures if size % step == 0)
        for at, group in enumerate(self.send_groups):
            if group[0] == size and group[1] + size * repeat <= limit:
                group[1] += size * repeat
                return at
        self.send_groups.append([size, size * repeat])
        assert len(self.send_groups) <= SENDS
        return len(self.send_groups) - 1

    def make(self, src, dst, device, at, sent_at):
        return pltpu.make_async_remote_copy(
            src_ref=src,
            dst_ref=dst,
            send_sem=self.ssem.at[sent_at],
            recv_sem=self.rsem.at[at],
            device_id=device,
            device_id_type=MESH,
        )

    def near(self, ku, kb, src, dst, batch=None):
        at = self.take(1) if batch is None else batch.at
        copy = self.make(src, dst, (flip(self.u, ku), flip(self.b, kb)), at, self.send_slot(src))
        copy.start()
        if batch is not None:
            batch.size += self.size_of(src)
        return copy

    def size_of(self, src):
        size = src.dtype.itemsize
        for extent in src.shape:
            size *= extent
        return size

    def blk(self, k, src, dst, batch=None):
        return self.near(0, k, src, dst, batch)

    def uly(self, k, src, dst, batch=None):
        return self.near(k, 0, src, dst, batch)

    def here(self, src, dst):
        copy = pltpu.make_async_copy(src, dst, self.lsem.at[self.local])
        self.local += 1
        copy.start()
        return copy

    def finish(self):
        for at, (size, total) in enumerate(self.send_groups):
            if size is not None:
                self.await_bytes(self.ssem.at[at], total)


def partners(u, b):
    near = [(u, flip(b, k)) for k in range(1, 8)] + [(flip(u, k), b) for k in range(1, 4)]
    return near + [(flip(u, 1), flip(b, k)) for k in range(1, 4)]


def send_barrier(u, b):
    for device in partners(u, b):
        pl.semaphore_signal(pltpu.get_barrier_semaphore(), inc=1, device_id=device, device_id_type=MESH)


def wait_barrier():
    pl.semaphore_wait(pltpu.get_barrier_semaphore(), 13)


def norm_parts(values):
    center = jnp.mean(values, axis=-1, keepdims=True)
    offset = values - center
    spread = jnp.mean(offset * offset, axis=-1, keepdims=True)
    inv = lax.rsqrt(spread + 1e-05)
    return offset * inv, inv


def head_mask(shape, head):
    lane = lax.broadcasted_iota(jnp.int32, shape, len(shape) - 1)
    return (lane // 64) == head


def doc_begin(starts_ref, positions):
    begin = jnp.zeros_like(positions)
    for d in range(starts_ref.shape[0]):
        first = starts_ref[d]
        begin = jnp.where(positions >= first, jnp.full_like(positions, first), begin)
    return begin


def buffer_shapes(rows, width, hidden, heads):
    group = 8 * rows
    cols = 3 * heads
    third = hidden // 4
    return (
        ("wqkv_in", (32, 3 * width), BF),
        ("wup_in", (32, 8 * hidden), BF),
        ("x_all", (group, width), BF),
        ("n1", (group, width), BF),
        ("q_out", (8, 32, cols), BF),
        ("wqkv", (width, cols), BF),
        ("up_out", (8, 32, hidden), BF),
        ("wup", (2, 4, 2, 128, hidden), BF),
        ("wdown", (2, 2, 2, rows, width), BF),
        ("wproj", (4, 4, 2, 32, width), BF),
        ("q", (group, heads), BF),
        ("kv", (2 * group, 2 * heads), BF),
        ("lse", (2, group), F32),
        ("row_max", (2, group), F32),
        ("row_sum", (2, group), F32),
        ("o_rows", (heads, group), F32),
        ("att_heads", (group, heads), BF),
        ("att_in", (8, rows, heads), BF),
        ("att", (rows, width), BF),
        ("par", (32, 8, 128), F32),
        ("vec", (8, width), F32),
        ("n2_all", (4 * rows, width), BF),
        ("c_all", (4 * rows, width), BF),
        ("act", (2, 4 * rows, hidden), BF),
        ("gup", (2, 4 * rows, hidden), BF),
        ("out_part", (4 * rows, width), BF),
        ("g2_part", (4 * rows, width), BF),
        ("g2_far", (3, rows, width), BF),
        ("out_via", (2, rows // 2, width), BF),
        ("out_far", (2, rows, width), BF),
        ("mixed", (rows, width), F32),
        ("gmix", (rows, width), F32),
        ("gbr", (rows, width), BF),
        ("gatt", (8, rows, heads), BF),
        ("dwn", (2, 2, rows, width), BF),
        ("dup", (4, 2, 128, hidden), BF),
        ("dwn_out", (2, 2, rows, width), BF),
        ("dup_out", (4, 2, 128, hidden), BF),
        ("dwn_sib", (2, 2, rows, width), BF),
        ("dup_sib", (4, 2, 128, hidden), BF),
        ("dwn_y", (2, rows, width), BF),
        ("dup_y", (2, 2, 128, hidden), BF),
        ("dwn_keep", (rows, width), BF),
        ("dup_keep", (2, 128, hidden), BF),
        ("dwn_z", (rows, width), BF),
        ("dup_z", (2, 128, hidden), BF),
        ("dup_own", (8, 32, hidden), BF),
        ("gh", (group, heads), BF),
        ("delta", (2, group), F32),
        ("dq_rows", (heads, group), F32),
        ("dkv", (2 * group, 2 * heads), F32),
        ("halo_out", (group, 2 * heads), BF),
        ("halo_in", (group, 2 * heads), BF),
        ("gqkv", (group, cols), BF),
        ("g1_part", (group, width), BF),
        ("g1_sib", (4, rows, width), BF),
        ("g1_keep", (3, rows, width), BF),
        ("g1_far", (3, rows, width), BF),
        ("dpr", (4, 4, 2, 32, width), BF),
        ("dpr_sib", (4, 4, 32, width), BF),
        ("dpr_keep", (4, 4, 32, width), BF),
        ("dpr_via", (2, 2, 32, width), BF),
        ("dpr_u", (2, 2, 2, 32, width), BF),
        ("dpr_own", (4, 32, width), BF),
        ("dpr_z", (3, 32, width), BF),
        ("dq", (width, cols), BF),
        ("dq_via", (2, 128, cols), BF),
        ("dq_u", (2, 2, 128, cols), BF),
        ("dq_own", (8, 32, cols), BF),
        ("sm", (32, 8, 128), F32),
        ("sm_u", (3, 8, 8, 128), F32),
        ("sm_keep", (8, 8, 128), F32),
        ("sm_b", (7, 8, 128), F32),
    )


RECEIVES = 101
SENDS = 19


def block_kernel(shapes, *refs):
    (
        tok, wqkv_hbm, wproj_in, wup_hbm, wdown_in, cot,
        ln1_gain, ln1_bias, proj_bias, ln2_gain, ln2_bias, down_bias, qv_bias, up_bias_in, slopes, starts,
    ) = refs[:16]
    out_o, in_o, down_o, up_o, qkv_o, proj_o, vec_o = refs[16:23]
    ssem, rsem, lsem = refs[23 + len(shapes):]
    m = collections.namedtuple("Buffers", [s[0] for s in shapes])(*refs[23:23 + len(shapes)])

    w = Wire(
        ssem, rsem, lsem, ((32768, m.x_all, 16), (4096, m.sm, 1), (12288, m.wqkv, 16))
    )
    u, b = w.u, w.b
    z, c, zh = b // 2, b % 2, b // 4
    x, y = u % 2, u // 2
    rows, width = tok.shape
    group = 8 * rows
    pair = 2 * rows
    rank = x * 4 + b % 4
    mine_b = ds(b * rows, rows)
    own_rows = ds(0, rows)
    at = u * 8 + b
    send_barrier(u, b)
    l_q = w.here(wqkv_hbm, m.wqkv_in)
    l_tok = w.here(tok, m.x_all.at[mine_b])
    l_w = w.here(wup_hbm, m.wup_in)
    l_cot = w.here(cot, m.c_all.at[own_rows])
    m.par[at] = jnp.zeros((8, 128), F32)
    for row, v in enumerate((ln1_gain, ln1_bias, proj_bias, ln2_gain, ln2_bias, down_bias, qv_bias, up_bias_in)):
        m.par[at, row:row + 1, 0:v.shape[0]] = v[...].astype(F32).reshape(1, v.shape[0])
    l_q.wait()
    for r in range(8):
        for part in range(3):
            m.q_out[r, :, part * 128:(part + 1) * 128] = m.wqkv_in[
                :, part * width + r * 128:part * width + (r + 1) * 128
            ]
    wrow = ds(at * 32, 32)
    m.wqkv[wrow] = m.q_out[b]
    l_w.wait()
    for r in range(8):
        for ch in range(4):
            src = ((ch // 2) * 16 + (r // 4) * 8 + (ch % 2) * 4 + r % 4) * 128
            m.up_out[r, :, ch * 128:(ch + 1) * 128] = m.wup_in[:, src:src + 128]
    l_tok.wait()
    l_cot.wait()
    wait_barrier()

    q1 = Batch(w)
    for k in range(1, 8):
        w.blk(k, m.q_out.at[flip(b, k)], m.wqkv.at[wrow], batch=q1)
    p1 = Batch(w)
    for k in range(1, 8):
        w.blk(k, m.par.at[at], m.par.at[at], batch=p1)
    up_row = ds((b % 4) * 32, 32)
    pr1 = {k: w.blk(2 * k, wproj_in, m.wproj.at[u, z, c]) for k in (2, 1)}
    pr2 = Batch(w)
    for k in range(1, 4):
        w.uly(k, wproj_in, m.wproj.at[u, z, c], batch=pr2)

    def proj_on(k):
        pr1[k].wait_recv()
        slot = m.wproj.at[u, flip(z, k), c]
        for j in range(1, 4):
            w.uly(j, slot, slot, batch=pr2)

    slot = m.x_all.at[mine_b]
    t_z = {2: w.blk(4, slot, slot), 1: w.blk(2, slot, slot)}
    t_sib = w.blk(1, m.x_all.at[mine_b], m.x_all.at[mine_b])
    c_x = w.uly(1, m.c_all.at[own_rows], m.c_all.at[ds(2 * rows, rows)])
    d2 = [w.uly(2, wdown_in, m.wdown.at[c, y, zh])]
    w_sib = [w.blk(1, wdown_in, m.wdown.at[c, y, zh])]

    def to_sib(piece):
        w_sib.append(w.blk(1, piece, piece))

    l_up = w.here(m.up_out.at[rank], m.wup.at[c, u, zh, up_row])
    l_down = w.here(wdown_in, m.wdown.at[c, y, zh])
    l_proj = w.here(wproj_in, m.wproj.at[u, z, c])

    p1.wait_recv()
    mine = m.par.at[ds(u * 8, 8)]
    p2 = Batch(w)
    for k in range(1, 4):
        w.uly(k, mine, mine, batch=p2)
    q1.wait_recv()
    mine = m.wqkv.at[ds(u * 256, 256)]
    q2 = Batch(w)
    for k in range(1, 4):
        w.uly(k, mine, mine, batch=q2)
    proj_on(2)
    slot = m.wproj.at[u, flip(z, 2), c]
    pr1[3] = w.blk(2, slot, slot)
    proj_on(1)

    fwd = {}

    def to_sibling(k):
        slot = m.x_all.at[ds(flip(b, 2 * k) * rows, rows)]
        fwd[k] = w.blk(1, slot, slot)

    t_z[2].wait_recv()
    slot = m.x_all.at[ds(flip(b, 4) * rows, rows)]
    t_z[3] = w.blk(2, slot, slot)
    to_sibling(2)
    p2.wait_recv()
    for t in range(8):
        tiles = [pltpu.roll(m.par[4 * t + k], 32 * k, 1) if k else m.par[4 * t] for k in range(4)]
        m.vec[:, t * 128:(t + 1) * 128] = (tiles[0] + tiles[1]) + (tiles[2] + tiles[3])
    vec = m.vec
    q_bias = (m.par[2 * b] + pltpu.roll(m.par[2 * b + 1], 64, 1))[6:7]
    v_bias = (m.par[16 + 2 * b] + pltpu.roll(m.par[17 + 2 * b], 64, 1))[6:7]
    bias = jnp.concatenate([q_bias, jnp.zeros_like(q_bias), v_bias], axis=1)
    up_bias = [
        jnp.concatenate(
            [m.par[(ch // 2) * 16 + x * 8 + (ch % 2) * 4 + (b // 2) % 2 * 2 + core][7:8] for ch in range(4)], axis=1
        )
        for core in range(2)
    ]

    def normalize(zc):
        at = ds(zc * pair, pair)
        n, _ = norm_parts(m.x_all[at].astype(F32))
        m.n1[at] = (n * vec[0:1] + vec[1:2]).astype(BF)

    halo = w.take(4)
    halo_sent = w.take_send()

    def project(zc):
        at = ds(zc * pair, pair)
        out = (dot(m.n1[at], m.wqkv[...]) + bias).astype(BF)
        m.q[at] = out[:, :128]
        own = ds(group + zc * pair, pair)
        m.kv[own] = out[:, 128:]
        copy = w.make(m.kv.at[own], m.kv.at[at], (jnp.minimum(u + 1, 3), b), halo + zc, halo_sent)

        @pl.when(u < 3)
        def _():
            copy.start()

    t_sib.wait_recv()
    normalize(z)
    t_z[1].wait_recv()
    to_sibling(1)
    up1 = Batch(w)
    for k in range(1, 8):
        w.near(k // 4, k % 4, m.up_out.at[flip(rank, k)], m.wup.at[flip(c, k % 2), u, zh, up_row], batch=up1)
    proj_on(3)
    fwd[2].wait_recv()
    normalize(flip(z, 2))
    q2.wait_recv()
    project(z)
    project(flip(z, 2))
    fwd[1].wait_recv()
    normalize(flip(z, 1))
    project(flip(z, 1))
    t_z[3].wait_recv()
    to_sibling(3)
    c_z = w.blk(2, m.c_all.at[own_rows], m.c_all.at[ds(rows, rows)])
    d1 = w.blk(4, wdown_in, m.wdown.at[c, y, zh])
    d2[0].wait_recv()
    to_sib(m.wdown.at[c, 1 - y, zh])
    fwd[3].wait_recv()
    normalize(flip(z, 3))
    project(flip(z, 3))
    up1.wait_recv()
    l_up.wait()
    mine = m.wup.at[c, ds(y * 2, 2), zh]
    up2 = w.blk(4, mine, mine)
    up3 = [w.uly(2, mine, mine)]
    to_sib(mine)
    @pl.when(u == 0)
    def _():
        m.kv[0:group] = jnp.zeros((group, 256), BF)

    att_at = w.take(1)
    att_sent = w.take_send()

    def stretch(i, own):
        count = (i + 1) * pair if own else group - i * pair
        first = 0 if own else i * pair - group
        place = lax.broadcasted_iota(jnp.int32, (count, pair), 0) + first
        qpos = lax.broadcasted_iota(jnp.int32, (1, pair), 1) + i * pair
        allowed = place >= doc_begin(starts, qpos + u * group) - u * group
        if own:
            allowed = allowed & (place <= qpos)
        return slice(group + first, group + first + count), allowed, (place[:, :1] - i * pair).astype(F32)

    def one_head(rows_of, h):
        return jnp.where(head_mask((pair, 128), h), rows_of, jnp.zeros_like(rows_of))

    def scores(keys, query, h, place):
        return dot(keys, one_head(query, h), NT) * 0.125 + slopes[2 * b + h] * place

    def by_head(first, second):
        line = lax.broadcasted_iota(jnp.int32, (128, pair), 0)
        return jnp.where(line < 64, first, second)

    def attend_own(i):
        span, allowed, place = stretch(i, True)
        at = slice(i * pair, (i + 1) * pair)
        out = []
        for h in range(2):
            s = jnp.where(allowed, scores(m.kv[span, 0:128], m.q[at], h, place), -1e30)
            top = jnp.max(s, axis=0, keepdims=True)
            p = jnp.exp(s - top)
            m.row_max[h:h + 1, at] = top
            m.row_sum[h:h + 1, at] = jnp.sum(p, axis=0, keepdims=True)
            out.append(dot(m.kv[span, 128:256], p.astype(BF), TN))
        m.o_rows[:, at] = by_head(*out)

    def attend(i):
        @pl.when(u > 0)
        def _():
            w.make(
                m.kv.at[ds(i * pair, pair)], m.kv.at[ds(i * pair, pair)], (u, b), halo + i, halo_sent
            ).wait_recv()

        span, allowed, place = stretch(i, False)
        at = slice(i * pair, (i + 1) * pair)
        out, shrinks, inverses = [], [], []
        for h in range(2):
            s = jnp.where(allowed, scores(m.kv[span, 0:128], m.q[at], h, place), -1e30)
            old = m.row_max[h:h + 1, at]
            top = jnp.maximum(old, jnp.max(s, axis=0, keepdims=True))
            p = jnp.exp(s - top)
            shrink = jnp.exp(old - top)
            total = m.row_sum[h:h + 1, at] * shrink + jnp.sum(p, axis=0, keepdims=True)
            m.lse[h:h + 1, at] = top + jnp.log(total)
            out.append(dot(m.kv[span, 128:256], p.astype(BF), TN))
            shrinks.append(shrink)
            inverses.append(1.0 / total)
        mixed_rows = (m.o_rows[:, at] * by_head(*shrinks) + by_head(*out)) * by_head(*inverses)
        m.o_rows[:, at] = mixed_rows
        m.att_heads[at] = mixed_rows.T.astype(BF)
        for half in range(2):
            target = 2 * i + half
            piece = m.att_heads.at[ds(target * rows, rows)]

            @pl.when(target != b)
            def _():
                w.make(piece, m.att_in.at[b], (u, target), att_at, att_sent).start()

    for i in range(4):
        attend_own(i)
    attend(3)
    l_proj.wait()
    pr2.wait_recv()
    mine = m.wproj.at[:, :, c]
    pr3 = w.blk(1, mine, mine)
    attend(2)
    d1.wait_recv()
    slot = m.wdown.at[c, y, 1 - zh]
    d2.append(w.uly(2, slot, slot))
    to_sib(slot)
    c_z.wait_recv()
    c_zx = w.uly(1, m.c_all.at[ds(rows, rows)], m.c_all.at[ds(3 * rows, rows)])
    up3[0].wait_recv()
    to_sib(m.wup.at[c, ds((1 - y) * 2, 2), zh])
    attend(1)
    attend(0)
    m.att_in[b] = m.att_heads[mine_b]
    cot_f = m.c_all[own_rows].astype(F32)
    down_bias_sum = jnp.sum(cot_f, axis=0, keepdims=True)
    up2.wait_recv()
    mine = m.wup.at[c, ds(y * 2, 2), 1 - zh]
    up3.append(w.uly(2, mine, mine))
    to_sib(mine)
    att_bytes = 7 * w.size_of(m.att_in.at[0])
    w.await_bytes(w.rsem.at[att_at], att_bytes)
    w.await_bytes(w.ssem.at[att_sent], att_bytes)
    pr3.wait_recv()

    wproj = m.wproj[...].reshape(width, width)
    for r in range(8):
        m.att[:, r * 128:(r + 1) * 128] = m.att_in[r]
    mixed = m.x_all[mine_b].astype(F32) + dot(m.att[...], wproj) + vec[2:3]
    m.mixed[...] = mixed
    n2, inv2 = norm_parts(mixed)
    m.n2_all[own_rows] = (n2 * vec[3:4] + vec[4:5]).astype(BF)
    half_rows = rows // 2
    top, low = ds(0, half_rows), ds(half_rows, half_rows)

    def halves(owner, h):
        return m.n2_all.at[ds(owner * rows + h * half_rows, half_rows)]

    n_z = [w.blk(2, halves(0, 0), halves(1, 0))]
    n_x = [w.uly(1, halves(0, 1), halves(2, 1))]
    n_z.append(w.blk(2, halves(0, 1), halves(1, 1)))
    n_x.append(w.uly(1, halves(0, 0), halves(2, 0)))
    d2[1].wait_recv()
    to_sib(m.wdown.at[c, 1 - y, 1 - zh])
    up3[1].wait_recv()
    to_sib(m.wup.at[c, ds((1 - y) * 2, 2), 1 - zh])
    l_down.wait()
    hidden = m.act.shape[2]

    def feed(first, count):
        at = ds(first * rows, count * rows)
        out = g2 = 0.0
        for core in range(2):
            up = dot(m.n2_all[at], m.wup[core].reshape(width, hidden)) + up_bias[core]
            square = up * up
            th = jnp.tanh(0.7978845608028654 * (up + 0.044715 * square * up))
            act = (0.5 * up * (1.0 + th)).astype(BF)
            slope = 0.5 * (1.0 + th) + 0.5 * up * (1.0 - th * th) * (
                0.7978845608028654 * (1.0 + 3.0 * 0.044715 * square)
            )
            gup = (dot(m.c_all[at], m.wdown[core].reshape(hidden, width), NT) * slope).astype(BF)
            m.act[core, at] = act
            m.gup[core, at] = gup
            g2 = g2 + dot(gup, m.wup[core].reshape(width, hidden), NT)
            out = out + dot(act, m.wdown[core].reshape(hidden, width))
        m.g2_part[at] = g2.astype(BF)
        m.out_part[at] = out.astype(BF)

    hops = ((0, 2), (1, 0), (1, 2))
    g2_sends = []

    def return_g2(i):
        ku, kb = hops[i]
        far = ku * 2 + kb // 2
        g2_sends.append(w.near(ku, kb, m.g2_part.at[ds(far * rows, rows)], m.g2_far.at[i]))

    for copy in w_sib:
        copy.wait_recv()
    feed(0, 1)
    n_z[0].wait_recv()
    n_diag = [w.uly(1, halves(1, 0), halves(3, 0))]
    n_x[0].wait_recv()
    n_diag.append(w.blk(2, halves(2, 1), halves(3, 1)))
    n_z[1].wait_recv()
    n_x[1].wait_recv()
    c_x.wait_recv()
    feed(1, 2)
    return_g2(0)
    return_g2(1)
    for copy in n_diag:
        copy.wait_recv()
    c_zx.wait_recv()
    feed(3, 1)
    return_g2(2)
    other = 1 - c
    m.dwn_out[...] = dot(m.act[other], m.c_all[...], TN).astype(BF).reshape(2, 2, rows, width)
    s_dwn = w.blk(1, m.dwn_out, m.dwn_sib)
    m.dwn[...] = dot(m.act[c], m.c_all[...], TN).astype(BF).reshape(2, 2, rows, width)
    m.dup_out[...] = dot(m.n2_all[...], m.gup[other], TN).astype(BF).reshape(4, 2, 128, hidden)
    s_dup = w.blk(1, m.dup_out, m.dup_sib)
    others = ds((1 - y) * 2, 2)
    s_dwn.wait_recv()
    m.dwn[...] = (m.dwn[...].astype(F32) + m.dwn_sib[...].astype(F32)).astype(BF)
    y_dwn = [w.uly(2, m.dwn.at[1 - y, 1 - zh], m.dwn_y.at[1 - zh])]
    m.dup[...] = dot(m.n2_all[...], m.gup[c], TN).astype(BF).reshape(4, 2, 128, hidden)
    s_dup.wait_recv()
    m.dup[...] = (m.dup[...].astype(F32) + m.dup_sib[...].astype(F32)).astype(BF)
    y_dup = [w.uly(2, m.dup.at[others, 1 - zh], m.dup_y.at[:, 1 - zh])]
    y_dwn.append(w.uly(2, m.dwn.at[1 - y, zh], m.dwn_y.at[zh]))
    y_dup.append(w.uly(2, m.dup.at[others, zh], m.dup_y.at[:, zh]))
    up_bias_sums = [jnp.sum(m.gup[core].astype(F32), axis=0, keepdims=True) for core in range(2)]
    def out_rows(mask, part):
        return m.out_part.at[ds(mask * rows + part * half_rows, half_rows)]

    out_via = w.uly(1, out_rows(3, 1), m.out_via.at[1])
    out_sends = [w.uly(1, out_rows(2, 1), m.out_far.at[1, low])]
    g = m.g2_part[own_rows].astype(F32)
    for i in range(3):
        g2_sends[i].wait_recv()
        g = g + m.g2_far[i].astype(F32)
    ln2_gain_sum = jnp.sum(g * n2, axis=0, keepdims=True)
    ln2_bias_sum = jnp.sum(g, axis=0, keepdims=True)
    e = g * vec[3:4]
    gmix = cot_f + inv2 * (
        e - jnp.mean(e, axis=-1, keepdims=True) - n2 * jnp.mean(e * n2, axis=-1, keepdims=True)
    )
    m.gmix[...] = gmix
    proj_bias_sum = jnp.sum(gmix, axis=0, keepdims=True)
    gbr = gmix.astype(BF)
    m.gbr[...] = gbr
    gatt = dot(gbr, wproj, NT).astype(BF)
    for r in range(8):
        m.gatt[r] = gatt[:, r * 128:(r + 1) * 128]

    g_to = w.take(8)
    g_sent = w.take_send()
    for k in range(1, 8):
        other = flip(b, k)
        w.make(m.gatt.at[other], m.gh.at[mine_b], (u, other), g_to + b, g_sent).start()
    m.gh[mine_b] = m.gatt[b]
    out_via = [w.blk(2, out_rows(3, 0), m.out_via.at[0]), out_via]
    out_sends.append(w.blk(2, out_rows(1, 0), m.out_far.at[0, top]))
    for j in range(4):
        m.dpr[j] = dot(m.att[:, j * 256:(j + 1) * 256], gbr, TN).astype(BF).reshape(4, 2, 32, width)
    pg1 = w.blk(1, m.dpr.at[:, :, 1 - c], m.dpr_sib)
    m.dkv[...] = jnp.zeros_like(m.dkv)
    back = w.take(4)
    back_sent = w.take_send()

    def hand_back(i):
        at = ds(i * pair, pair)
        return w.make(m.halo_out.at[at], m.halo_in.at[at], (jnp.maximum(u - 1, 0), b), back + i, back_sent)

    def gradients(i, own):
        span, allowed, place = stretch(i, own)
        at = slice(i * pair, (i + 1) * pair)
        keys, vals = m.kv[span, 0:128], m.kv[span, 128:256]
        dk = dv = 0.0
        dq = []
        for h in range(2):
            gr = one_head(m.gh[at], h)
            s = scores(keys, m.q[at], h, place)
            p = jnp.where(allowed, jnp.exp(s - m.lse[h:h + 1, at]), 0.0)
            gs = (p * (dot(vals, gr, NT) - m.delta[h:h + 1, at])).astype(BF)
            dv = dv + dot(p.astype(BF), gr)
            dk = dk + dot(gs, one_head(m.q[at], h))
            dq.append(dot(keys, gs, TN))
        m.dkv[span, 0:128] += dk
        m.dkv[span, 128:256] += dv
        return by_head(*dq)

    def attend_back(i):
        for half in range(2):
            source = 2 * i + half

            @pl.when(source != b)
            def _():
                w.make(
                    m.gatt.at[b], m.gh.at[ds(source * rows, rows)], (u, b), g_to + source, g_sent
                ).wait_recv()

        at = slice(i * pair, (i + 1) * pair)
        products = m.gh[at].astype(F32).T * m.o_rows[:, at]
        m.delta[0:1, at] = jnp.sum(products[:64], axis=0, keepdims=True)
        m.delta[1:2, at] = jnp.sum(products[64:], axis=0, keepdims=True)
        m.dq_rows[:, at] = gradients(i, False)
        m.halo_out[at] = m.dkv[at].astype(BF)

        @pl.when(u > 0)
        def _():
            hand_back(i).start()

    class Fold:
        def __init__(self, part, via, far):
            self.part, self.via, self.far = part, via, far
            self.first = [w.uly(1, part(3, 0), via.at[0]), w.uly(2, part(3, 1), via.at[1])]
            self.all = [w.uly(1, part(1, 0), far.at[0, 0]), w.uly(2, part(2, 1), far.at[1, 1])]

        def second(self):
            for h, mask in enumerate((2, 1)):
                self.first[h].wait_recv()
                ref = self.part(mask, h)
                ref[...] = (ref[...].astype(F32) + self.via[h].astype(F32)).astype(BF)
                self.all.append(w.uly(mask, ref, self.far.at[mask - 1, h]))

        def total(self):
            for copy in self.all:
                copy.wait_recv()
            return [
                self.part(0, h)[...].astype(F32) + (self.far[0, h].astype(F32) + self.far[1, h].astype(F32))
                for h in range(2)
            ]

    attend_back(0)
    y_dwn[0].wait_recv()
    m.dwn_keep[...] = (m.dwn[y, 1 - zh].astype(F32) + m.dwn_y[1 - zh].astype(F32)).astype(BF)
    z1 = [w.blk(4, m.dwn_keep, m.dwn_z)]
    attend_back(1)
    attend_back(2)
    attend_back(3)
    for h, mask in enumerate((2, 1)):
        out_via[h].wait_recv()
        at = ds(mask * rows + h * half_rows, half_rows)
        m.out_part[at] = (m.out_part[at].astype(F32) + m.out_via[h].astype(F32)).astype(BF)
    out_sends += [w.uly(1, out_rows(2, 0), m.out_far.at[1, top]), w.blk(2, out_rows(1, 1), m.out_far.at[0, low])]
    y_dup[0].wait_recv()
    m.dup_keep[...] = (m.dup[ds(y * 2, 2), 1 - zh].astype(F32) + m.dup_y[:, 1 - zh].astype(F32)).astype(BF)
    z2 = w.blk(4, m.dup_keep, m.dup_z)
    for i in range(4):
        at = slice(i * pair, (i + 1) * pair)
        m.gqkv[at, 0:128] = ((m.dq_rows[:, at] + gradients(i, True)).T * 0.125).astype(BF)
    def complete(i):
        @pl.when(u < 3)
        def _():
            at = ds(i * pair, pair)
            own = ds(group + i * pair, pair)
            w.make(m.halo_out.at[at], m.halo_in.at[at], (u, b), back + i, back_sent).wait_recv()
            m.dkv[own] += m.halo_in[at].astype(F32)

        at = ds(i * pair, pair)
        own = ds(group + i * pair, pair)
        m.gqkv[at, 128:256] = (m.dkv[own, 0:128] * 0.125).astype(BF)
        m.gqkv[at, 256:384] = m.dkv[own, 128:256].astype(BF)

    swaps1 = {}

    def spread(k):
        chip = flip(z, k)
        complete(chip)
        at = ds(chip * pair, pair)
        m.g1_part[at] = dot(m.gqkv[at], m.wqkv[...], NT).astype(BF)
        other = ds(chip * pair + (1 - c) * rows, rows)
        swaps1[k] = w.blk(1, m.g1_part.at[other], m.g1_sib.at[k])

    def chip_sum(k):
        own = ds(flip(z, k) * pair + c * rows, rows)
        swaps1[k].wait_recv()
        return m.g1_part[own].astype(F32) + m.g1_sib[k].astype(F32)

    spread(3)
    n, inv = norm_parts(m.x_all[mine_b].astype(F32))
    m.g1_keep[2] = chip_sum(3).astype(BF)
    via = [w.blk(2, m.g1_keep.at[2, part], m.g1_far.at[2, part]) for part in (top, low)]
    spread(1)
    pg1.wait_recv()
    m.dpr_keep[...] = (m.dpr[:, :, c].astype(F32) + m.dpr_sib[...].astype(F32)).astype(BF)
    pg2 = Fold(lambda mask, h: m.dpr_keep.at[flip(u, mask), ds(2 * h, 2)], m.dpr_via, m.dpr_u)
    spread(2)
    spread(0)
    m.dq[...] = dot(m.n1[...], m.gqkv[...], TN).astype(BF)
    q2g = Fold(lambda mask, h: m.dq.at[ds(flip(u, mask) * 256 + h * 128, 128)], m.dq_via, m.dq_u)
    gain_sum = bias_sum = 0.0
    for i in range(4):
        at = slice(i * pair, (i + 1) * pair)
        part = m.g1_part[at].astype(F32)
        bias_sum = bias_sum + jnp.sum(part, axis=0, keepdims=True)
        gain_sum = gain_sum + jnp.sum(part * norm_parts(m.x_all[at].astype(F32))[0], axis=0, keepdims=True)
    qv_sums = jnp.sum(m.gqkv[...].astype(F32), axis=0, keepdims=True)
    lines = jnp.concatenate(
        [gain_sum, bias_sum, proj_bias_sum, ln2_gain_sum, ln2_bias_sum, down_bias_sum, jnp.zeros((2, width), F32)],
        axis=0,
    )
    for d in range(32):
        m.sm[d] = lines[:, (d // 4) * 128:(d // 4 + 1) * 128]
    for at, line in ((2 * b, qv_sums[:, 0:128]), (16 + 2 * b, qv_sums[:, 256:384])):
        m.sm[at, 6:7] = line
        m.sm[at + 1, 6:7] = line
    for core in range(2):
        for ch in range(4):
            at = (ch // 2) * 16 + x * 8 + (ch % 2) * 4 + (b // 2) % 2 * 2 + core
            m.sm[at, 7:8] = up_bias_sums[core][:, ch * 128:(ch + 1) * 128]
    s1 = Batch(w)
    for k in range(1, 4):
        w.uly(k, m.sm.at[ds(flip(u, k) * 8, 8)], m.sm_u.at[k - 1], batch=s1)
    pg2.second()
    sum2 = chip_sum(2)
    g1_cross = []
    def cross(h):
        part = (top, low)[h]
        via[h].wait_recv()
        m.g1_keep[1, part] = (
            sum2[h * half_rows:(h + 1) * half_rows] + m.g1_far[2, part].astype(F32)
        ).astype(BF)
        g1_cross.append(w.blk(4, m.g1_keep.at[1, part], m.g1_far.at[1, part]))

    cross(0)
    q2g.second()
    cross(1)
    m.g1_keep[0] = chip_sum(1).astype(BF)
    g1_near = w.blk(2, m.g1_keep.at[0], m.g1_far.at[0])

    s1.wait_recv()
    m.sm_keep[...] = (m.sm[ds(u * 8, 8)] + m.sm_u[0]) + (m.sm_u[1] + m.sm_u[2])
    s2 = Batch(w)
    for k in range(1, 8):
        w.blk(k, m.sm_keep.at[flip(b, k)], m.sm_b.at[k - 1], batch=s2)
    for copy in z1:
        copy.wait_recv()
    y_dwn[1].wait_recv()
    down_o[...] = (m.dwn[y, zh].astype(F32) + m.dwn_y[zh].astype(F32)) + m.dwn_z[...].astype(F32)
    z2.wait_recv()
    y_dup[1].wait_recv()
    m.dup_own[...] = (
        (m.dup[ds(y * 2, 2), zh].astype(F32) + m.dup_y[:, zh].astype(F32)) + m.dup_z[...].astype(F32)
    ).astype(BF).reshape(8, 32, hidden)
    up3g = Batch(w)
    for k in range(1, 8):
        w.near(k // 4, k % 4, m.dup_own.at[flip(rank, k)], up_o.at[rank], batch=up3g)
    up_o[rank] = m.dup_own[rank]
    out = m.mixed[...] + vec[5:6] + m.out_part[own_rows].astype(F32)
    for copy in out_sends:
        copy.wait_recv()
    for i in range(2):
        out = out + m.out_far[i].astype(F32)
    out_o[...] = out.astype(BF)
    for h, total in enumerate(pg2.total()):
        m.dpr_own[2 * h:2 * h + 2] = total.astype(BF)
    pg3 = Batch(w)
    for k in range(1, 4):
        w.blk(2 * k, m.dpr_own.at[flip(z, k)], m.dpr_z.at[k - 1], batch=pg3)
    for h, total in enumerate(q2g.total()):
        m.dq_own[4 * h:4 * h + 4] = total.astype(BF).reshape(4, 32, 384)
    q3g = Batch(w)
    for k in range(1, 8):
        w.blk(k, m.dq_own.at[flip(b, k)], qkv_o.at[b], batch=q3g)
    qkv_o[b] = m.dq_own[b]

    g = chip_sum(0)
    g1_near.wait_recv()
    for copy in g1_cross:
        copy.wait_recv()
    g = g + m.g1_far[0].astype(F32) + m.g1_far[1].astype(F32)
    e = g * vec[0:1]
    in_o[...] = (
        m.gmix[...]
        + inv * (e - jnp.mean(e, axis=-1, keepdims=True) - n * jnp.mean(e * n, axis=-1, keepdims=True))
    ).astype(BF)
    pg3.wait_recv()
    proj_o[...] = (m.dpr_own[z].astype(F32) + m.dpr_z[0].astype(F32)) + (
        m.dpr_z[1].astype(F32) + m.dpr_z[2].astype(F32)
    )
    for batch in (up3g, q3g, s2):
        batch.wait_recv()
    total = m.sm_keep[b]
    for k in range(7):
        total = total + m.sm_b[k]
    line = lax.broadcasted_iota(jnp.int32, (8, 128), 0)
    by32 = pltpu.roll(total, (128 - 32 * (b % 4)) % 128, 1)
    by64 = pltpu.roll(total, (128 - 64 * (b % 2)) % 128, 1)
    vec_o[...] = jnp.where(line < 6, by32, jnp.where(line == 6, by64, total))

    w.await_bytes(w.ssem.at[g_sent], 7 * w.size_of(m.gatt.at[0]))

    @pl.when(u < 3)
    def _():
        w.await_bytes(w.ssem.at[halo_sent], w.size_of(m.halo_in))

    @pl.when(u > 0)
    def _():
        w.await_bytes(w.ssem.at[back_sent], w.size_of(m.halo_in))

    w.finish()


def finish_kernel(
    out, grad_in, down, up, qkv, proj, vec,
    out_o, in_o, g1_o, b1_o, qkv_o, qv_o, proj_o, pb_o, g2_o, b2_o, up_o, ub_o, down_o, db_o,
):
    out_o[...] = out[...]
    in_o[...] = grad_in[...]
    down_o[...] = down[...]
    proj_o[...] = proj[...]
    for r in range(8):
        for ch in range(4):
            to = ((ch // 2) * 16 + (r // 4) * 8 + (ch % 2) * 4 + r % 4) * 128
            up_o[:, to:to + 128] = up[r, :, ch * 128:(ch + 1) * 128].astype(F32)
        for part in range(3):
            to = part * 1024 + r * 128
            qkv_o[:, to:to + 128] = qkv[r, :, part * 128:(part + 1) * 128].astype(F32)
    for row, ref in enumerate((g1_o, b1_o, pb_o, g2_o, b2_o, db_o, qv_o, ub_o)):
        ref[...] = vec[row, 0:ref.shape[0]]


def fast_body(
    tokens, ln1_gain, ln1_bias, qkv_weight, qv_bias, proj_weight, proj_bias, ln2_gain, ln2_bias,
    up_weight, up_bias, down_weight, down_bias, alibi_slopes, doc_starts, cotangent,
):
    rows, width = tokens.shape
    shapes = buffer_shapes(rows, width, 512, 128)
    v = pl.BlockSpec(memory_space=pltpu.VMEM)
    s = pl.BlockSpec(memory_space=pltpu.SMEM)
    sds = jax.ShapeDtypeStruct
    a = pl.BlockSpec(memory_space=pl.ANY)
    parts = pl.pallas_call(
        functools.partial(block_kernel, shapes),
        name="transformer_block",
        out_shape=(
            sds((rows, width), BF),
            sds((rows, width), BF),
            sds((rows, width), F32),
            sds((8, 32, 512), BF),
            sds((8, 32, 384), BF),
            sds((32, width), F32),
            sds((8, 128), F32),
        ),
        in_specs=[a] * 6 + [v] * 8 + [s, s],
        out_specs=(v,) * 7,
        scratch_shapes=[pltpu.VMEM(shape, kind) for _, shape, kind in shapes]
        + [
            pltpu.SemaphoreType.DMA((SENDS,)),
            pltpu.SemaphoreType.DMA((RECEIVES,)),
            pltpu.SemaphoreType.DMA((7,)),
        ],
        compiler_params=pltpu.CompilerParams(
            collective_id=0, has_side_effects=True, vmem_limit_bytes=VMEM_LIMIT
        ),
    )(
        tokens, qkv_weight, proj_weight, up_weight, down_weight, cotangent,
        ln1_gain, ln1_bias, proj_bias, ln2_gain, ln2_bias, down_bias, qv_bias, up_bias,
        alibi_slopes, doc_starts,
    )
    vector = sds((32,), F32)
    return pl.pallas_call(
        finish_kernel,
        name="lay_out",
        out_shape=(
            sds((rows, width), BF), sds((rows, width), BF), vector, vector, sds((32, 3072), F32),
            sds((64,), F32), sds((32, width), F32), vector, vector, vector, sds((32, 4096), F32),
            sds((128,), F32), sds((rows, width), F32), vector,
        ),
        in_specs=[v] * 7,
        out_specs=(v,) * 14,
        compiler_params=pltpu.CompilerParams(vmem_limit_bytes=VMEM_LIMIT),
    )(*parts)


HEADS = 16
HEAD_DIM = 64


def layer_norm(values, norm_gain, norm_shift):
    center = jnp.mean(values, axis=-1, keepdims=True)
    offset = values - center
    spread = jnp.mean(offset * offset, axis=-1, keepdims=True)
    return offset * lax.rsqrt(spread + 1e-05) * norm_gain + norm_shift


def gelu_tanh(values):
    return (
        0.5
        * values
        * (1.0 + jnp.tanh(0.7978845608028654 * (values + 0.044715 * values * values * values)))
    )


def place_rows(local_rows, team_size, blk_count, tok_rows):
    team_span = team_size * tok_rows
    return (
        local_rows % team_span // tok_rows * blk_count + local_rows // team_span
    ) * tok_rows + local_rows % tok_rows


def doc_index(positions, doc_starts):
    return jnp.sum((positions[:, None] >= doc_starts[None, :]).astype(jnp.int32), axis=1) - 1


def split_rows(row_count, step_rows):
    return (row_count // step_rows, step_rows)


def score_block(queries, keys, query_pos, key_pos, query_doc, key_doc, slopes):
    raw_scores = jnp.einsum(
        "qhd,khd->hqk", queries, keys, preferred_element_type=jnp.float32
    ) * HEAD_DIM ** (-0.5)
    distance = (query_pos[:, None] - key_pos[None, :]).astype(jnp.float32)
    raw_scores = raw_scores - slopes[:, None, None] * distance[None]
    allowed = (key_pos[None, :] <= query_pos[:, None]) & (query_doc[:, None] == key_doc[None, :])
    return (jnp.where(allowed[None], raw_scores, -1e30), allowed[None])


def general_body(
    tokens,
    ln1_gain,
    ln1_bias,
    qkv_weight,
    qv_bias,
    proj_weight,
    proj_bias,
    ln2_gain,
    ln2_bias,
    up_weight,
    up_bias,
    down_weight,
    down_bias,
    alibi_slopes,
    doc_starts,
    cotangent,
):
    team_size = lax.axis_size("ulysses")
    blk_count = lax.axis_size("blk")
    tok_rows = tokens.shape[0]
    width_all = tokens.shape[1]
    head_rows = team_size * tok_rows
    heads_here = HEADS // team_size
    features = heads_here * HEAD_DIM
    scale_factor = HEAD_DIM ** (-0.5)
    gathered = (
        lax.all_gather(ln1_gain, ("ulysses", "blk"), axis=0, tiled=True),
        lax.all_gather(ln1_bias, ("ulysses", "blk"), axis=0, tiled=True),
        lax.all_gather(qkv_weight, ("ulysses", "blk"), axis=0, tiled=True),
        lax.all_gather(qv_bias, ("ulysses", "blk"), axis=0, tiled=True),
        lax.all_gather(proj_weight, ("ulysses", "blk"), axis=0, tiled=True),
        lax.all_gather(proj_bias, ("ulysses", "blk"), axis=0, tiled=True),
        lax.all_gather(ln2_gain, ("ulysses", "blk"), axis=0, tiled=True),
        lax.all_gather(ln2_bias, ("ulysses", "blk"), axis=0, tiled=True),
        lax.all_gather(up_weight, ("ulysses", "blk"), axis=0, tiled=True),
        lax.all_gather(up_bias, ("ulysses", "blk"), axis=0, tiled=True),
        lax.all_gather(down_weight, ("ulysses", "blk"), axis=0, tiled=True),
        lax.all_gather(down_bias, ("ulysses", "blk"), axis=0, tiled=True),
    )
    gain_one = gathered[0].astype(jnp.float32)
    shift_one = gathered[1].astype(jnp.float32)
    qkv_proj = gathered[2]
    qv_shift = gathered[3].astype(jnp.float32)
    proj_mat = gathered[4]
    proj_shift = gathered[5].astype(jnp.float32)
    gain_two = gathered[6].astype(jnp.float32)
    shift_two = gathered[7].astype(jnp.float32)
    up_mat = gathered[8]
    up_shift = gathered[9].astype(jnp.float32)
    down_mat = gathered[10]
    down_shift = gathered[11].astype(jnp.float32)
    inputs_f = tokens.astype(jnp.float32)
    normed_one = layer_norm(inputs_f, gain_one, shift_one).astype(jnp.bfloat16)
    joined_bias = jnp.concatenate(
        [qv_shift[:width_all], jnp.zeros((width_all,), jnp.float32), qv_shift[width_all:]]
    )
    joined = (
        jnp.dot(normed_one, qkv_proj, preferred_element_type=jnp.float32) + joined_bias
    ).astype(jnp.bfloat16)
    head_local = lax.all_to_all(
        joined.reshape(tok_rows, 3, team_size, features),
        "ulysses",
        split_axis=2,
        concat_axis=0,
        tiled=True,
    )
    queries_flat = head_local[:, 0, 0]
    queries = queries_flat.reshape(head_rows, heads_here, HEAD_DIM)
    key_value = head_local[:, 1:, 0]
    own_keys = key_value[:, 0].reshape(head_rows, heads_here, HEAD_DIM)
    own_values = key_value[:, 1].reshape(head_rows, heads_here, HEAD_DIM)
    slopes = lax.dynamic_slice_in_dim(
        alibi_slopes, lax.axis_index("ulysses") * heads_here, heads_here, 0
    )
    own_rows = lax.axis_index("blk") * head_rows + jnp.arange(head_rows, dtype=jnp.int32)
    own_pos = place_rows(own_rows, team_size, blk_count, tok_rows)
    own_doc = doc_index(own_pos, doc_starts)
    start_state = (
        jnp.full((heads_here, head_rows), -1e30, jnp.float32),
        jnp.zeros((heads_here, head_rows), jnp.float32),
        jnp.zeros((heads_here, head_rows, HEAD_DIM), jnp.float32),
    )
    carried = start_state
    piece_rows = lax.all_gather(key_value, "blk", axis=0, tiled=True)
    number, step_rows = split_rows(piece_rows.shape[0], head_rows)
    stacked = piece_rows.reshape(number, step_rows, 2, heads_here, HEAD_DIM)
    offsets = step_rows * jnp.arange(number, dtype=jnp.int32)

    def online_step(running, inputs_pair):
        best_now, norm_sum, accumulated = running
        kv_block, offset_now = inputs_pair
        key_pos = place_rows(
            offset_now + jnp.arange(step_rows, dtype=jnp.int32), team_size, blk_count, tok_rows
        )
        key_doc = doc_index(key_pos, doc_starts)
        masked, allowed = score_block(
            queries, kv_block[:, 0], own_pos, key_pos, own_doc, key_doc, slopes
        )
        best_next = jnp.maximum(best_now, jnp.max(masked, axis=-1))
        weights = jnp.where(allowed, jnp.exp(masked - best_next[..., None]), 0.0)
        shrink = jnp.exp(best_now - best_next)
        norm_sum = norm_sum * shrink + jnp.sum(weights, axis=-1)
        accumulated = accumulated * shrink[..., None] + jnp.einsum(
            "hqk,khd->hqd",
            weights.astype(jnp.bfloat16),
            kv_block[:, 1],
            preferred_element_type=jnp.float32,
        )
        return ((best_next, norm_sum, accumulated), None)

    carried, _ = lax.scan(online_step, carried, (stacked, offsets))
    best_all, norm_all, acc_all = carried
    attended_heads = acc_all / norm_all[..., None]
    log_norm = best_all + jnp.log(norm_all)
    attended_rows = (
        attended_heads.transpose(1, 0, 2).reshape(head_rows, 1, features).astype(jnp.bfloat16)
    )
    attended = lax.all_to_all(
        attended_rows, "ulysses", split_axis=0, concat_axis=1, tiled=True
    ).reshape(tok_rows, width_all)
    mixed = inputs_f + jnp.dot(attended, proj_mat, preferred_element_type=jnp.float32) + proj_shift
    normed_two = layer_norm(mixed, gain_two, shift_two).astype(jnp.bfloat16)
    up_values = jnp.dot(normed_two, up_mat, preferred_element_type=jnp.float32) + up_shift
    activated = gelu_tanh(up_values).astype(jnp.bfloat16)
    output = (
        mixed + jnp.dot(activated, down_mat, preferred_element_type=jnp.float32) + down_shift
    ).astype(jnp.bfloat16)
    contract_rows = (((0,), (0,)), ((), ()))
    contract_cols = (((1,), (1,)), ((), ()))
    grad_out = cotangent.astype(jnp.float32)
    down_grad = lax.dot_general(
        activated, cotangent, contract_rows, preferred_element_type=jnp.float32
    )
    down_bias_grad = jnp.sum(grad_out, axis=0)
    grad_act = lax.dot_general(
        cotangent, down_mat, contract_cols, preferred_element_type=jnp.float32
    )
    _, gelu_pull = jax.vjp(gelu_tanh, up_values)
    grad_up = gelu_pull(grad_act)[0].astype(jnp.bfloat16)
    up_grad = lax.dot_general(
        normed_two, grad_up, contract_rows, preferred_element_type=jnp.float32
    )
    up_bias_grad = jnp.sum(grad_up.astype(jnp.float32), axis=0)
    grad_norm_two = lax.dot_general(
        grad_up, up_mat, contract_cols, preferred_element_type=jnp.float32
    )
    _, norm_two_pull = jax.vjp(layer_norm, mixed, gain_two, shift_two)
    grad_mixed_part, ln2_gain_grad, ln2_bias_grad = norm_two_pull(grad_norm_two)
    grad_mixed = grad_out + grad_mixed_part
    grad_branch = grad_mixed.astype(jnp.bfloat16)
    proj_grad = lax.dot_general(
        attended, grad_branch, contract_rows, preferred_element_type=jnp.float32
    )
    proj_bias_grad = jnp.sum(grad_mixed, axis=0)
    grad_att = lax.dot_general(
        grad_branch, proj_mat, contract_cols, preferred_element_type=jnp.float32
    ).astype(jnp.bfloat16)
    grad_heads = lax.all_to_all(
        grad_att.reshape(tok_rows, team_size, features),
        "ulysses",
        split_axis=1,
        concat_axis=0,
        tiled=True,
    )
    grad_heads_flat = grad_heads[:, 0]
    grad_att_heads = grad_heads_flat.reshape(head_rows, heads_here, HEAD_DIM)
    delta = jnp.sum(grad_att_heads.astype(jnp.float32).transpose(1, 0, 2) * attended_heads, axis=-1)
    carried = jnp.zeros((heads_here, head_rows, HEAD_DIM), jnp.float32)
    piece_rows = lax.all_gather(key_value, "blk", axis=0, tiled=True)
    number, query_step_rows = split_rows(piece_rows.shape[0], head_rows)
    stacked = piece_rows.reshape(number, query_step_rows, 2, heads_here, HEAD_DIM)
    offsets = query_step_rows * jnp.arange(number, dtype=jnp.int32)

    def query_step(running, inputs_pair):
        kv_block, offset_now = inputs_pair
        key_pos = place_rows(
            offset_now + jnp.arange(query_step_rows, dtype=jnp.int32),
            team_size,
            blk_count,
            tok_rows,
        )
        key_doc = doc_index(key_pos, doc_starts)
        masked, allowed = score_block(
            queries, kv_block[:, 0], own_pos, key_pos, own_doc, key_doc, slopes
        )
        probs = jnp.where(allowed, jnp.exp(masked - log_norm[..., None]), 0.0)
        grad_probs = jnp.einsum(
            "qhd,khd->hqk", grad_att_heads, kv_block[:, 1], preferred_element_type=jnp.float32
        )
        grad_scores = (probs * (grad_probs - delta[..., None])).astype(jnp.bfloat16)
        running = running + jnp.einsum(
            "hqk,khd->hqd", grad_scores, kv_block[:, 0], preferred_element_type=jnp.float32
        )
        return (running, None)

    carried, _ = lax.scan(query_step, carried, (stacked, offsets))
    grad_queries = carried * scale_factor
    all_norms, all_deltas = (
        lax.all_gather(log_norm.T, "blk", axis=0, tiled=True),
        lax.all_gather(delta.T, "blk", axis=0, tiled=True),
    )
    empty_keys = jnp.zeros((head_rows, heads_here, HEAD_DIM), jnp.float32)
    carried = (empty_keys, empty_keys)
    pieces = (
        lax.all_gather(queries_flat, "blk", axis=0, tiled=True),
        lax.all_gather(grad_heads_flat, "blk", axis=0, tiled=True),
    )
    number, key_step_rows = split_rows(pieces[0].shape[0], head_rows)
    query_stack = pieces[0].reshape(number, key_step_rows, heads_here, HEAD_DIM)
    grad_stack = pieces[1].reshape(number, key_step_rows, heads_here, HEAD_DIM)
    offsets = key_step_rows * jnp.arange(number, dtype=jnp.int32)

    def key_step(running, inputs_triple):
        grad_keys_now, grad_values_now = running
        query_block, grad_block, offset_now = inputs_triple
        query_pos = place_rows(
            offset_now + jnp.arange(key_step_rows, dtype=jnp.int32), team_size, blk_count, tok_rows
        )
        query_doc = doc_index(query_pos, doc_starts)
        norm_block = lax.dynamic_slice_in_dim(all_norms, offset_now, key_step_rows, 0).T
        delta_block = lax.dynamic_slice_in_dim(all_deltas, offset_now, key_step_rows, 0).T
        masked, allowed = score_block(
            query_block, own_keys, query_pos, own_pos, query_doc, own_doc, slopes
        )
        probs = jnp.where(allowed, jnp.exp(masked - norm_block[..., None]), 0.0)
        grad_values_now = grad_values_now + jnp.einsum(
            "hqk,qhd->khd",
            probs.astype(jnp.bfloat16),
            grad_block,
            preferred_element_type=jnp.float32,
        )
        grad_probs = jnp.einsum(
            "qhd,khd->hqk", grad_block, own_values, preferred_element_type=jnp.float32
        )
        grad_scores = (probs * (grad_probs - delta_block[..., None])).astype(jnp.bfloat16)
        grad_keys_now = grad_keys_now + jnp.einsum(
            "hqk,qhd->khd", grad_scores, query_block, preferred_element_type=jnp.float32
        )
        return ((grad_keys_now, grad_values_now), None)

    carried, _ = lax.scan(key_step, carried, (query_stack, grad_stack, offsets))
    grad_keys, grad_values = carried
    grad_pack = jnp.stack(
        [
            grad_queries.transpose(1, 0, 2).reshape(head_rows, features),
            (grad_keys * scale_factor).reshape(head_rows, features),
            grad_values.reshape(head_rows, features),
        ],
        axis=1,
    ).astype(jnp.bfloat16)
    grad_joined = lax.all_to_all(
        grad_pack.reshape(head_rows, 3, 1, features),
        "ulysses",
        split_axis=0,
        concat_axis=2,
        tiled=True,
    ).reshape(tok_rows, 3 * width_all)
    qkv_grad = lax.dot_general(
        normed_one, grad_joined, contract_rows, preferred_element_type=jnp.float32
    )
    joined_sums = jnp.sum(grad_joined.astype(jnp.float32), axis=0)
    qv_bias_grad = jnp.concatenate([joined_sums[:width_all], joined_sums[2 * width_all :]])
    grad_norm_one = lax.dot_general(
        grad_joined, qkv_proj, contract_cols, preferred_element_type=jnp.float32
    )
    _, norm_one_pull = jax.vjp(layer_norm, inputs_f, gain_one, shift_one)
    grad_inputs_part, ln1_gain_grad, ln1_bias_grad = norm_one_pull(grad_norm_one)
    input_grad = (grad_mixed + grad_inputs_part).astype(jnp.bfloat16)
    shares = (
        lax.psum_scatter(ln1_gain_grad, ("ulysses", "blk"), scatter_dimension=0, tiled=True),
        lax.psum_scatter(ln1_bias_grad, ("ulysses", "blk"), scatter_dimension=0, tiled=True),
        lax.psum_scatter(qkv_grad, ("ulysses", "blk"), scatter_dimension=0, tiled=True),
        lax.psum_scatter(qv_bias_grad, ("ulysses", "blk"), scatter_dimension=0, tiled=True),
        lax.psum_scatter(proj_grad, ("ulysses", "blk"), scatter_dimension=0, tiled=True),
        lax.psum_scatter(proj_bias_grad, ("ulysses", "blk"), scatter_dimension=0, tiled=True),
        lax.psum_scatter(ln2_gain_grad, ("ulysses", "blk"), scatter_dimension=0, tiled=True),
        lax.psum_scatter(ln2_bias_grad, ("ulysses", "blk"), scatter_dimension=0, tiled=True),
        lax.psum_scatter(up_grad, ("ulysses", "blk"), scatter_dimension=0, tiled=True),
        lax.psum_scatter(up_bias_grad, ("ulysses", "blk"), scatter_dimension=0, tiled=True),
        lax.psum_scatter(down_grad, ("ulysses", "blk"), scatter_dimension=0, tiled=True),
        lax.psum_scatter(down_bias_grad, ("ulysses", "blk"), scatter_dimension=0, tiled=True),
    )
    return (
        output,
        input_grad,
        shares[0],
        shares[1],
        shares[2],
        shares[3],
        shares[4],
        shares[5],
        shares[6],
        shares[7],
        shares[8],
        shares[9],
        shares[10],
        shares[11],
    )


TOKEN_ROWS = P(("ulysses", "blk"), None)
VECTOR = P(("ulysses", "blk"))


def solution(mesh):
    whole = P()
    in_specs = (
        TOKEN_ROWS, VECTOR, VECTOR, TOKEN_ROWS, VECTOR, TOKEN_ROWS, VECTOR, VECTOR, VECTOR, TOKEN_ROWS,
        VECTOR, TOKEN_ROWS, VECTOR, whole, whole, TOKEN_ROWS,
    )
    out_specs = (
        TOKEN_ROWS, TOKEN_ROWS, VECTOR, VECTOR, TOKEN_ROWS, VECTOR, TOKEN_ROWS, VECTOR, VECTOR, VECTOR,
        TOKEN_ROWS, VECTOR, TOKEN_ROWS, VECTOR,
    )
    fits = mesh.shape["ulysses"] == 4 and mesh.shape["blk"] == 8
    return jax.shard_map(
        fast_body if fits else general_body,
        mesh=mesh, in_specs=in_specs, out_specs=out_specs, check_vma=False,
    )
```
